32 devices in a mesh: seq: 16 (over z, y, x), head: 2 (over core).
Axes of the slice: x: 2, y: 2, z: 4, core: 2. Of those that a mesh axis runs over, the one named last changes fastest.
Arguments:
- ssm_input: bfloat16 [4096, 2048], P('seq', 'head'), may hold values from -6 to 6
- bc_input: bfloat16 [4096, 512], P('seq', 'head'), may hold values from -4 to 4
- conv_taps: float32 [4, 2048], P(None, 'head'), may hold values from -3 to 3
- conv_bias: float32 [2048], P('head'), may hold values from -1 to 0
- bc_taps: float32 [4, 512], P(None, 'head'), may hold values from -3 to 3
- bc_bias: float32 [512], P('head'), may hold values from -0.6 to 0.35
- step_input: float32 [32, 4096], P('head', 'seq'), may hold values from -4 to 4
- step_bias: float32 [32], P('head'), may hold values from -8 to -2
- decay_log: float32 [32], P('head'), may hold values from -8 to -1
- skip_gain: float32 [32], P('head'), may hold values from 0.5 to 2
- request_offset: int32 [4096], P('seq'), may hold values from 0 to 2047, as said below
Outputs:
- ssm_output: bfloat16 [4096, 2048], P('seq', 'head')
The draws below stay inside these ranges and needn't reach their ends.
Inputs may be any that keep to these rules, and one draw needn't show every extreme that they name: request_offset counts the earlier tokens of the token's request: 0 at the first token and wherever a request starts, else one more than at the token before; one request has exactly 2048 tokens and none has more.
All inputs are finite; a program needn't handle non-finite values.
Results may differ from the reference program's by a relative error of at most 0.0095.
Values may be sent and summed in bfloat16 or wider, within the bound.
No kernel may reach another device: no remote copies, remote signals or barrier semaphores. Data moves between devices by JAX's collectives and lax.ppermute only.
A program may use at most 192 MiB of HBM per device.

```python
import jax
import jax.numpy as jnp
from jax import lax

HEADDIM = 64
STATE = 256
KERNEL = 4
BLOCK = 256
TOK_DEV = 256
TOKENS = 4096
HEADS = 32
GROUPS = 1
GROUP_HEADS = 32
CHANNELS = 2048


def head_rates(key):
    pick_key, spread_key, keep_key, rate_key = jax.random.split(jax.random.fold_in(key, 11), 4)
    slow_heads = jax.random.randint(pick_key, (HEADS,), 0, 10) < 5
    root_tokens = jnp.sqrt(jnp.float32(TOKENS))
    slow_step = jax.random.uniform(spread_key, (HEADS,), jnp.float32, 0.25, 0.6) / root_tokens
    kept_nats = jax.random.uniform(keep_key, (HEADS,), jnp.float32, 0.3, 1.5)
    slow_coef = kept_nats / (1.65 * slow_step * jnp.float32(TOKENS))
    lowest = jnp.log(jnp.float32(0.1) / jnp.float32(TOK_DEV))
    highest = jnp.log(jnp.float32(1.0 / 30.0))
    fraction = jax.random.uniform(rate_key, (HEADS,), jnp.float32, 0.0, 1.0)
    fast_rate = jnp.exp(lowest + (highest - lowest) * fraction)
    fast_coef = jnp.sqrt(fast_rate / 0.825)
    fast_step = 0.5 * fast_coef
    step_value = jnp.where(slow_heads, slow_step, fast_step)
    coef_value = jnp.where(slow_heads, slow_coef, fast_coef)
    return (jnp.log(step_value).astype(jnp.float32), jnp.log(coef_value).astype(jnp.float32))


def draw_step_bias(key, part):
    return head_rates(key)[0]


def draw_decay_log(key, part):
    return head_rates(key)[1]


def draw_request_offset(key, part):
    place_key, start_key = jax.random.split(jax.random.fold_in(key, 23))
    half_tokens = TOKENS // 2
    long_start = jax.random.randint(place_key, (), 0, half_tokens + 1)
    places = lax.iota(jnp.int32, TOKENS)
    starts = jax.random.randint(start_key, (TOKENS,), 0, 2 * TOK_DEV) == 0
    inside = (places > long_start) & (places < long_start + half_tokens)
    starts = jnp.where(inside, False, starts)
    starts = starts | (places == 0) | (places == long_start) | (places == long_start + half_tokens)
    latest = lax.cummax(jnp.where(starts, places, 0), axis=0)
    return (places - latest).astype(jnp.int32)


def steps_of(own_key, shape, cuts, least, largest):
    loudness, own = 1.0, jax.random.fold_in(own_key, 6)
    for dim, blocks in cuts:
        heights = jnp.exp(jax.random.uniform(jax.random.fold_in(own, dim), (blocks,), jnp.float32, least / len(cuts), largest / len(cuts)))
        loudness = loudness * jnp.repeat(heights, shape[dim] // blocks).reshape([-1 if axis == dim else 1 for axis in range(len(shape))])
    return loudness


def centred(own_key, shape, spread, most, shards=(), held_as=jnp.bfloat16):
    gain = steps_of(own_key, shape, shards, -0.22, 0.18) if shards else 1.0
    entries = jax.random.normal(own_key, shape, jnp.float32) * spread * gain
    return jnp.minimum(jnp.maximum(entries, -most), most).astype(held_as)


def setup_inputs(seed: int = 0) -> dict:
    arg_keys = jax.random.split(jax.random.key(seed), 12)
    ssm_input = centred(arg_keys[0], (TOKENS, CHANNELS), 1.0, 6.0, ((0, 16), (1, 2)))
    bc_input = centred(arg_keys[1], (TOKENS, GROUPS * 2 * STATE), 0.5, 4.0, ((0, 16), (1, 2)))
    conv_taps = centred(arg_keys[2], (KERNEL, CHANNELS), KERNEL ** -0.5, 3.0, ((1, 2),), jnp.float32)
    conv_bias = jnp.clip(-1.0 + 1.0 * jax.random.uniform(arg_keys[3], (CHANNELS,), jnp.float32) ** steps_of(arg_keys[3], (CHANNELS,), ((0, 2),), -0.2, 0.2), -1.0, 0.0)
    bc_taps = centred(arg_keys[4], (KERNEL, GROUPS * 2 * STATE), KERNEL ** -0.5, 3.0, ((1, 2),), jnp.float32)
    bc_bias = jnp.clip(-0.6 + 0.95000002 * jax.random.uniform(arg_keys[5], (GROUPS * 2 * STATE,), jnp.float32) ** steps_of(arg_keys[5], (GROUPS * 2 * STATE,), ((0, 2),), -0.2, 0.2), -0.6, 0.35)
    step_input = centred(arg_keys[6], (HEADS, TOKENS), 1.0, 4.0, ((0, 2), (1, 16)), jnp.float32)
    step_bias = draw_step_bias(jax.random.fold_in(arg_keys[11], 71), 0)
    decay_log = draw_decay_log(jax.random.fold_in(arg_keys[11], 71), 0)
    skip_gain = jnp.clip(0.5 + 1.5 * jax.random.uniform(arg_keys[9], (HEADS,), jnp.float32) ** steps_of(arg_keys[9], (HEADS,), ((0, 2),), -0.2, 0.2), 0.5, 2.0)
    request_offset = draw_request_offset(jax.random.fold_in(arg_keys[11], 71), 0)
    return {"ssm_input": ssm_input, "bc_input": bc_input, "conv_taps": conv_taps, "conv_bias": conv_bias, "bc_taps": bc_taps, "bc_bias": bc_bias, "step_input": step_input, "step_bias": step_bias, "decay_log": decay_log, "skip_gain": skip_gain, "request_offset": request_offset}


def conv_silu(source, tap_weights, tap_bias, offset):
    tok_rows = source.shape[0]
    tap_count = tap_weights.shape[0]
    summed = jnp.zeros(source.shape, jnp.float32) + tap_bias[None, :]
    for lag_steps in range(tap_count):
        shifted = jnp.pad(source, ((lag_steps, 0), (0, 0)))[:tok_rows].astype(jnp.float32)
        in_request = (offset >= lag_steps).astype(jnp.float32)[:, None]
        summed = summed + tap_weights[tap_count - 1 - lag_steps][None, :] * shifted * in_request
    return jax.nn.silu(summed).astype(jnp.bfloat16)


def reference(ssm_input, bc_input, conv_taps, conv_bias, bc_taps, bc_bias, step_input, step_bias, decay_log, skip_gain, request_offset):
    precise = lax.Precision.HIGHEST
    x_conv = conv_silu(ssm_input, conv_taps, conv_bias, request_offset)
    bc_conv = conv_silu(bc_input, bc_taps, bc_bias, request_offset)
    time_step = jax.nn.softplus(step_input + step_bias[:, None])
    log_decay = -jnp.exp(decay_log)[:, None] * time_step
    block_count = TOKENS // BLOCK
    blocked = (x_conv.reshape(block_count, BLOCK, HEADS, HEADDIM),
               bc_conv.reshape(block_count, BLOCK, GROUPS, 2, STATE),
               time_step.reshape(HEADS, block_count, BLOCK).transpose(1, 0, 2),
               log_decay.reshape(HEADS, block_count, BLOCK).transpose(1, 0, 2),
               request_offset.reshape(block_count, BLOCK))

    def advance(entering, block_item):
        x_block, bc_block, step_block, decay_block, offset_block = block_item
        b_group = bc_block[:, :, 0, :].astype(jnp.float32)
        c_group = bc_block[:, :, 1, :].astype(jnp.float32)
        b_head = jnp.repeat(b_group, GROUP_HEADS, axis=1)
        c_head = jnp.repeat(c_group, GROUP_HEADS, axis=1)
        x_float = x_block.astype(jnp.float32)
        rate_sum = jnp.cumsum(decay_block, axis=1)
        positions = lax.iota(jnp.int32, BLOCK)
        linked = (positions[None, :] <= positions[:, None]) & (offset_block[:, None] >= positions[:, None] - positions[None, :])
        scores = jnp.einsum('ign,jgn->gij', c_group, b_group, precision=precise)
        scores = jnp.repeat(scores, GROUP_HEADS, axis=0)
        rate_gap = jnp.where(linked[None], rate_sum[:, :, None] - rate_sum[:, None, :], -1e30)
        weights = (scores * jnp.exp(rate_gap) * step_block[:, None, :]).astype(jnp.bfloat16)
        intra_part = jnp.einsum('hij,jhp->ihp', weights.astype(jnp.float32), x_float, precision=precise)
        tail_gap = jnp.where(offset_block[-1] >= BLOCK - 1 - positions[None, :], rate_sum[:, -1:] - rate_sum, -1e30)
        weighted_b = (b_head.transpose(1, 0, 2) * (jnp.exp(tail_gap) * step_block)[:, :, None]).astype(jnp.bfloat16)
        block_state = jnp.einsum('hjn,jhp->hnp', weighted_b.astype(jnp.float32), x_float, precision=precise)
        carry_scale = jnp.exp(rate_sum) * (offset_block >= positions + 1).astype(jnp.float32)[None, :]
        inter_part = jnp.einsum('ihn,hnp->ihp', c_head, entering, precision=precise) * carry_scale.T[:, :, None]
        passing = jnp.exp(rate_sum[:, -1]) * (offset_block[-1] >= BLOCK).astype(jnp.float32)
        block_out = intra_part + inter_part + skip_gain[None, :, None] * x_float
        next_state = passing[:, None, None] * entering + block_state
        return next_state, block_out.reshape(BLOCK, HEADS * HEADDIM).astype(jnp.bfloat16)

    start_state = jnp.zeros((HEADS, STATE, HEADDIM), jnp.float32)
    final_state, outputs = lax.scan(advance, start_state, blocked)
    return outputs.reshape(TOKENS, HEADS * HEADDIM)
```

```python
import functools

import jax
import jax.numpy as jnp
from jax import lax
from jax.experimental import pallas as pl
from jax.experimental.pallas import tpu as pltpu
from jax.sharding import PartitionSpec as P

HEADDIM = 64
BLOCK = 256
GROUP = 4
PAD = 16
HALO = 16
LANES = 128
NEG = -1e30
F32 = jnp.float32
BF16 = jnp.bfloat16
SMALL = pltpu.CompilerParams(vmem_limit_bytes=24 * 1024 * 1024)


def dot(a, b, dims=((1,), (0,))):
    return lax.dot_general(a, b, (dims, ((), ())), preferred_element_type=F32)


def exact_dot(a, b, dims=((1,), (0,))):
    return lax.dot_general(
        a, b, (dims, ((), ())), preferred_element_type=F32, precision=lax.Precision.HIGHEST
    )


def two_parts(value):
    high = value.astype(BF16)
    return high, (value - high.astype(F32)).astype(BF16)


def silu(v):
    return 0.5 * v * (1.0 + jnp.tanh(0.5 * v))


def spread(per_head, first_channel, width):
    heads = per_head.shape[1]
    head = lax.broadcasted_iota(jnp.int32, (heads, width), 0)
    channel = lax.broadcasted_iota(jnp.int32, (heads, width), 1) + first_channel
    member = (channel // HEADDIM == head).astype(BF16)
    high, low = two_parts(per_head)
    return dot(high, member) + dot(low, member)


def rates(step, step_bias, decay_log):
    block = step.shape[1]
    time_step = jax.nn.softplus(step + step_bias)
    log_decay = -jnp.exp(decay_log) * time_step
    row = lax.broadcasted_iota(jnp.int32, (block, block), 0)
    column = lax.broadcasted_iota(jnp.int32, (block, block), 1)
    return time_step, exact_dot(log_decay, (row <= column).astype(F32))


def offset_columns(offset_row):
    wide = jnp.broadcast_to(offset_row.astype(F32), (LANES, offset_row.shape[1]))
    return wide.T


def convolve(ext, source, halo, taps, bias, masks, store):
    rows, width = source.shape
    count = taps.shape[0]
    ext[0:8, 0:width] = halo[HALO - 8 : HALO, :].astype(F32)
    ext[8 : 8 + rows, 0:width] = source[...].astype(F32)
    step = 64
    for lane in range(0, width, LANES):
        cols = slice(lane, lane + LANES)
        tap_rows = [taps[k : k + 1, cols] for k in range(count)]
        for top in range(0, rows, step):
            total = tap_rows[count - 1] * ext[8 + top : 8 + top + step, cols] + bias[:, cols]
            for lag in range(1, count):
                shifted = ext[8 - lag + top : 8 - lag + top + step, cols]
                total = total + tap_rows[count - 1 - lag] * shifted * masks[lag - 1, top : top + step, :]
            store(top, step, cols, silu(total))


def front_kernel(
    place, x, own, other, halo_x, halo_own, halo_other, taps, bias, own_taps, other_taps,
    step, step_bias, decay_log, offset, x_out, b_out, c_out, s0, s1, s2, s3, ext, masks, gates,
):
    member = place[0]
    first = place[1] == 0
    block = x.shape[0]
    offset_col = offset_columns(offset[...])
    for lag in range(1, taps.shape[0]):
        masks[lag - 1] = (offset_col >= lag).astype(F32)
    count = taps.shape[0]

    def to_b(top, size, cols, value):
        b_out[top : top + size, cols] = value.astype(BF16)

    def to_c(top, size, cols, value):
        c_out[top : top + size, cols] = value.astype(BF16)

    def pick(a, b, shape):
        return jnp.where(first, a[...], b[...]) if shape is None else jnp.where(first, a, b)

    own_t, other_t = own_taps[...], other_taps[...]
    b_t, c_t = jnp.where(first, own_t, other_t), jnp.where(first, other_t, own_t)
    own_v, other_v = own[...].astype(F32), other[...].astype(F32)
    own_h, other_h = halo_own[...].astype(F32), halo_other[...].astype(F32)
    convolve(
        ext, jnp.where(first, own_v, other_v), jnp.where(first, own_h, other_h),
        b_t[0:count], b_t[count : count + 1], masks, to_b,
    )
    convolve(
        ext, jnp.where(first, other_v, own_v), jnp.where(first, other_h, own_h),
        c_t[0:count], c_t[count : count + 1], masks, to_c,
    )
    time_step, rate_sum = rates(step[...], step_bias[...], decay_log[...])
    last_offset = offset[0, block - 1]
    behind = block - 1 - lax.broadcasted_iota(jnp.int32, rate_sum.shape, 1)
    last = rate_sum[:, block - 1 : block]
    gate = jnp.exp(jnp.where(last_offset >= behind, last - rate_sum, NEG)) * time_step
    gates[...] = gate.T
    passing = jnp.exp(last) * (last_offset >= block).astype(F32)
    passing_rows = jnp.broadcast_to(passing, (passing.shape[0], LANES)).T[0:8, :]

    def to_x(top, size, cols, value):
        x_out[top : top + size, cols] = value.astype(BF16)

    convolve(ext, x, halo_x, taps, bias, masks, to_x)
    slices = (s0, s1, s2, s3)
    width = x.shape[1] // len(slices)
    b_rows = b_out[...]
    for k, out in enumerate(slices):
        channel = pl.multiple_of((member ^ k) * width, width)
        scale = spread(gates[...], channel, width)
        scaled = (x_out[:, pl.ds(channel, width)].astype(F32) * scale).astype(BF16)
        state = dot(b_rows, scaled, ((0,), (0,)))
        out[0 : b_rows.shape[1], :] = state.astype(BF16)
        high, low = two_parts(spread(passing_rows, channel, width)[0:1, :])
        line = lax.broadcasted_iota(jnp.int32, (PAD, width), 0)
        tail = jnp.where(line == 0, high.astype(F32), jnp.where(line == 1, low.astype(F32), 0.0))
        out[b_rows.shape[1] :, :] = tail.astype(BF16)


def decay_of(state):
    rows = state.shape[0] - PAD
    tail = state[rows : rows + PAD, :].astype(F32)
    return tail[0:1, :] + tail[1:2, :]


def over(condition, decay):
    return jnp.where(condition, decay, jnp.ones_like(decay))


def group_kernel(place, r0, r1, r2, r3, total):
    member = place[0]
    states = (r0, r1, r2, r3)
    rows = r0.shape[0] - PAD
    decays = [decay_of(state) for state in states]
    factors = []
    for k in range(len(states)):
        factor = jnp.ones_like(decays[0])
        for other in range(len(states)):
            if other != k:
                factor = factor * over((member ^ other) > (member ^ k), decays[other])
        factors.append(factor)
    step = 64
    for top in range(0, rows, step):
        value = factors[0] * r0[top : top + step, :].astype(F32)
        for k in range(1, len(states)):
            value = value + factors[k] * states[k][top : top + step, :].astype(F32)
        total[top : top + step, :] = value.astype(BF16)
    whole = decays[0] * decays[1] * decays[2] * decays[3]
    high, low = two_parts(whole)
    line = lax.broadcasted_iota(jnp.int32, (PAD, whole.shape[1]), 0)
    tail = jnp.where(line == 0, high.astype(F32), jnp.where(line == 1, low.astype(F32), 0.0))
    total[rows:, :] = tail.astype(BF16)


def entering_kernel(place, r0, r1, r2, r3, near_odd, near_even, far, e0, e1, e2, e3):
    member, group = place[0], place[2]
    states, outs = (r0, r1, r2, r3), (e0, e1, e2, e3)
    rows = r0.shape[0] - PAD
    decays = [decay_of(state) for state in states]
    one = jnp.ones_like(decays[0])
    odd = (group & 1) == 1
    from_odd = jnp.where(odd, one, 0.0)
    from_even = jnp.where(jnp.logical_and(group >= 2, jnp.logical_not(odd)), one, 0.0)
    near_decay = from_odd * decay_of(near_odd) + from_even * decay_of(near_even)
    from_far = jnp.where(group >= 2, near_decay, 0.0)
    heads, terms = [], []
    for k in range(len(states)):
        head = one
        for source in range(len(states)):
            if source != k:
                head = head * over((member ^ source) < (member ^ k), decays[source])
        heads.append(head)
        mine = []
        for source in range(len(states)):
            if source == k:
                mine.append(None)
                continue
            factor = jnp.where((member ^ source) < (member ^ k), one, 0.0)
            for between in range(len(states)):
                if between not in (k, source):
                    inside = jnp.logical_and(
                        (member ^ between) > (member ^ source), (member ^ between) < (member ^ k)
                    )
                    factor = factor * over(inside, decays[between])
            mine.append(factor)
        terms.append(mine)
    step = 32
    for top in range(0, rows, step):
        part = slice(top, top + step)
        carried = (
            from_odd * near_odd[part, :].astype(F32)
            + from_even * near_even[part, :].astype(F32)
            + from_far * far[part, :].astype(F32)
        )
        held = [state[part, :].astype(F32) for state in states]
        for k, out in enumerate(outs):
            value = heads[k] * carried
            for source in range(len(states)):
                if source != k:
                    value = value + terms[k][source] * held[source]
            out[part, :] = value.astype(BF16)


def intra_kernel(x, b, c, step, step_bias, decay_log, skip, offset, y, carry, bias, scores, columns):
    block = x.shape[0]
    half = block // 2
    time_step, rate_sum = rates(step[...], step_bias[...], decay_log[...])
    columns[...] = rate_sum.T
    offset_col = offset_columns(offset[...])
    row = lax.broadcasted_iota(jnp.int32, (block, LANES), 0)
    for left in range(0, block, LANES):
        column = lax.broadcasted_iota(jnp.int32, (block, LANES), 1) + left
        gap = row - column
        linked = jnp.logical_and(gap >= 0, offset_col >= gap.astype(F32))
        bias[:, left : left + LANES] = jnp.where(linked, 0.0, NEG)
    scores[...] = dot(c[...], b[...], ((1,), (1,)))
    reach = rate_sum - jnp.log(time_step)
    starts = row[:, 0 : carry.shape[1]].astype(F32) + 1.0
    carry[...] = jnp.where(offset_col[:, 0 : carry.shape[1]] >= starts, jnp.exp(columns[...]), 0.0)
    lane = lax.broadcasted_iota(jnp.int32, (1, LANES), 1)
    heads = step.shape[0]
    per_tile = LANES // HEADDIM
    for tile in range(heads // per_tile):
        cols = slice(tile * LANES, (tile + 1) * LANES)
        skip_row = jnp.zeros((1, LANES), F32)
        for k in range(per_tile):
            h = tile * per_tile + k
            skip_row = jnp.where(lane // HEADDIM == k, skip[h : h + 1, 0:1], skip_row)
        for top in range(0, block, half):
            part = slice(top, top + half)
            seen = top + half
            value = skip_row * x[part, cols].astype(F32)
            for k in range(per_tile):
                h = tile * per_tile + k
                gap = columns[part, h : h + 1] - reach[h : h + 1, 0:seen] + bias[part, 0:seen]
                weights = (scores[part, 0:seen] * jnp.exp(gap)).astype(BF16)
                chosen = jnp.where(lane // HEADDIM == k, x[0:seen, cols], jnp.zeros((), BF16))
                value = value + dot(weights, chosen)
            y[part, cols] = value


def back_kernel(place, c, f0, f1, f2, f3, intra, carry, out):
    member = place[0]
    parts = (f0, f1, f2, f3)
    width = out.shape[1] // len(parts)
    for k, state in enumerate(parts):
        channel = pl.multiple_of((member ^ k) * width, width)
        scale = spread(carry[...], channel, width)
        cols = pl.ds(channel, width)
        value = intra[:, cols] + scale * dot(c[...], state[...])
        out[:, cols] = value.astype(BF16)


def exchange(array, mask):
    return lax.ppermute(array, "seq", [(i, i ^ mask) for i in range(lax.axis_size("seq"))])


def shifted(array, distance):
    count = lax.axis_size("seq")
    return lax.ppermute(array, "seq", [(i, i + distance) for i in range(count - distance)])


def earlier_groups(total, groups):
    if groups == 4:
        far = exchange(total, 2 * GROUP)
        pairs = []
        for member in range(GROUP):
            low, high = GROUP + member, 2 * GROUP + member
            pairs += [(low, high), (high, low)]
        near_even = lax.ppermute(total, "seq", pairs)
        near_odd = exchange(total, GROUP)
        return near_odd, near_even, far
    rows = total.shape[0] - PAD
    held = shifted(total, GROUP)
    distance = 1
    while distance < groups:
        earlier = shifted(held, GROUP * distance)
        decay, before = decay_of(held), decay_of(earlier)
        state = held[:rows].astype(F32) + decay * earlier[:rows].astype(F32)
        high, low = two_parts(decay * before)
        tail = jnp.concatenate([high, low, jnp.zeros((PAD - 2, high.shape[1]), BF16)], axis=0)
        held = jnp.concatenate([state.astype(BF16), tail], axis=0)
        distance *= 2
    odd = (lax.axis_index("seq") // GROUP) % 2 == 1
    nothing = jnp.zeros_like(held)
    return jnp.where(odd, held, nothing), jnp.where(odd, nothing, held), nothing


def on_device(
    ssm_input, bc_input, conv_taps, conv_bias, bc_taps, bc_bias,
    step_input, step_bias, decay_log, skip_gain, request_offset,
):
    block, channels = ssm_input.shape
    state_size = bc_input.shape[1]
    heads = step_input.shape[0]
    width = channels // GROUP
    groups = lax.axis_size("seq") // GROUP
    here = lax.axis_index("seq")
    place = jnp.stack([here % GROUP, lax.axis_index("head") % 2, here // GROUP]).astype(jnp.int32)

    swap = [(i, i ^ 1) for i in range(lax.axis_size("head"))]
    other_bc = lax.ppermute(bc_input, "head", swap)
    own_taps = jnp.concatenate([bc_taps, bc_bias[None, :]], axis=0)
    other_taps = lax.ppermute(own_taps, "head", swap)
    first_row = block - HALO
    halo = shifted(
        jnp.concatenate([ssm_input[first_row:], bc_input[first_row:], other_bc[first_row:]], axis=1), 1
    )
    halo_x = halo[:, :channels]
    halo_own = halo[:, channels : channels + state_size]
    halo_other = halo[:, channels + state_size :]
    step_col, decay_col = step_bias[:, None], decay_log[:, None]
    offset_row = request_offset[None, :]

    smem = pl.BlockSpec(memory_space=pltpu.SMEM)
    vmem = pl.BlockSpec(memory_space=pltpu.VMEM)
    slice_shape = jax.ShapeDtypeStruct((state_size + PAD, width), BF16)
    bc_shape = jax.ShapeDtypeStruct((block, state_size), BF16)
    x_conv, b_conv, c_conv, *slices = pl.pallas_call(
        front_kernel,
        out_shape=[jax.ShapeDtypeStruct(ssm_input.shape, BF16), bc_shape, bc_shape] + [slice_shape] * GROUP,
        in_specs=[smem] + [vmem] * 14,
        out_specs=[vmem] * (3 + GROUP),
        scratch_shapes=[
            pltpu.VMEM((block + 8, channels), F32),
            pltpu.VMEM((conv_taps.shape[0] - 1, block, LANES), F32),
            pltpu.VMEM((block, heads), F32),
        ],
        compiler_params=SMALL,
        name="front",
    )(
        place, ssm_input, bc_input, other_bc, halo_x, halo_own, halo_other, conv_taps, conv_bias[None, :],
        own_taps, other_taps, step_input, step_col, decay_col, offset_row,
    )
    received = [slices[0]] + [exchange(slices[k], k) for k in (1, 2, 3)]
    intra, carry = pl.pallas_call(
        intra_kernel,
        out_shape=[
            jax.ShapeDtypeStruct((block, channels), F32),
            jax.ShapeDtypeStruct((block, heads), F32),
        ],
        in_specs=[vmem] * 8,
        out_specs=[vmem] * 2,
        scratch_shapes=[
            pltpu.VMEM((block, block), F32),
            pltpu.VMEM((block, block), F32),
            pltpu.VMEM((block, heads), F32),
        ],
        compiler_params=SMALL,
        cost_estimate=pl.CostEstimate(flops=600_000_000, bytes_accessed=2_500_000, transcendentals=1_000_000),
        name="intra",
    )(x_conv, b_conv, c_conv, step_input, step_col, decay_col, skip_gain[:, None], offset_row)
    total = pl.pallas_call(
        group_kernel,
        out_shape=slice_shape,
        in_specs=[smem] + [vmem] * GROUP,
        out_specs=vmem,
        compiler_params=SMALL,
        name="group",
    )(place, *received)
    near_odd, near_even, far = earlier_groups(total, groups)
    entering = pl.pallas_call(
        entering_kernel,
        out_shape=[jax.ShapeDtypeStruct((state_size, width), BF16)] * GROUP,
        in_specs=[smem] + [vmem] * (GROUP + 3),
        out_specs=[vmem] * GROUP,
        compiler_params=SMALL,
        name="entering",
    )(place, *received, near_odd, near_even, far)
    mine = [entering[0]] + [exchange(entering[k], k) for k in (1, 2, 3)]
    return pl.pallas_call(
        back_kernel,
        out_shape=jax.ShapeDtypeStruct((block, channels), BF16),
        in_specs=[smem] + [vmem] * (GROUP + 3),
        out_specs=vmem,
        compiler_params=SMALL,
        name="back",
    )(place, c_conv, *mine, intra, carry)


def solution(mesh):
    return jax.shard_map(
        on_device,
        mesh=mesh,
        in_specs=(
            P("seq", "head"),
            P("seq", "head"),
            P(None, "head"),
            P("head"),
            P(None, "head"),
            P("head"),
            P("head", "seq"),
            P("head"),
            P("head"),
            P("head"),
            P("seq"),
        ),
        out_specs=P("seq", "head"),
        check_vma=False,
    )
```

```python
import jax
import jax.numpy as jnp
from jax import lax
from jax.experimental import pallas as pl
from jax.experimental.pallas import tpu as pltpu
from jax.sharding import PartitionSpec as P

HEADDIM = 64
GROUP = 4
TAIL = 16
GATE_AT, X_LAST_AT, X_FIRST_AT, B_LAST_AT, B_FIRST_AT = 1, 4, 7, 10, 13
HALO = 16
LANES = 128
NEG = -1e30
F32 = jnp.float32
BF16 = jnp.bfloat16
PARAMS = pltpu.CompilerParams(vmem_limit_bytes=24 * 1024 * 1024)


def dot(a, b, dims=((1,), (0,))):
    return lax.dot_general(a, b, (dims, ((), ())), preferred_element_type=F32)


def two_parts(value):
    high = value.astype(BF16).astype(F32)
    return high, value - high


def silu(v):
    return 0.5 * v * (1.0 + jnp.tanh(0.5 * v))


def iota(shape, dim):
    return lax.broadcasted_iota(jnp.int32, shape, dim)


def column(scalars, count):
    row = iota((count, LANES), 0)
    value = jnp.zeros((count, LANES), F32)
    for k in range(count):
        value = jnp.where(row == k, scalars[k], value)
    return value[:, 0:1]


def spread(parts, first_channel, width):
    heads = parts.shape[1] // 2
    shape = (2 * heads, width)
    head = iota(shape, 0) & (heads - 1)
    channel = iota(shape, 1) + first_channel
    return dot(parts, (channel // HEADDIM == head).astype(F32).astype(BF16))


def turned(per_head):
    high, low = two_parts(per_head)
    return jnp.concatenate([high, low], axis=0).T.astype(BF16)


def rates(step, step_bias, decay_log):
    heads, block = step.shape
    time_step = jax.nn.softplus(step + step_bias)
    log_decay = -jnp.exp(decay_log) * time_step
    shape = (block, block)
    upto = (iota(shape, 0) <= iota(shape, 1)).astype(F32).astype(BF16)
    first, rest = two_parts(log_decay)
    second, third = two_parts(rest)
    sums = dot(jnp.concatenate([first, second, third], axis=0).astype(BF16), upto)
    return time_step, sums[0:heads] + (sums[heads : 2 * heads] + sums[2 * heads :])


def offset_columns(offset_row):
    wide = jnp.broadcast_to(offset_row.astype(F32), (LANES, offset_row.shape[1]))
    return wide.T


def lag_matrices(offset_col, count):
    block = offset_col.shape[0]
    gap = iota((block, block), 0) - iota((block, block), 1)
    offset_wide = jnp.concatenate([offset_col] * (block // LANES), axis=1)
    return [
        jnp.where(jnp.logical_and(gap == lag, offset_wide >= lag), 1.0, 0.0).astype(BF16)
        for lag in range(1, count)
    ]


def convolve(source, taps, bias, lags):
    count = len(lags) + 1
    total = taps[count - 1 : count] * source.astype(F32) + bias
    for lag, matrix in enumerate(lags, 1):
        total = total + taps[count - 1 - lag : count - lag] * dot(matrix, source)
    return total


def channels_kernel(x, taps, bias, step, step_bias, decay_log, offset, x_out, gated, aux, passing_out):
    block, channels = x.shape
    count = taps.shape[0]
    heads = step.shape[0]
    offset_col = offset_columns(offset[...])
    lags = lag_matrices(offset_col, count)
    time_step, rate_sum = rates(step[...], column(step_bias, heads), column(decay_log, heads))
    last_offset = offset[0, block - 1]
    place = iota(rate_sum.shape, 1)
    last = rate_sum[:, block - 1 : block]
    gate = jnp.exp(jnp.where(last_offset >= block - 1 - place, last - rate_sum, NEG)) * time_step
    passing = jnp.exp(last) * (last_offset >= block).astype(F32)
    passing_out[...] = jnp.broadcast_to(passing, passing_out.shape)
    gate_early = turned(gate)[0:TAIL]
    gate_late = turned(jnp.where(place >= count - 1, gate, 0.0))
    width = channels // GROUP
    for k in range(GROUP):
        cols = slice(k * width, (k + 1) * width)
        source = x[:, cols]
        before = convolve(source, taps[:, cols], bias[:, cols], lags)
        value = silu(before).astype(BF16)
        x_out[:, cols] = value
        gated[:, cols] = (value.astype(F32) * spread(gate_late, k * width, width)).astype(BF16)
        aux[0:8, cols] = before[0:8]
        early = spread(gate_early, k * width, width)
        first = source[0:TAIL].astype(F32)
        last_rows = source[block - TAIL : block].astype(F32)
        aux[8:24, cols] = jnp.concatenate(
            [early[0:1], early[0:3], last_rows[TAIL - 3 :], first[0:3], jnp.zeros((TAIL - 10, width), F32)], axis=0
        )


def states_kernel(
    place, own, other, own_taps, other_taps, own_bias, other_bias, gated, aux, passing, offset,
    s0, s1, s2, s3, b_out, b_taps, turn,
):
    member = place[0]
    first = place[1] == 0
    block, state_size = own.shape
    count = own_taps.shape[0]
    lags = lag_matrices(offset_columns(offset[...]), count)
    taps = jnp.where(first, own_taps[...], other_taps[...])
    bias = jnp.where(first, own_bias[...], other_bias[...])
    source = jnp.where(first, own[...].astype(F32), other[...].astype(F32))
    before = convolve(source.astype(BF16), taps, bias, lags)
    value = silu(before)
    b_out[...] = value.astype(BF16)
    turn[...] = value.T.astype(BF16)
    b_taps[...] = jnp.concatenate([taps, bias, jnp.zeros((8 - count - 1, state_size), F32), before[0:8]], axis=0)
    width = gated.shape[1] // GROUP
    heads = passing.shape[0]
    slice_heads = heads // GROUP
    lane = iota((heads, width), 1)
    head = iota((heads, width), 0)
    high, low = two_parts(passing[:, 0:1])
    offsets = pltpu.roll(jnp.minimum(offset[...], count - 1).astype(F32), 2 * slice_heads, 1)
    offsets = jnp.where(
        jnp.logical_and(lane[0:1] >= 2 * slice_heads, lane[0:1] < 2 * slice_heads + count - 1), offsets, 0.0
    )
    row = iota((TAIL, width), 0)
    b_tail = jnp.concatenate(
        [jnp.zeros((B_LAST_AT, width), F32), source[block - 3 :], source[0:3]], axis=0
    )
    for k, out in enumerate((s0, s1, s2, s3)):
        quarter = member ^ k
        cols = pl.ds(pl.multiple_of(quarter * width, width), width)
        out[0:state_size, :] = dot(turn[...], gated[:, cols]).astype(BF16)
        at = lane + quarter * slice_heads
        packed = jnp.where(lane < slice_heads, jnp.where(at == head, high, 0.0), 0.0)
        packed = jnp.where(jnp.logical_and(lane >= slice_heads, at == head + slice_heads), low, packed)
        packed = jnp.where(lane < 2 * slice_heads, packed, 0.0)
        misc = jnp.sum(packed, axis=0, keepdims=True) + offsets
        tail = jnp.where(row == 0, misc, jnp.where(row < B_LAST_AT, aux[8:24, cols], b_tail))
        out[state_size:, :] = tail.astype(BF16)


def tail_of(state):
    rows = state.shape[0]
    return state[rows - TAIL : rows, :].astype(F32)


def decay_of(tail):
    width = tail.shape[1]
    slice_heads = width // HEADDIM
    channel = iota((1, width), 1)
    value = jnp.zeros((1, width), F32)
    for head in range(slice_heads):
        both = tail[0:1, head : head + 1] + tail[0:1, slice_heads + head : slice_heads + head + 1]
        value = jnp.where(channel // HEADDIM == head, both, value)
    return value


def pack_decay(decay, tail):
    width = decay.shape[1]
    slice_heads = width // HEADDIM
    lane = iota((1, width), 1)
    high, low = two_parts(decay)
    row = jnp.where(lane >= 2 * slice_heads, tail[0:1], 0.0)
    for head in range(slice_heads):
        at = head * HEADDIM
        row = jnp.where(lane == head, high[:, at : at + 1], row)
        row = jnp.where(lane == slice_heads + head, low[:, at : at + 1], row)
    return row


def tail_taps(x_taps, x_bias, b_taps, count):
    width = x_taps.shape[1]
    upper = iota((TAIL, width), 0) < B_LAST_AT
    taps = [jnp.where(upper, x_taps[k : k + 1], b_taps[k : k + 1]) for k in range(count)]
    return taps, jnp.where(upper, x_bias, b_taps[count : count + 1])


def early_tokens(tail, earlier, taps, bias):
    width = tail.shape[1]
    slice_heads = width // HEADDIM
    count = len(taps)
    row = iota(tail.shape, 0)
    is_last = jnp.logical_or(
        jnp.logical_and(row >= X_LAST_AT, row < X_FIRST_AT),
        jnp.logical_and(row >= B_LAST_AT, row < B_FIRST_AT),
    )
    rows = jnp.where(is_last, earlier, tail)
    offset = jnp.full(tail.shape, -1.0, F32)
    for token in range(count - 1):
        lane = 2 * slice_heads + token
        here = jnp.logical_or(row == X_FIRST_AT + token, row == B_FIRST_AT + token)
        offset = jnp.where(here, tail[0:1, lane : lane + 1], offset)
    total = taps[count - 1] * rows + bias
    for lag in range(1, count):
        total = total + taps[count - 1 - lag] * jnp.where(offset >= lag, pltpu.roll(rows, lag, 0), 0.0)
    value = silu(total).astype(BF16).astype(F32)
    gate = pltpu.roll(tail, B_FIRST_AT - GATE_AT, 0)
    wanted = row >= B_FIRST_AT
    b = jnp.where(wanted, value, 0.0)
    x = jnp.where(wanted, pltpu.roll(value, B_FIRST_AT - X_FIRST_AT, 0) * gate, 0.0)
    return b, x


def group_kernel(place, r0, r1, r2, r3, earlier, x_taps, x_bias, b_taps, total, *, complete):
    rows = r0.shape[0] - TAIL
    width = r0.shape[1]
    count = x_taps.shape[0]
    held = (r0, r1, r2, r3)

    def run(member):
        cols = slice(member * width, (member + 1) * width)
        taps, bias = tail_taps(x_taps[:, cols], x_bias[:, cols], b_taps[...], count)
        states = [held[member ^ k] for k in range(GROUP)]
        tails = [tail_of(state) for state in states]
        decays = [decay_of(tail) for tail in tails]
        factors = [None] * GROUP
        factor = jnp.ones((1, width), F32)
        for k in reversed(range(GROUP)):
            factors[k] = factor
            factor = factor * decays[k]
        early_b, early_x = [], []
        for k in range(0 if complete else 1, GROUP):
            before = tails[k - 1] if k else tail_of(earlier)
            b, x = early_tokens(tails[k], before, taps, bias)
            early_b.append(b)
            early_x.append(x * factors[k])
        b_turned = jnp.concatenate(early_b, axis=0).T.astype(BF16)
        added = dot(b_turned, jnp.concatenate(early_x, axis=0).astype(BF16))
        step = 64
        for top in range(0, rows, step):
            part = slice(top, top + step)
            value = added[part]
            for k in range(GROUP):
                value = value + factors[k] * states[k][part, :].astype(F32)
            total[part, :] = value.astype(BF16)
        row = iota((TAIL, width), 0)
        is_last = jnp.logical_or(
            jnp.logical_and(row >= X_LAST_AT, row < X_FIRST_AT),
            jnp.logical_and(row >= B_LAST_AT, row < B_FIRST_AT),
        )
        gates = jnp.zeros((1, width), F32) if complete else factors[0]
        tail = jnp.where(is_last, tails[GROUP - 1], tails[0])
        tail = jnp.where(row < X_LAST_AT, tail * gates, tail)
        tail = jnp.where(row == 0, pack_decay(factor, tails[0]), tail)
        total[rows:, :] = tail.astype(BF16)

    for member in range(GROUP):
        pl.when(place[0] == member)(lambda member=member: run(member))


def entering_kernel(
    place, r0, r1, r2, r3, near_odd, near_even, far, x_taps, x_bias, b_taps, e0, e1, e2, e3
):
    group = place[2]
    odd = (group & 1) == 1
    one = jnp.ones((1, r0.shape[1]), F32)
    from_odd = jnp.where(odd, one, 0.0)
    from_even = jnp.where(jnp.logical_and(group >= 2, jnp.logical_not(odd)), one, 0.0)
    from_far = jnp.where(group >= 2, one, 0.0)
    rows = r0.shape[0] - TAIL
    width = r0.shape[1]
    count = x_taps.shape[0]
    held, outs = (r0, r1, r2, r3), (e0, e1, e2, e3)

    def run(member):
        cols = slice(member * width, (member + 1) * width)
        taps, bias = tail_taps(x_taps[:, cols], x_bias[:, cols], b_taps[...], count)
        states = [held[member ^ k] for k in range(GROUP)]
        targets = [outs[member ^ k] for k in range(GROUP)]
        tails = [tail_of(state) for state in states]
        near_tail = from_odd * tail_of(near_odd) + from_even * tail_of(near_even)
        far_tail = from_far * tail_of(far)
        decays = [decay_of(tail) for tail in tails]
        near_decay = decay_of(near_tail)
        far_factor = near_decay * from_far
        far_b, far_x = early_tokens(far_tail, jnp.zeros_like(far_tail), taps, bias)
        near_b, near_x = early_tokens(near_tail, far_tail, taps, bias)
        early_b, early_x = [far_b, near_b], [far_x * near_decay, near_x]
        for k in range(GROUP - 1):
            b, x = early_tokens(tails[k], tails[k - 1] if k else near_tail, taps, bias)
            early_b.append(b)
            early_x.append(x)
        b_turned = jnp.concatenate(early_b, axis=0).T.astype(BF16)
        x_rows = jnp.concatenate(early_x, axis=0).astype(BF16)
        added = [dot(b_turned[:, : 2 * TAIL], x_rows[: 2 * TAIL])]
        for k in range(GROUP - 1):
            part = slice((k + 2) * TAIL, (k + 3) * TAIL)
            added.append(dot(b_turned[:, part], x_rows[part]))
        step = 32
        for top in range(0, rows, step):
            part = slice(top, top + step)
            value = from_odd * near_odd[part, :].astype(F32) + from_even * near_even[part, :].astype(F32)
            value = value + far_factor * far[part, :].astype(F32) + added[0][part]
            targets[0][part, :] = value.astype(BF16)
            for k in range(GROUP - 1):
                value = decays[k] * value + states[k][part, :].astype(F32) + added[k + 1][part]
                targets[k + 1][part, :] = value.astype(BF16)

    for member in range(GROUP):
        pl.when(place[0] == member)(lambda member=member: run(member))


def patched(before, halo, taps, offset_col):
    width = before.shape[1]
    count = taps.shape[0]
    extended = jnp.concatenate([halo[HALO - 8 :].astype(F32), jnp.zeros((8, width), F32)], axis=0)
    total = before
    for lag in range(1, count):
        shifted_rows = extended[8 - lag : 16 - lag]
        total = total + taps[count - 1 - lag : count - lag] * jnp.where(
            offset_col[0:8, 0:1] >= lag, shifted_rows, 0.0
        )
    return silu(total)


def intra_kernel(
    place, x, aux, halo, own, other, own_taps, other_taps, own_bias, other_bias, b, b_aux, x_taps,
    step, step_bias, decay_log, skip, offset, y, c_out, carry, bias, scores, columns, x_full, b_full,
):
    first = place[1] == 0
    block, channels = x.shape
    heads = step.shape[0]
    state_size = b.shape[1]
    count = x_taps.shape[0]
    half = block // 2
    time_step, rate_sum = rates(step[...], column(step_bias, heads), column(decay_log, heads))
    columns[...] = rate_sum.T
    offset_col = offset_columns(offset[...])

    x_full[...] = x[...]
    early = patched(aux[0:8, :], halo[:, 0:channels], x_taps[...], offset_col)
    x_full[0:16, :] = jnp.concatenate([early, x[0:16, :].astype(F32)[8:16]], axis=0).astype(BF16)
    own_halo = halo[:, channels : channels + state_size].astype(F32)
    other_halo = halo[:, channels + state_size :].astype(F32)
    b_full[...] = b[...]
    early = patched(b_aux[8:16, :], jnp.where(first, own_halo, other_halo), b_aux[0:count, :], offset_col)
    b_full[0:16, :] = jnp.concatenate([early, b[0:16, :].astype(F32)[8:16]], axis=0).astype(BF16)
    c_taps = jnp.where(first, other_taps[...], own_taps[...])
    c_bias = jnp.where(first, other_bias[...], own_bias[...])
    c_source = jnp.where(first, other[...].astype(F32), own[...].astype(F32)).astype(BF16)
    before = convolve(c_source, c_taps, c_bias, lag_matrices(offset_col, count))
    c_value = silu(before)
    early = patched(before[0:8], jnp.where(first, other_halo, own_halo), c_taps, offset_col)
    c_out[...] = c_value.astype(BF16)
    c_out[0:16, :] = jnp.concatenate([early, c_value[8:16]], axis=0).astype(BF16)

    row = iota((block, LANES), 0)
    for left in range(0, block, LANES):
        gap = row - (iota((block, LANES), 1) + left)
        linked = jnp.logical_and(gap >= 0, offset_col >= gap.astype(F32))
        bias[:, left : left + LANES] = jnp.where(linked, 0.0, NEG)
    scores[...] = dot(c_out[...], b_full[...], ((1,), (1,)))
    reach = rate_sum - jnp.log(time_step)
    starts = iota(rate_sum.shape, 1) + 1
    factor = turned(jnp.where(offset[...] >= starts, jnp.exp(rate_sum), 0.0))
    width = channels // GROUP
    for k in range(GROUP):
        carry[:, k * width : (k + 1) * width] = spread(factor, k * width, width)
    lane = iota((1, LANES), 1)
    per_tile = LANES // HEADDIM
    for tile in range(heads // per_tile):
        cols = slice(tile * LANES, (tile + 1) * LANES)
        skip_row = jnp.zeros((1, LANES), F32)
        for k in range(per_tile):
            skip_row = jnp.where(lane // HEADDIM == k, skip[tile * per_tile + k], skip_row)
        for top in range(0, block, half):
            part = slice(top, top + half)
            seen = top + half
            value = skip_row * x_full[part, cols].astype(F32)
            for k in range(per_tile):
                h = tile * per_tile + k
                gap = columns[part, h : h + 1] - reach[h : h + 1, 0:seen] + bias[part, 0:seen]
                weights = (scores[part, 0:seen] * jnp.exp(gap)).astype(BF16)
                chosen = jnp.where(lane // HEADDIM == k, x_full[0:seen, cols], jnp.zeros((), BF16))
                value = value + dot(weights, chosen)
            y[part, cols] = value


def back_kernel(place, c, f0, f1, f2, f3, intra, carry, out):
    member = place[0]
    parts = (f0, f1, f2, f3)
    width = out.shape[1] // len(parts)
    for k, state in enumerate(parts):
        cols = pl.ds(pl.multiple_of((member ^ k) * width, width), width)
        value = intra[:, cols] + carry[:, cols] * dot(c[...], state[...])
        out[:, cols] = value.astype(BF16)


def exchange(array, mask):
    return lax.ppermute(array, "seq", [(i, i ^ mask) for i in range(lax.axis_size("seq"))])


def shifted(array, distance):
    count = lax.axis_size("seq")
    return lax.ppermute(array, "seq", [(i, i + distance) for i in range(count - distance)])


def scan_groups(total, groups):
    rows = total.shape[0] - TAIL
    last = shifted(total[rows:], GROUP)
    held, decay = total[:rows].astype(F32), decay_of(total[rows:].astype(F32))
    held = shifted(held, GROUP)
    decay = shifted(decay, GROUP)
    distance = 1
    while distance < groups:
        held = held + decay * shifted(held, GROUP * distance)
        decay = decay * shifted(decay, GROUP * distance)
        distance *= 2
    near_tail = jnp.concatenate([jnp.zeros((X_LAST_AT, last.shape[1]), BF16), last[X_LAST_AT:]], axis=0)
    near = jnp.concatenate([held.astype(BF16), near_tail], axis=0)
    odd = (lax.axis_index("seq") // GROUP) % 2 == 1
    nothing = jnp.zeros_like(near)
    return jnp.where(odd, near, nothing), jnp.where(odd, nothing, near), nothing


def on_device(
    ssm_input, bc_input, conv_taps, conv_bias, bc_taps, bc_bias,
    step_input, step_bias, decay_log, skip_gain, request_offset,
):
    block, channels = ssm_input.shape
    state_size = bc_input.shape[1]
    heads = step_input.shape[0]
    width = channels // GROUP
    groups = lax.axis_size("seq") // GROUP
    here = lax.axis_index("seq")
    place = jnp.stack([here % GROUP, lax.axis_index("head") % 2, here // GROUP]).astype(jnp.int32)
    smem = pl.BlockSpec(memory_space=pltpu.SMEM)
    vmem = pl.BlockSpec(memory_space=pltpu.VMEM)
    x_bias, offset_row, own_bias = conv_bias[None, :], request_offset[None, :], bc_bias[None, :]

    swap = [(i, i ^ 1) for i in range(lax.axis_size("head"))]
    other_bc, other_taps, other_bias = [lax.ppermute(part, "head", swap) for part in (bc_input, bc_taps, bc_bias)]
    other_bias = other_bias[None, :]

    x_main, gated, aux, passing = pl.pallas_call(
        channels_kernel,
        out_shape=[
            jax.ShapeDtypeStruct((block, channels), BF16),
            jax.ShapeDtypeStruct((block, channels), BF16),
            jax.ShapeDtypeStruct((24, channels), F32),
            jax.ShapeDtypeStruct((heads, LANES), F32),
        ],
        in_specs=[vmem] * 4 + [smem] * 2 + [vmem],
        out_specs=[vmem] * 4,
        compiler_params=PARAMS,
        name="channels",
    )(ssm_input, conv_taps, x_bias, step_input, step_bias, decay_log, offset_row)

    slice_shape = jax.ShapeDtypeStruct((state_size + TAIL, width), BF16)
    *slices, b_main, b_aux = pl.pallas_call(
        states_kernel,
        out_shape=[slice_shape] * GROUP
        + [jax.ShapeDtypeStruct((block, state_size), BF16), jax.ShapeDtypeStruct((16, state_size), F32)],
        in_specs=[smem] + [vmem] * 10,
        out_specs=[vmem] * (GROUP + 2),
        scratch_shapes=[pltpu.VMEM((state_size, block), BF16)],
        compiler_params=PARAMS,
        name="states",
    )(place, bc_input, other_bc, bc_taps, other_taps, own_bias, other_bias, gated, aux, passing, offset_row)
    first_row = block - HALO
    ends = jnp.concatenate([ssm_input[first_row:], bc_input[first_row:], other_bc[first_row:]], axis=1)
    ends, _ = lax.optimization_barrier((ends, slices[0]))
    halo = shifted(ends, 1)
    received = [slices[0]] + [exchange(slices[k], k) for k in (1, 2, 3)]

    direct = groups == GROUP
    if direct:
        earlier = jnp.zeros((TAIL, width), BF16)
    else:
        last = received[0]
        for k in (1, 2, 3):
            last = jnp.where((here % GROUP) ^ k == GROUP - 1, received[k], last)
        earlier = shifted(last[state_size:], GROUP)
    total = pl.pallas_call(
        lambda *refs: group_kernel(*refs, complete=not direct),
        out_shape=slice_shape,
        in_specs=[smem] + [vmem] * (GROUP + 4),
        out_specs=vmem,
        compiler_params=PARAMS,
        name="group",
    )(place, *received, earlier, conv_taps, x_bias, b_aux)
    total, halo = lax.optimization_barrier((total, halo))
    if direct:
        far = exchange(total, 2 * GROUP)
        pairs = [(GROUP + k, 2 * GROUP + k) for k in range(GROUP)]
        near_even = lax.ppermute(total, "seq", pairs + [(high, low) for low, high in pairs])
        near_odd = exchange(total, GROUP)
    else:
        near_odd, near_even, far = scan_groups(total, groups)

    entering = pl.pallas_call(
        entering_kernel,
        out_shape=[jax.ShapeDtypeStruct((state_size, width), BF16)] * GROUP,
        in_specs=[smem] + [vmem] * (GROUP + 6),
        out_specs=[vmem] * GROUP,
        compiler_params=PARAMS,
        name="entering",
    )(place, *received, near_odd, near_even, far, conv_taps, x_bias, b_aux)
    mine = [entering[0]] + [exchange(entering[k], k) for k in (1, 2, 3)]

    intra, c_conv, carry = pl.pallas_call(
        intra_kernel,
        out_shape=[
            jax.ShapeDtypeStruct((block, channels), F32),
            jax.ShapeDtypeStruct((block, state_size), BF16),
            jax.ShapeDtypeStruct((block, channels), F32),
        ],
        in_specs=[smem] + [vmem] * 13 + [smem] * 3 + [vmem],
        out_specs=[vmem] * 3,
        scratch_shapes=[
            pltpu.VMEM((block, block), F32),
            pltpu.VMEM((block, block), F32),
            pltpu.VMEM((block, heads), F32),
            pltpu.VMEM((block, channels), BF16),
            pltpu.VMEM((block, state_size), BF16),
        ],
        compiler_params=PARAMS,
        cost_estimate=pl.CostEstimate(flops=600_000_000, bytes_accessed=4_000_000, transcendentals=1_000_000),
        name="intra",
    )(
        place, x_main, aux, halo, bc_input, other_bc, bc_taps, other_taps, own_bias, other_bias, b_main, b_aux,
        conv_taps, step_input, step_bias, decay_log, skip_gain, offset_row,
    )
    return pl.pallas_call(
        back_kernel,
        out_shape=jax.ShapeDtypeStruct((block, channels), BF16),
        in_specs=[smem] + [vmem] * (GROUP + 3),
        out_specs=vmem,
        compiler_params=PARAMS,
        name="back",
    )(place, c_conv, *mine, intra, carry)


def solution(mesh):
    return jax.shard_map(
        on_device,
        mesh=mesh,
        in_specs=(
            P("seq", "head"),
            P("seq", "head"),
            P(None, "head"),
            P("head"),
            P(None, "head"),
            P("head"),
            P("head", "seq"),
            P("head"),
            P("head"),
            P("head"),
            P("seq"),
        ),
        out_specs=P("seq", "head"),
        check_vma=False,
    )
```

```python
import jax
import jax.numpy as jnp
from jax import lax
from jax.experimental import pallas as pl
from jax.experimental.pallas import tpu as pltpu
from jax.sharding import PartitionSpec as P

HEADDIM = 64
GROUP = 4
TAIL = 16
GATE_AT, X_LAST_AT, X_FIRST_AT, B_LAST_AT, B_FIRST_AT = 1, 4, 7, 10, 13
HALO = 16
LANES = 128
NEG = -1e30
F32 = jnp.float32
BF16 = jnp.bfloat16
PARAMS = pltpu.CompilerParams(vmem_limit_bytes=24 * 1024 * 1024)


def dot(a, b, dims=((1,), (0,))):
    return lax.dot_general(a, b, (dims, ((), ())), preferred_element_type=F32)


def two_parts(value):
    high = value.astype(BF16).astype(F32)
    return high, value - high


def silu(v):
    return 0.5 * v * (1.0 + jnp.tanh(0.5 * v))


def iota(shape, dim):
    return lax.broadcasted_iota(jnp.int32, shape, dim)


def member_here():
    return lax.axis_index("seq") % GROUP


def group_here():
    return lax.axis_index("seq") // GROUP


def holds_b():
    return lax.axis_index("head") % 2 == 0


def column(row):
    shape = (row.shape[1], row.shape[1])
    wide = jnp.broadcast_to(row, shape)
    return jnp.sum(jnp.where(iota(shape, 0) == iota(shape, 1), wide, 0.0), axis=1, keepdims=True)


def spread(parts, first_channel, width):
    heads = parts.shape[1] // 2
    shape = (2 * heads, width)
    head = iota(shape, 0) & (heads - 1)
    channel = iota(shape, 1) + first_channel
    return dot(parts, (channel // HEADDIM == head).astype(F32).astype(BF16))


def turned(per_head):
    high, low = two_parts(per_head)
    return jnp.concatenate([high, low], axis=0).T.astype(BF16)


def rates(step, step_bias, decay_log):
    heads, block = step.shape
    time_step = jax.nn.softplus(step + step_bias)
    log_decay = -jnp.exp(decay_log) * time_step
    shape = (block, block)
    upto = (iota(shape, 0) <= iota(shape, 1)).astype(F32).astype(BF16)
    first, rest = two_parts(log_decay)
    second, third = two_parts(rest)
    sums = dot(jnp.concatenate([first, second, third], axis=0).astype(BF16), upto)
    return time_step, sums[0:heads] + (sums[heads : 2 * heads] + sums[2 * heads :])


def offset_columns(offset_row):
    wide = jnp.broadcast_to(offset_row.astype(F32), (LANES, offset_row.shape[1]))
    return wide.T


def lag_matrices(offset_col, count):
    block = offset_col.shape[0]
    gap = iota((block, block), 0) - iota((block, block), 1)
    offset_wide = jnp.concatenate([offset_col] * (block // LANES), axis=1)
    return [
        jnp.where(jnp.logical_and(gap == lag, offset_wide >= lag), 1.0, 0.0).astype(BF16)
        for lag in range(1, count)
    ]


def convolve(source, taps, bias, lags):
    count = len(lags) + 1
    total = taps[count - 1 : count] * source.astype(F32) + bias
    for lag, matrix in enumerate(lags, 1):
        total = total + taps[count - 1 - lag : count - lag] * dot(matrix, source)
    return total


def channels_kernel(
    x_hbm, taps_hbm, bias_hbm, own_hbm, own_taps_hbm, own_bias_hbm, step_hbm, offset_hbm,
    step_bias_hbm, decay_hbm, skip_hbm,
    x_out, gated, aux, passing_out, step_out, sums_out, taps, bias, own, own_taps, own_bias, offset,
    x, step, step_bias, decay_log, skip, sems,
):
    block, channels = x.shape
    count = taps.shape[0]
    heads = step.shape[0]
    width = channels // GROUP
    whole = [
        (offset_hbm, offset), (step_hbm, step), (step_bias_hbm, step_bias), (decay_hbm, decay_log),
        (skip_hbm, skip), (taps_hbm, taps), (bias_hbm, bias),
    ]
    later = [(own_hbm, own), (own_taps_hbm, own_taps), (own_bias_hbm, own_bias)]
    parts = [slice(k * width, (k + 1) * width) for k in range(GROUP)]
    pairs = whole + [(x_hbm.at[:, cols], x.at[:, cols]) for cols in parts] + later
    copies = [pltpu.make_async_copy(*pair, sems.at[k]) for k, pair in enumerate(pairs)]
    for copy in copies:
        copy.start()
    for copy in copies[: len(whole)]:
        copy.wait()
    offset_col = offset_columns(offset[...])
    lags = lag_matrices(offset_col, count)
    time_step, rate_sum = rates(step[...], column(step_bias[...]), column(decay_log[...]))
    step_out[...] = time_step
    sums_out[...] = rate_sum
    last_offset = offset[0, block - 1]
    place = iota(rate_sum.shape, 1)
    last = rate_sum[:, block - 1 : block]
    gate = jnp.exp(jnp.where(last_offset >= block - 1 - place, last - rate_sum, NEG)) * time_step
    passing = jnp.exp(last) * (last_offset >= block).astype(F32)
    passing_out[...] = jnp.broadcast_to(passing, passing_out.shape)
    early_parts = turned(jnp.where(place == count - 1, column(skip[...]), gate))[0:TAIL]
    late_parts = turned(jnp.where(place >= count - 1, gate, 0.0))
    for k, cols in enumerate(parts):
        copies[len(whole) + k].wait()
        source = x[:, cols]
        before = convolve(source, taps[:, cols], bias[:, cols], lags)
        value = silu(before).astype(BF16)
        x_out[:, cols] = value
        gated[:, cols] = (value.astype(F32) * spread(late_parts, k * width, width)).astype(BF16)
        aux[0:8, cols] = before[0:8]
        early = spread(early_parts, k * width, width)
        first = source[0:TAIL].astype(F32)
        last_rows = source[block - TAIL : block].astype(F32)
        aux[8:24, cols] = jnp.concatenate(
            [early[3:4], early[0:3], last_rows[TAIL - 3 :], first[0:3], jnp.zeros((TAIL - 10, width), F32)], axis=0
        )
    for copy in copies[len(whole) + GROUP :]:
        copy.wait()


def states_kernel(
    own, other, own_taps, other_taps, own_bias, other_bias, gated, aux, passing, offset,
    s0, s1, s2, s3, b_out, b_taps, ends, turn,
):
    member = member_here()
    first = holds_b()
    block, state_size = own.shape
    count = own_taps.shape[0]
    lags = lag_matrices(offset_columns(offset[...]), count)
    taps = jnp.where(first, own_taps[...], other_taps[...])
    bias = jnp.where(first, own_bias[...], other_bias[...])
    source = jnp.where(first, own[...].astype(F32), other[...].astype(F32))
    before = convolve(source.astype(BF16), taps, bias, lags)
    value = silu(before)
    b_out[...] = value.astype(BF16)
    turn[...] = value.T.astype(BF16)
    b_taps[...] = jnp.concatenate([taps, bias, jnp.zeros((8 - count - 1, state_size), F32), before[0:8]], axis=0)
    channels = gated.shape[1]
    width = channels // GROUP
    heads = passing.shape[0]
    blank = HALO - 3
    ends[:, 0:channels] = jnp.concatenate(
        [jnp.zeros((blank, channels), F32), aux[8 + X_LAST_AT : 8 + X_LAST_AT + 3, :]], axis=0
    ).astype(BF16)
    ends[:, channels : channels + state_size] = own[block - HALO : block, :]
    ends[:, channels + state_size :] = other[block - HALO : block, :]
    slice_heads = heads // GROUP
    lane = iota((heads, width), 1)
    head = iota((heads, width), 0)
    high, low = two_parts(passing[:, 0:1])
    offsets = pltpu.roll(jnp.minimum(offset[...], count - 1).astype(F32), 2 * slice_heads, 1)
    offsets = jnp.where(
        jnp.logical_and(lane[0:1] >= 2 * slice_heads, lane[0:1] < 2 * slice_heads + count - 1), offsets, 0.0
    )
    row = iota((TAIL, width), 0)
    b_tail = jnp.concatenate(
        [jnp.zeros((B_LAST_AT, width), F32), source[block - 3 :], source[0:3]], axis=0
    )
    for k, out in enumerate((s0, s1, s2, s3)):
        quarter = member ^ k
        cols = pl.ds(pl.multiple_of(quarter * width, width), width)
        out[0:state_size, :] = dot(turn[...], gated[:, cols]).astype(BF16)
        at = lane + quarter * slice_heads
        packed = jnp.where(lane < slice_heads, jnp.where(at == head, high, 0.0), 0.0)
        packed = jnp.where(jnp.logical_and(lane >= slice_heads, at == head + slice_heads), low, packed)
        packed = jnp.where(lane < 2 * slice_heads, packed, 0.0)
        misc = jnp.sum(packed, axis=0, keepdims=True) + offsets
        tail = jnp.where(row == 0, misc, jnp.where(row < B_LAST_AT, aux[8:24, cols], b_tail))
        out[state_size:, :] = tail.astype(BF16)


def tail_of(state):
    rows = state.shape[0]
    return state[rows - TAIL : rows, :].astype(F32)


def decay_of(tail):
    width = tail.shape[1]
    slice_heads = width // HEADDIM
    channel = iota((1, width), 1)
    value = jnp.zeros((1, width), F32)
    for head in range(slice_heads):
        both = tail[0:1, head : head + 1] + tail[0:1, slice_heads + head : slice_heads + head + 1]
        value = jnp.where(channel // HEADDIM == head, both, value)
    return value


def pack_decay(decay, tail):
    width = decay.shape[1]
    slice_heads = width // HEADDIM
    lane = iota((1, width), 1)
    high, low = two_parts(decay)
    row = jnp.where(lane >= 2 * slice_heads, tail[0:1], 0.0)
    for head in range(slice_heads):
        at = head * HEADDIM
        row = jnp.where(lane == head, high[:, at : at + 1], row)
        row = jnp.where(lane == slice_heads + head, low[:, at : at + 1], row)
    return row


def tail_taps(x_taps, x_bias, b_taps, count):
    width = x_taps.shape[1]
    upper = iota((TAIL, width), 0) < B_LAST_AT
    taps = [jnp.where(upper, x_taps[k : k + 1], b_taps[k : k + 1]) for k in range(count)]
    return taps, jnp.where(upper, x_bias, b_taps[count : count + 1])


def early_tokens(tail, earlier, taps, bias):
    width = tail.shape[1]
    slice_heads = width // HEADDIM
    count = len(taps)
    row = iota(tail.shape, 0)
    is_last = jnp.logical_or(
        jnp.logical_and(row >= X_LAST_AT, row < X_FIRST_AT),
        jnp.logical_and(row >= B_LAST_AT, row < B_FIRST_AT),
    )
    rows = jnp.where(is_last, earlier, tail)
    offset = jnp.full(tail.shape, -1.0, F32)
    for token in range(count - 1):
        lane = 2 * slice_heads + token
        here = jnp.logical_or(row == X_FIRST_AT + token, row == B_FIRST_AT + token)
        offset = jnp.where(here, tail[0:1, lane : lane + 1], offset)
    total = taps[count - 1] * rows + bias
    for lag in range(1, count):
        total = total + taps[count - 1 - lag] * jnp.where(offset >= lag, pltpu.roll(rows, lag, 0), 0.0)
    value = silu(total).astype(BF16).astype(F32)
    gate = pltpu.roll(tail, B_FIRST_AT - GATE_AT, 0)
    wanted = row >= B_FIRST_AT
    b = jnp.where(wanted, value, 0.0)
    x = jnp.where(wanted, pltpu.roll(value, B_FIRST_AT - X_FIRST_AT, 0) * gate, 0.0)
    return b, x


def group_kernel(r0, r1, r2, r3, earlier, x_taps, x_bias, b_taps, total, *, complete):
    rows = r0.shape[0] - TAIL
    width = r0.shape[1]
    count = x_taps.shape[0]
    held = (r0, r1, r2, r3)

    def run(member):
        cols = slice(member * width, (member + 1) * width)
        taps, bias = tail_taps(x_taps[:, cols], x_bias[:, cols], b_taps[...], count)
        states = [held[member ^ k] for k in range(GROUP)]
        tails = [tail_of(state) for state in states]
        decays = [decay_of(tail) for tail in tails]
        factors = [None] * GROUP
        factor = jnp.ones((1, width), F32)
        for k in reversed(range(GROUP)):
            factors[k] = factor
            factor = factor * decays[k]
        early_b, early_x = [], []
        for k in range(0 if complete else 1, GROUP):
            before = tails[k - 1] if k else tail_of(earlier)
            b, x = early_tokens(tails[k], before, taps, bias)
            early_b.append(b)
            early_x.append(x * factors[k])
        b_turned = jnp.concatenate(early_b, axis=0).T.astype(BF16)
        added = dot(b_turned, jnp.concatenate(early_x, axis=0).astype(BF16))
        step = 64
        for top in range(0, rows, step):
            part = slice(top, top + step)
            value = added[part]
            for k in range(GROUP):
                value = value + factors[k] * states[k][part, :].astype(F32)
            total[part, :] = value.astype(BF16)
        row = iota((TAIL, width), 0)
        is_last = jnp.logical_or(
            jnp.logical_and(row >= X_LAST_AT, row < X_FIRST_AT),
            jnp.logical_and(row >= B_LAST_AT, row < B_FIRST_AT),
        )
        gates = jnp.zeros((1, width), F32) if complete else factors[0]
        tail = jnp.where(is_last, tails[GROUP - 1], tails[0])
        tail = jnp.where(row < X_LAST_AT, tail * gates, tail)
        tail = jnp.where(row == 0, pack_decay(factor, tails[0]), tail)
        total[rows:, :] = tail.astype(BF16)

    for member in range(GROUP):
        pl.when(member_here() == member)(lambda member=member: run(member))


def entering_kernel(
    r0, r1, r2, r3, near_odd, near_even, far, x_taps, x_bias, b_taps, e0, e1, e2, e3
):
    group = group_here()
    odd = (group & 1) == 1
    one = jnp.ones((1, r0.shape[1]), F32)
    from_odd = jnp.where(odd, one, 0.0)
    from_even = jnp.where(jnp.logical_and(group >= 2, jnp.logical_not(odd)), one, 0.0)
    from_far = jnp.where(group >= 2, one, 0.0)
    rows = r0.shape[0] - TAIL
    width = r0.shape[1]
    count = x_taps.shape[0]
    held, outs = (r0, r1, r2, r3), (e0, e1, e2, e3)

    def run(member):
        cols = slice(member * width, (member + 1) * width)
        taps, bias = tail_taps(x_taps[:, cols], x_bias[:, cols], b_taps[...], count)
        states = [held[member ^ k] for k in range(GROUP)]
        targets = [outs[member ^ k] for k in range(GROUP)]
        tails = [tail_of(state) for state in states]
        near_tail = from_odd * tail_of(near_odd) + from_even * tail_of(near_even)
        far_tail = from_far * tail_of(far)
        decays = [decay_of(tail) for tail in tails]
        near_decay = decay_of(near_tail)
        far_factor = near_decay * from_far
        far_b, far_x = early_tokens(far_tail, jnp.zeros_like(far_tail), taps, bias)
        near_b, near_x = early_tokens(near_tail, far_tail, taps, bias)
        early_b, early_x = [far_b, near_b], [far_x * near_decay, near_x]
        for k in range(GROUP - 1):
            b, x = early_tokens(tails[k], tails[k - 1] if k else near_tail, taps, bias)
            early_b.append(b)
            early_x.append(x)
        b_turned = jnp.concatenate(early_b, axis=0).T.astype(BF16)
        x_rows = jnp.concatenate(early_x, axis=0).astype(BF16)
        added = [dot(b_turned[:, : 2 * TAIL], x_rows[: 2 * TAIL])]
        for k in range(GROUP - 1):
            part = slice((k + 2) * TAIL, (k + 3) * TAIL)
            added.append(dot(b_turned[:, part], x_rows[part]))
        step = 32
        for top in range(0, rows, step):
            part = slice(top, top + step)
            value = from_odd * near_odd[part, :].astype(F32) + from_even * near_even[part, :].astype(F32)
            value = value + far_factor * far[part, :].astype(F32) + added[0][part]
            targets[0][part, :] = value.astype(BF16)
            for k in range(GROUP - 1):
                value = decays[k] * value + states[k][part, :].astype(F32) + added[k + 1][part]
                targets[k + 1][part, :] = value.astype(BF16)

    for member in range(GROUP):
        pl.when(member_here() == member)(lambda member=member: run(member))


def patched(before, halo, taps, offset_col):
    width = before.shape[1]
    count = taps.shape[0]
    extended = jnp.concatenate([halo[HALO - 8 :].astype(F32), jnp.zeros((8, width), F32)], axis=0)
    total = before
    for lag in range(1, count):
        shifted_rows = extended[8 - lag : 16 - lag]
        total = total + taps[count - 1 - lag : count - lag] * jnp.where(
            offset_col[0:8, 0:1] >= lag, shifted_rows, 0.0
        )
    return silu(total)


def intra_kernel(
    x, aux, halo, own, other, own_taps, other_taps, own_bias, other_bias, b, b_aux, x_taps,
    step, sums, offset, y, c_out, carry, bias, scores, columns, x_full, b_full,
):
    first = holds_b()
    block, channels = x.shape
    heads = step.shape[0]
    state_size = b.shape[1]
    count = x_taps.shape[0]
    half = block // 2
    time_step, rate_sum = step[...], sums[...]
    columns[...] = rate_sum.T
    offset_col = offset_columns(offset[...])

    x_full[...] = x[...]
    early = patched(aux[0:8, :], halo[:, 0:channels], x_taps[...], offset_col)
    x_full[0:16, :] = jnp.concatenate([early, x[0:16, :].astype(F32)[8:16]], axis=0).astype(BF16)
    own_halo = halo[:, channels : channels + state_size].astype(F32)
    other_halo = halo[:, channels + state_size :].astype(F32)
    b_full[...] = b[...]
    early = patched(b_aux[8:16, :], jnp.where(first, own_halo, other_halo), b_aux[0:count, :], offset_col)
    b_full[0:16, :] = jnp.concatenate([early, b[0:16, :].astype(F32)[8:16]], axis=0).astype(BF16)
    c_taps = jnp.where(first, other_taps[...], own_taps[...])
    c_bias = jnp.where(first, other_bias[...], own_bias[...])
    c_source = jnp.where(first, other[...].astype(F32), own[...].astype(F32)).astype(BF16)
    before = convolve(c_source, c_taps, c_bias, lag_matrices(offset_col, count))
    c_value = silu(before)
    early = patched(before[0:8], jnp.where(first, other_halo, own_halo), c_taps, offset_col)
    c_out[...] = c_value.astype(BF16)
    c_out[0:16, :] = jnp.concatenate([early, c_value[8:16]], axis=0).astype(BF16)

    row = iota((block, LANES), 0)
    for left in range(0, block, LANES):
        gap = row - (iota((block, LANES), 1) + left)
        linked = jnp.logical_and(gap >= 0, offset_col >= gap.astype(F32))
        bias[:, left : left + LANES] = jnp.where(linked, 0.0, NEG)
    scores[...] = dot(c_out[...], b_full[...], ((1,), (1,)))
    reach = rate_sum - jnp.log(time_step)
    starts = iota(rate_sum.shape, 1) + 1
    factor = turned(jnp.where(offset[...] >= starts, jnp.exp(rate_sum), 0.0))
    width = channels // GROUP
    for k in range(GROUP):
        carry[:, k * width : (k + 1) * width] = spread(factor, k * width, width)
    lane = iota((1, LANES), 1)
    per_tile = LANES // HEADDIM
    for tile in range(heads // per_tile):
        cols = slice(tile * LANES, (tile + 1) * LANES)
        skip_row = aux[8:9, cols]
        for top in range(0, block, half):
            part = slice(top, top + half)
            seen = top + half
            value = skip_row * x_full[part, cols].astype(F32)
            for k in range(per_tile):
                h = tile * per_tile + k
                gap = columns[part, h : h + 1] - reach[h : h + 1, 0:seen] + bias[part, 0:seen]
                weights = (scores[part, 0:seen] * jnp.exp(gap)).astype(BF16)
                chosen = jnp.where(lane // HEADDIM == k, x_full[0:seen, cols], jnp.zeros((), BF16))
                value = value + dot(weights, chosen)
            y[part, cols] = value


def back_kernel(c, *refs, first):
    *parts, intra, carry, out, held, sems = refs
    member = member_here()
    width = out.shape[1] // GROUP
    copies = []
    for k, state in enumerate(parts):
        cols = pl.ds(pl.multiple_of((member ^ (first + k)) * width, width), width)
        value = intra[:, cols] + carry[:, cols] * dot(c[...], state[...])
        held[k] = value.astype(BF16)
        copies.append(pltpu.make_async_copy(held.at[k], out.at[:, cols], sems.at[k]))
        copies[-1].start()
    for copy in copies:
        copy.wait()


def exchange(array, mask):
    return lax.ppermute(array, "seq", [(i, i ^ mask) for i in range(lax.axis_size("seq"))])


def shifted(array, distance):
    count = lax.axis_size("seq")
    return lax.ppermute(array, "seq", [(i, i + distance) for i in range(count - distance)])


def scan_groups(total, groups):
    rows = total.shape[0] - TAIL
    last = shifted(total[rows:], GROUP)
    held, decay = total[:rows].astype(F32), decay_of(total[rows:].astype(F32))
    held = shifted(held, GROUP)
    decay = shifted(decay, GROUP)
    distance = 1
    while distance < groups:
        held = held + decay * shifted(held, GROUP * distance)
        decay = decay * shifted(decay, GROUP * distance)
        distance *= 2
    near_tail = jnp.concatenate([jnp.zeros((X_LAST_AT, last.shape[1]), BF16), last[X_LAST_AT:]], axis=0)
    near = jnp.concatenate([held.astype(BF16), near_tail], axis=0)
    odd = (lax.axis_index("seq") // GROUP) % 2 == 1
    nothing = jnp.zeros_like(near)
    return jnp.where(odd, near, nothing), jnp.where(odd, nothing, near), nothing


def on_device(
    ssm_input, bc_input, conv_taps, conv_bias, bc_taps, bc_bias,
    step_input, step_bias, decay_log, skip_gain, request_offset,
):
    block, channels = ssm_input.shape
    state_size = bc_input.shape[1]
    heads = step_input.shape[0]
    width = channels // GROUP
    groups = lax.axis_size("seq") // GROUP
    here = lax.axis_index("seq")
    hbm = pl.BlockSpec(memory_space=pltpu.HBM)
    vmem = pl.BlockSpec(memory_space=pltpu.VMEM)

    swap = [(i, i ^ 1) for i in range(lax.axis_size("head"))]
    other_bc, other_taps, other_bias = [lax.ppermute(part, "head", swap) for part in (bc_input, bc_taps, bc_bias)]
    other_bias = other_bias[None, :]

    x_main, gated, aux, passing, time_step, rate_sum, x_taps, x_bias, own, own_taps, own_bias, offset = pl.pallas_call(
        channels_kernel,
        out_shape=[
            jax.ShapeDtypeStruct((block, channels), BF16),
            jax.ShapeDtypeStruct((block, channels), BF16),
            jax.ShapeDtypeStruct((24, channels), F32),
            jax.ShapeDtypeStruct((heads, LANES), F32),
            jax.ShapeDtypeStruct((heads, block), F32),
            jax.ShapeDtypeStruct((heads, block), F32),
            jax.ShapeDtypeStruct(conv_taps.shape, F32),
            jax.ShapeDtypeStruct((1, channels), F32),
            jax.ShapeDtypeStruct(bc_input.shape, BF16),
            jax.ShapeDtypeStruct(bc_taps.shape, F32),
            jax.ShapeDtypeStruct((1, state_size), F32),
            jax.ShapeDtypeStruct((1, block), jnp.int32),
        ],
        in_specs=[hbm] * 11,
        out_specs=[vmem] * 12,
        scratch_shapes=[
            pltpu.VMEM((block, channels), BF16),
            pltpu.VMEM((heads, block), F32),
            pltpu.VMEM((1, heads), F32),
            pltpu.VMEM((1, heads), F32),
            pltpu.VMEM((1, heads), F32),
            pltpu.SemaphoreType.DMA((10 + GROUP,)),
        ],
        compiler_params=PARAMS,
        name="channels",
    )(
        *[
            pltpu.with_memory_space_constraint(array, pltpu.HBM)
            for array in (
                ssm_input, conv_taps, conv_bias[None, :], bc_input, bc_taps, bc_bias[None, :], step_input,
                request_offset[None, :], step_bias[None, :], decay_log[None, :], skip_gain[None, :],
            )
        ]
    )

    slice_shape = jax.ShapeDtypeStruct((state_size + TAIL, width), BF16)
    *slices, b_main, b_aux, ends = pl.pallas_call(
        states_kernel,
        out_shape=[slice_shape] * GROUP
        + [
            jax.ShapeDtypeStruct((block, state_size), BF16),
            jax.ShapeDtypeStruct((16, state_size), F32),
            jax.ShapeDtypeStruct((HALO, channels + 2 * state_size), BF16),
        ],
        in_specs=[vmem] * 10,
        out_specs=[vmem] * (GROUP + 3),
        scratch_shapes=[pltpu.VMEM((state_size, block), BF16)],
        compiler_params=PARAMS,
        name="states",
    )(own, other_bc, own_taps, other_taps, own_bias, other_bias, gated, aux, passing, offset)
    halo = shifted(ends, 1)
    received = [slices[0]] + [exchange(slices[k], k) for k in (1, 2, 3)]

    direct = groups == GROUP
    if direct:
        earlier = jnp.zeros((TAIL, width), BF16)
    else:
        last = received[0]
        for k in (1, 2, 3):
            last = jnp.where((here % GROUP) ^ k == GROUP - 1, received[k], last)
        earlier = shifted(last[state_size:], GROUP)
    total = pl.pallas_call(
        lambda *refs: group_kernel(*refs, complete=not direct),
        out_shape=slice_shape,
        in_specs=[vmem] * (GROUP + 4),
        out_specs=vmem,
        compiler_params=PARAMS,
        name="group",
    )(*received, earlier, x_taps, x_bias, b_aux)
    total, halo = lax.optimization_barrier((total, halo))
    if direct:
        far = exchange(total, 2 * GROUP)
        pairs = [(GROUP + k, 2 * GROUP + k) for k in range(GROUP)]
        near_even = lax.ppermute(total, "seq", pairs + [(high, low) for low, high in pairs])
        near_odd = exchange(total, GROUP)
    else:
        near_odd, near_even, far = scan_groups(total, groups)

    entering = pl.pallas_call(
        entering_kernel,
        out_shape=[jax.ShapeDtypeStruct((state_size, width), BF16)] * GROUP,
        in_specs=[vmem] * (GROUP + 6),
        out_specs=[vmem] * GROUP,
        compiler_params=PARAMS,
        name="entering",
    )(*received, near_odd, near_even, far, x_taps, x_bias, b_aux)
    mine = [entering[0]] + [exchange(entering[k], k) for k in (1, 2, 3)]

    intra, c_conv, carry = pl.pallas_call(
        intra_kernel,
        out_shape=[
            jax.ShapeDtypeStruct((block, channels), F32),
            jax.ShapeDtypeStruct((block, state_size), BF16),
            jax.ShapeDtypeStruct((block, channels), F32),
        ],
        in_specs=[vmem] * 15,
        out_specs=[vmem] * 3,
        scratch_shapes=[
            pltpu.VMEM((block, block), F32),
            pltpu.VMEM((block, block), F32),
            pltpu.VMEM((block, heads), F32),
            pltpu.VMEM((block, channels), BF16),
            pltpu.VMEM((block, state_size), BF16),
        ],
        compiler_params=PARAMS,
        cost_estimate=pl.CostEstimate(flops=600_000_000, bytes_accessed=4_000_000, transcendentals=1_000_000),
        name="intra",
    )(
        x_main, aux, halo, own, other_bc, own_taps, other_taps, own_bias, other_bias, b_main, b_aux,
        x_taps, time_step, rate_sum, offset,
    )
    out_shape = jax.ShapeDtypeStruct((block, channels), BF16)
    early = GROUP - 1
    partial = pl.pallas_call(
        lambda *refs: back_kernel(*refs, first=0),
        out_shape=out_shape,
        in_specs=[vmem] * (early + 3),
        out_specs=hbm,
        scratch_shapes=[pltpu.VMEM((early, block, width), BF16), pltpu.SemaphoreType.DMA((early,))],
        compiler_params=PARAMS,
        name="back",
    )(c_conv, *mine[:early], intra, carry)

    def last_slice(c, state, intra, carry, partial, out, held, sems):
        back_kernel(c, state, intra, carry, out, held, sems, first=early)

    return pl.pallas_call(
        last_slice,
        out_shape=out_shape,
        in_specs=[vmem] * 4 + [hbm],
        out_specs=hbm,
        scratch_shapes=[pltpu.VMEM((1, block, width), BF16), pltpu.SemaphoreType.DMA((1,))],
        input_output_aliases={4: 0},
        compiler_params=PARAMS,
        name="last",
    )(c_conv, mine[early], intra, carry, partial)


def solution(mesh):
    return jax.shard_map(
        on_device,
        mesh=mesh,
        in_specs=(
            P("seq", "head"),
            P("seq", "head"),
            P(None, "head"),
            P("head"),
            P(None, "head"),
            P("head"),
            P("head", "seq"),
            P("head"),
            P("head"),
            P("head"),
            P("seq"),
        ),
        out_specs=P("seq", "head"),
        check_vma=False,
    )
```

```python
import jax
import jax.numpy as jnp
from jax import lax
from jax.experimental import pallas as pl
from jax.experimental.pallas import tpu as pltpu
from jax.sharding import PartitionSpec as P

HEADDIM = 64
GROUP = 4
TAIL = 16
GATE_AT, X_LAST_AT, X_FIRST_AT, B_LAST_AT, B_FIRST_AT = 1, 4, 7, 10, 13
HALO = 16
LANES = 128
NEG = -1e30
F32 = jnp.float32
BF16 = jnp.bfloat16
PARAMS = pltpu.CompilerParams(vmem_limit_bytes=24 * 1024 * 1024)


def dot(a, b, dims=((1,), (0,))):
    return lax.dot_general(a, b, (dims, ((), ())), preferred_element_type=F32)


def two_parts(value):
    high = value.astype(BF16).astype(F32)
    return high, value - high


def silu(v):
    return 0.5 * v * (1.0 + jnp.tanh(0.5 * v))


def iota(shape, dim):
    return lax.broadcasted_iota(jnp.int32, shape, dim)


def member_here():
    return lax.axis_index("seq") % GROUP


def group_here():
    return lax.axis_index("seq") // GROUP


def holds_b():
    return lax.axis_index("head") % 2 == 0


def column(row):
    shape = (row.shape[1], row.shape[1])
    wide = jnp.broadcast_to(row, shape)
    return jnp.sum(jnp.where(iota(shape, 0) == iota(shape, 1), wide, 0.0), axis=1, keepdims=True)


def spread(parts, first_channel, width):
    heads = parts.shape[1] // 2
    shape = (2 * heads, width)
    head = iota(shape, 0) & (heads - 1)
    channel = iota(shape, 1) + first_channel
    return dot(parts, (channel // HEADDIM == head).astype(F32).astype(BF16))


def turned(per_head):
    high, low = two_parts(per_head)
    return jnp.concatenate([high, low], axis=0).T.astype(BF16)


def rates(step, step_bias, decay_log):
    heads, block = step.shape
    time_step = jax.nn.softplus(step + step_bias)
    log_decay = -jnp.exp(decay_log) * time_step
    shape = (block, block)
    upto = (iota(shape, 0) <= iota(shape, 1)).astype(F32).astype(BF16)
    first, rest = two_parts(log_decay)
    second, third = two_parts(rest)
    sums = dot(jnp.concatenate([first, second, third], axis=0).astype(BF16), upto)
    return time_step, sums[0:heads] + (sums[heads : 2 * heads] + sums[2 * heads :])


def offset_columns(offset_row):
    wide = jnp.broadcast_to(offset_row.astype(F32), (LANES, offset_row.shape[1]))
    return wide.T


def lag_matrices(offset_col, count):
    block = offset_col.shape[0]
    gap = iota((block, block), 0) - iota((block, block), 1)
    offset_wide = jnp.concatenate([offset_col] * (block // LANES), axis=1)
    return [
        jnp.where(jnp.logical_and(gap == lag, offset_wide >= lag), 1.0, 0.0).astype(BF16)
        for lag in range(1, count)
    ]


def convolve(source, taps, bias, lags):
    count = len(lags) + 1
    total = taps[count - 1 : count] * source.astype(F32) + bias
    for lag, matrix in enumerate(lags, 1):
        total = total + taps[count - 1 - lag : count - lag] * dot(matrix, source)
    return total


def quarter(k, width):
    return pl.ds(pl.multiple_of((member_here() ^ k) * width, width), width)


def channel_slice(k, slot, x, taps, bias, lags, late_parts, early_parts, x_out, gated, aux):
    block = x.shape[0]
    width = x.shape[1] // GROUP
    cols, to = quarter(k, width), slice(slot * width, (slot + 1) * width)
    source = x[:, cols]
    before = convolve(source, taps[:, cols], bias[:, cols], [lags[lag] for lag in range(lags.shape[0])])
    value = silu(before).astype(BF16)
    x_out[:, to] = value
    first_channel = (member_here() ^ k) * width
    gated[:, to] = (value.astype(F32) * spread(late_parts[...], first_channel, width)).astype(BF16)
    aux[0:8, to] = before[0:8]
    early = spread(early_parts[...], first_channel, width)
    first = source[0:TAIL].astype(F32)
    last_rows = source[block - TAIL : block].astype(F32)
    aux[8:24, to] = jnp.concatenate(
        [early[3:4], early[0:3], last_rows[TAIL - 3 :], first[0:3], jnp.zeros((TAIL - 10, width), F32)], axis=0
    )


def channels_kernel(
    x_hbm, taps_hbm, bias_hbm, own_hbm, own_taps_hbm, own_bias_hbm, step_hbm, offset_hbm,
    step_bias_hbm, decay_hbm, skip_hbm,
    x_out, gated, aux, passing_out, step_out, sums_out, x, taps, bias, own, own_taps, own_bias, offset,
    lags, late_parts, early_parts, step, step_bias, decay_log, skip, sems,
):
    block = x.shape[0]
    count = taps.shape[0]
    pairs = [
        (x_hbm, x), (offset_hbm, offset), (step_hbm, step), (step_bias_hbm, step_bias), (decay_hbm, decay_log),
        (skip_hbm, skip), (taps_hbm, taps), (bias_hbm, bias), (own_taps_hbm, own_taps), (own_bias_hbm, own_bias),
        (own_hbm, own),
    ]
    copies = [pltpu.make_async_copy(*pair, sems.at[k]) for k, pair in enumerate(pairs)]
    for copy in copies:
        copy.start()
    for copy in copies[1:8]:
        copy.wait()
    for lag, matrix in enumerate(lag_matrices(offset_columns(offset[...]), count)):
        lags[lag] = matrix
    time_step, rate_sum = rates(step[...], column(step_bias[...]), column(decay_log[...]))
    step_out[...] = time_step
    sums_out[...] = rate_sum
    last_offset = offset[0, block - 1]
    place = iota(rate_sum.shape, 1)
    last = rate_sum[:, block - 1 : block]
    gate = jnp.exp(jnp.where(last_offset >= block - 1 - place, last - rate_sum, NEG)) * time_step
    passing = jnp.exp(last) * (last_offset >= block).astype(F32)
    passing_out[...] = jnp.broadcast_to(passing, passing_out.shape)
    early_parts[...] = turned(jnp.where(place == count - 1, column(skip[...]), gate))[0:TAIL]
    late_parts[...] = turned(jnp.where(place >= count - 1, gate, 0.0))
    copies[0].wait()
    for slot, k in enumerate((1, 2, 3)):
        channel_slice(k, slot, x, taps, bias, lags, late_parts, early_parts, x_out, gated, aux)
    for copy in copies[8:]:
        copy.wait()


def message(out, k, state, passing, offset, count, gates_and_x, b_tail):
    rows, width = state.shape
    heads = passing.shape[0]
    slice_heads = heads // GROUP
    out[0:rows, :] = state.astype(BF16)
    lane = iota((heads, width), 1)
    head = iota((heads, width), 0)
    high, low = two_parts(passing[:, 0:1])
    offsets = pltpu.roll(jnp.minimum(offset[...], count - 1).astype(F32), 2 * slice_heads, 1)
    offsets = jnp.where(
        jnp.logical_and(lane[0:1] >= 2 * slice_heads, lane[0:1] < 2 * slice_heads + count - 1), offsets, 0.0
    )
    at = lane + (member_here() ^ k) * slice_heads
    packed = jnp.where(lane < slice_heads, jnp.where(at == head, high, 0.0), 0.0)
    packed = jnp.where(jnp.logical_and(lane >= slice_heads, at == head + slice_heads), low, packed)
    packed = jnp.where(lane < 2 * slice_heads, packed, 0.0)
    misc = jnp.sum(packed, axis=0, keepdims=True) + offsets
    row = iota((TAIL, width), 0)
    tail = jnp.where(row == 0, misc, jnp.where(row < B_LAST_AT, gates_and_x, b_tail))
    out[rows:, :] = tail.astype(BF16)


def states_kernel(
    x, own, other, own_taps, other_taps, own_bias, other_bias, lags, gated, aux, passing, offset,
    s1, s2, s3, b_out, b_taps, b_tail, turn, ends,
):
    first = holds_b()
    block, state_size = own.shape
    count = own_taps.shape[0]
    channels = x.shape[1]
    ends[:, 0:channels] = x[block - HALO : block, :]
    ends[:, channels : channels + state_size] = own[block - HALO : block, :]
    ends[:, channels + state_size :] = other[block - HALO : block, :]
    taps = jnp.where(first, own_taps[...], other_taps[...])
    bias = jnp.where(first, own_bias[...], other_bias[...])
    source = jnp.where(first, own[...].astype(F32), other[...].astype(F32))
    before = convolve(source.astype(BF16), taps, bias, [lags[lag] for lag in range(count - 1)])
    value = silu(before)
    b_out[...] = value.astype(BF16)
    turn[...] = value.T.astype(BF16)
    b_taps[...] = jnp.concatenate([taps, bias, jnp.zeros((8 - count - 1, state_size), F32), before[0:8]], axis=0)
    b_tail[...] = jnp.concatenate(
        [jnp.zeros((B_LAST_AT, state_size), F32), source[block - 3 :], source[0:3]], axis=0
    )
    width = gated.shape[1] // (GROUP - 1)
    for slot, (k, out) in enumerate(((1, s1), (2, s2), (3, s3))):
        cols = slice(slot * width, (slot + 1) * width)
        message(out, k, dot(turn[...], gated[:, cols]), passing, offset, count, aux[8:24, cols], b_tail[...])


def rest_kernel(
    x, taps, bias, lags, late_parts, early_parts, passing, offset, turn, b_tail, s0, x_out, aux, gated,
):
    channel_slice(0, 0, x, taps, bias, lags, late_parts, early_parts, x_out, gated, aux)
    state = dot(turn[...], gated[...])
    message(s0, 0, state, passing, offset, taps.shape[0], aux[8:24, :], b_tail[...])


def tail_of(state):
    rows = state.shape[0]
    return state[rows - TAIL : rows, :].astype(F32)


def decay_of(tail):
    width = tail.shape[1]
    slice_heads = width // HEADDIM
    channel = iota((1, width), 1)
    value = jnp.zeros((1, width), F32)
    for head in range(slice_heads):
        both = tail[0:1, head : head + 1] + tail[0:1, slice_heads + head : slice_heads + head + 1]
        value = jnp.where(channel // HEADDIM == head, both, value)
    return value


def pack_decay(decay, tail):
    width = decay.shape[1]
    slice_heads = width // HEADDIM
    lane = iota((1, width), 1)
    high, low = two_parts(decay)
    row = jnp.where(lane >= 2 * slice_heads, tail[0:1], 0.0)
    for head in range(slice_heads):
        at = head * HEADDIM
        row = jnp.where(lane == head, high[:, at : at + 1], row)
        row = jnp.where(lane == slice_heads + head, low[:, at : at + 1], row)
    return row


def tail_taps(x_taps, x_bias, b_taps, count):
    width = x_taps.shape[1]
    upper = iota((TAIL, width), 0) < B_LAST_AT
    taps = [jnp.where(upper, x_taps[k : k + 1], b_taps[k : k + 1]) for k in range(count)]
    return taps, jnp.where(upper, x_bias, b_taps[count : count + 1])


def early_tokens(tail, earlier, taps, bias):
    width = tail.shape[1]
    slice_heads = width // HEADDIM
    count = len(taps)
    row = iota(tail.shape, 0)
    is_last = jnp.logical_or(
        jnp.logical_and(row >= X_LAST_AT, row < X_FIRST_AT),
        jnp.logical_and(row >= B_LAST_AT, row < B_FIRST_AT),
    )
    rows = jnp.where(is_last, earlier, tail)
    offset = jnp.full(tail.shape, -1.0, F32)
    for token in range(count - 1):
        lane = 2 * slice_heads + token
        here = jnp.logical_or(row == X_FIRST_AT + token, row == B_FIRST_AT + token)
        offset = jnp.where(here, tail[0:1, lane : lane + 1], offset)
    total = taps[count - 1] * rows + bias
    for lag in range(1, count):
        total = total + taps[count - 1 - lag] * jnp.where(offset >= lag, pltpu.roll(rows, lag, 0), 0.0)
    value = silu(total).astype(BF16).astype(F32)
    gate = pltpu.roll(tail, B_FIRST_AT - GATE_AT, 0)
    wanted = row >= B_FIRST_AT
    b = jnp.where(wanted, value, 0.0)
    x = jnp.where(wanted, pltpu.roll(value, B_FIRST_AT - X_FIRST_AT, 0) * gate, 0.0)
    return b, x


def group_kernel(r3, r1, r2, r0, earlier, x_taps, x_bias, b_taps, total, *, complete):
    rows = r0.shape[0] - TAIL
    width = r0.shape[1]
    count = x_taps.shape[0]
    held = (r0, r1, r2, r3)

    def run(member):
        cols = slice(member * width, (member + 1) * width)
        taps, bias = tail_taps(x_taps[:, cols], x_bias[:, cols], b_taps[...], count)
        states = [held[member ^ k] for k in range(GROUP)]
        tails = [tail_of(state) for state in states]
        decays = [decay_of(tail) for tail in tails]
        factors = [None] * GROUP
        factor = jnp.ones((1, width), F32)
        for k in reversed(range(GROUP)):
            factors[k] = factor
            factor = factor * decays[k]
        early_b, early_x = [], []
        for k in range(0 if complete else 1, GROUP):
            before = tails[k - 1] if k else tail_of(earlier)
            b, x = early_tokens(tails[k], before, taps, bias)
            early_b.append(b)
            early_x.append(x * factors[k])
        b_turned = jnp.concatenate(early_b, axis=0).T.astype(BF16)
        added = dot(b_turned, jnp.concatenate(early_x, axis=0).astype(BF16))
        step = 64
        for top in range(0, rows, step):
            part = slice(top, top + step)
            value = added[part]
            for k in range(GROUP):
                value = value + factors[k] * states[k][part, :].astype(F32)
            total[part, :] = value.astype(BF16)
        row = iota((TAIL, width), 0)
        is_last = jnp.logical_or(
            jnp.logical_and(row >= X_LAST_AT, row < X_FIRST_AT),
            jnp.logical_and(row >= B_LAST_AT, row < B_FIRST_AT),
        )
        gates = jnp.zeros((1, width), F32) if complete else factors[0]
        tail = jnp.where(is_last, tails[GROUP - 1], tails[0])
        tail = jnp.where(row < X_LAST_AT, tail * gates, tail)
        tail = jnp.where(row == 0, pack_decay(factor, tails[0]), tail)
        total[rows:, :] = tail.astype(BF16)

    for member in range(GROUP):
        pl.when(member_here() == member)(lambda member=member: run(member))


def entering_kernel(
    r3, r1, r2, r0, near_even, far, near_odd, x_taps, x_bias, b_taps, e0, e1, e2, e3
):
    group = group_here()
    odd = (group & 1) == 1
    one = jnp.ones((1, r0.shape[1]), F32)
    from_odd = jnp.where(odd, one, 0.0)
    from_even = jnp.where(jnp.logical_and(group >= 2, jnp.logical_not(odd)), one, 0.0)
    from_far = jnp.where(group >= 2, one, 0.0)
    rows = r0.shape[0] - TAIL
    width = r0.shape[1]
    count = x_taps.shape[0]
    held, outs = (r0, r1, r2, r3), (e0, e1, e2, e3)

    def run(member):
        cols = slice(member * width, (member + 1) * width)
        taps, bias = tail_taps(x_taps[:, cols], x_bias[:, cols], b_taps[...], count)
        states = [held[member ^ k] for k in range(GROUP)]
        targets = [outs[member ^ k] for k in range(GROUP)]
        tails = [tail_of(state) for state in states]
        near_tail = from_odd * tail_of(near_odd) + from_even * tail_of(near_even)
        far_tail = from_far * tail_of(far)
        decays = [decay_of(tail) for tail in tails]
        near_decay = decay_of(near_tail)
        far_factor = near_decay * from_far
        far_b, far_x = early_tokens(far_tail, jnp.zeros_like(far_tail), taps, bias)
        near_b, near_x = early_tokens(near_tail, far_tail, taps, bias)
        early_b, early_x = [far_b, near_b], [far_x * near_decay, near_x]
        for k in range(GROUP - 1):
            b, x = early_tokens(tails[k], tails[k - 1] if k else near_tail, taps, bias)
            early_b.append(b)
            early_x.append(x)
        b_turned = jnp.concatenate(early_b, axis=0).T.astype(BF16)
        x_rows = jnp.concatenate(early_x, axis=0).astype(BF16)
        added = [dot(b_turned[:, : 2 * TAIL], x_rows[: 2 * TAIL])]
        for k in range(GROUP - 1):
            part = slice((k + 2) * TAIL, (k + 3) * TAIL)
            added.append(dot(b_turned[:, part], x_rows[part]))
        step = 32
        for top in range(0, rows, step):
            part = slice(top, top + step)
            value = from_odd * near_odd[part, :].astype(F32) + from_even * near_even[part, :].astype(F32)
            value = value + far_factor * far[part, :].astype(F32) + added[0][part]
            targets[0][part, :] = value.astype(BF16)
            for k in range(GROUP - 1):
                value = decays[k] * value + states[k][part, :].astype(F32) + added[k + 1][part]
                targets[k + 1][part, :] = value.astype(BF16)

    for member in range(GROUP):
        pl.when(member_here() == member)(lambda member=member: run(member))


def patched(before, halo, taps, offset_col):
    width = before.shape[1]
    count = taps.shape[0]
    extended = jnp.concatenate([halo[HALO - 8 :].astype(F32), jnp.zeros((8, width), F32)], axis=0)
    total = before
    for lag in range(1, count):
        shifted_rows = extended[8 - lag : 16 - lag]
        total = total + taps[count - 1 - lag : count - lag] * jnp.where(
            offset_col[0:8, 0:1] >= lag, shifted_rows, 0.0
        )
    return silu(total)


def intra_kernel(
    x_early, x_late, aux_early, aux_late, halo, own, other, own_taps, other_taps, own_bias, other_bias, b, b_aux,
    x_taps, step, sums, offset, lags, y, c_out, carry, bias, scores, columns, x_full, b_full, aux,
):
    first = holds_b()
    block, channels = x_full.shape
    heads = step.shape[0]
    state_size = b.shape[1]
    width = channels // GROUP
    for k, (part, rows, slot) in enumerate(
        ((x_late, aux_late, 0), (x_early, aux_early, 0), (x_early, aux_early, 1), (x_early, aux_early, 2))
    ):
        source = slice(slot * width, (slot + 1) * width)
        x_full[:, quarter(k, width)] = part[:, source]
        aux[:, quarter(k, width)] = rows[0:16, source]
    count = x_taps.shape[0]
    half = block // 2
    time_step, rate_sum = step[...], sums[...]
    columns[...] = rate_sum.T
    offset_col = offset_columns(offset[...])

    early = patched(aux[0:8, :], halo[:, 0:channels], x_taps[...], offset_col)
    x_full[0:16, :] = jnp.concatenate([early, x_full[0:16, :].astype(F32)[8:16]], axis=0).astype(BF16)
    own_halo = halo[:, channels : channels + state_size].astype(F32)
    other_halo = halo[:, channels + state_size :].astype(F32)
    b_full[...] = b[...]
    early = patched(b_aux[8:16, :], jnp.where(first, own_halo, other_halo), b_aux[0:count, :], offset_col)
    b_full[0:16, :] = jnp.concatenate([early, b[0:16, :].astype(F32)[8:16]], axis=0).astype(BF16)
    c_taps = jnp.where(first, other_taps[...], own_taps[...])
    c_bias = jnp.where(first, other_bias[...], own_bias[...])
    c_source = jnp.where(first, other[...].astype(F32), own[...].astype(F32)).astype(BF16)
    before = convolve(c_source, c_taps, c_bias, [lags[lag] for lag in range(count - 1)])
    c_value = silu(before)
    early = patched(before[0:8], jnp.where(first, other_halo, own_halo), c_taps, offset_col)
    c_out[...] = c_value.astype(BF16)
    c_out[0:16, :] = jnp.concatenate([early, c_value[8:16]], axis=0).astype(BF16)

    row = iota((block, LANES), 0)
    for left in range(0, block, LANES):
        gap = row - (iota((block, LANES), 1) + left)
        linked = jnp.logical_and(gap >= 0, offset_col >= gap.astype(F32))
        bias[:, left : left + LANES] = jnp.where(linked, 0.0, NEG)
    scores[...] = dot(c_out[...], b_full[...], ((1,), (1,)))
    reach = rate_sum - jnp.log(time_step)
    starts = iota(rate_sum.shape, 1) + 1
    factor = turned(jnp.where(offset[...] >= starts, jnp.exp(rate_sum), 0.0))
    for k in range(GROUP):
        carry[:, k * width : (k + 1) * width] = spread(factor, k * width, width)
    lane = iota((1, LANES), 1)
    per_tile = LANES // HEADDIM
    for tile in range(heads // per_tile):
        cols = slice(tile * LANES, (tile + 1) * LANES)
        skip_row = aux[8:9, cols]
        for top in range(0, block, half):
            part = slice(top, top + half)
            seen = top + half
            value = skip_row * x_full[part, cols].astype(F32)
            for k in range(per_tile):
                h = tile * per_tile + k
                gap = columns[part, h : h + 1] - reach[h : h + 1, 0:seen] + bias[part, 0:seen]
                weights = (scores[part, 0:seen] * jnp.exp(gap)).astype(BF16)
                chosen = jnp.where(lane // HEADDIM == k, x_full[0:seen, cols], jnp.zeros((), BF16))
                value = value + dot(weights, chosen)
            y[part, cols] = value


def back_kernel(c, f3, f1, f2, f0, intra, carry, out, held, sems):
    member = member_here()
    width = out.shape[1] // GROUP
    copies = []
    for k, state in enumerate((f0, f1, f2, f3)):
        cols = pl.ds(pl.multiple_of((member ^ k) * width, width), width)
        value = intra[:, cols] + carry[:, cols] * dot(c[...], state[...])
        held[k] = value.astype(BF16)
        copies.append(pltpu.make_async_copy(held.at[k], out.at[:, cols], sems.at[k]))
        copies[-1].start()
    for copy in copies:
        copy.wait()


def exchange(array, mask):
    return lax.ppermute(array, "seq", [(i, i ^ mask) for i in range(lax.axis_size("seq"))])


def shifted(array, distance):
    count = lax.axis_size("seq")
    return lax.ppermute(array, "seq", [(i, i + distance) for i in range(count - distance)])


def scan_groups(total, groups):
    rows = total.shape[0] - TAIL
    last = shifted(total[rows:], GROUP)
    held, decay = total[:rows].astype(F32), decay_of(total[rows:].astype(F32))
    held = shifted(held, GROUP)
    decay = shifted(decay, GROUP)
    distance = 1
    while distance < groups:
        held = held + decay * shifted(held, GROUP * distance)
        decay = decay * shifted(decay, GROUP * distance)
        distance *= 2
    near_tail = jnp.concatenate([jnp.zeros((X_LAST_AT, last.shape[1]), BF16), last[X_LAST_AT:]], axis=0)
    near = jnp.concatenate([held.astype(BF16), near_tail], axis=0)
    odd = (lax.axis_index("seq") // GROUP) % 2 == 1
    nothing = jnp.zeros_like(near)
    return jnp.where(odd, near, nothing), jnp.where(odd, nothing, near), nothing


def on_device(
    ssm_input, bc_input, conv_taps, conv_bias, bc_taps, bc_bias,
    step_input, step_bias, decay_log, skip_gain, request_offset,
):
    block, channels = ssm_input.shape
    state_size = bc_input.shape[1]
    heads = step_input.shape[0]
    width = channels // GROUP
    groups = lax.axis_size("seq") // GROUP
    here = lax.axis_index("seq")
    hbm = pl.BlockSpec(memory_space=pltpu.HBM)
    vmem = pl.BlockSpec(memory_space=pltpu.VMEM)

    swap = [(i, i ^ 1) for i in range(lax.axis_size("head"))]
    other_bc, other_taps, other_bias = [lax.ppermute(part, "head", swap) for part in (bc_input, bc_taps, bc_bias)]
    other_bias = other_bias[None, :]

    others = jax.ShapeDtypeStruct((block, (GROUP - 1) * width), BF16)
    slice_shape = jax.ShapeDtypeStruct((state_size + TAIL, width), BF16)
    (
        x_early, gated, aux_early, passing, time_step, rate_sum, x, x_taps, x_bias, own, own_taps, own_bias, offset,
        lags, late_parts, early_parts,
    ) = pl.pallas_call(
        channels_kernel,
        out_shape=[
            others,
            others,
            jax.ShapeDtypeStruct((24, (GROUP - 1) * width), F32),
            jax.ShapeDtypeStruct((heads, LANES), F32),
            jax.ShapeDtypeStruct((heads, block), F32),
            jax.ShapeDtypeStruct((heads, block), F32),
            jax.ShapeDtypeStruct((block, channels), BF16),
            jax.ShapeDtypeStruct(conv_taps.shape, F32),
            jax.ShapeDtypeStruct((1, channels), F32),
            jax.ShapeDtypeStruct(bc_input.shape, BF16),
            jax.ShapeDtypeStruct(bc_taps.shape, F32),
            jax.ShapeDtypeStruct((1, state_size), F32),
            jax.ShapeDtypeStruct((1, block), jnp.int32),
            jax.ShapeDtypeStruct((conv_taps.shape[0] - 1, block, block), BF16),
            jax.ShapeDtypeStruct((block, 2 * heads), BF16),
            jax.ShapeDtypeStruct((TAIL, 2 * heads), BF16),
        ],
        in_specs=[hbm] * 11,
        out_specs=[vmem] * 16,
        scratch_shapes=[
            pltpu.VMEM((heads, block), F32),
            pltpu.VMEM((1, heads), F32),
            pltpu.VMEM((1, heads), F32),
            pltpu.VMEM((1, heads), F32),
            pltpu.SemaphoreType.DMA((11,)),
        ],
        compiler_params=PARAMS,
        name="channels",
    )(
        *[
            pltpu.with_memory_space_constraint(array, pltpu.HBM)
            for array in (
                ssm_input, conv_taps, conv_bias[None, :], bc_input, bc_taps, bc_bias[None, :], step_input,
                request_offset[None, :], step_bias[None, :], decay_log[None, :], skip_gain[None, :],
            )
        ]
    )
    s1, s2, s3, b_main, b_aux, b_tail, turn, ends = pl.pallas_call(
        states_kernel,
        out_shape=[
            slice_shape,
            slice_shape,
            slice_shape,
            jax.ShapeDtypeStruct((block, state_size), BF16),
            jax.ShapeDtypeStruct((16, state_size), F32),
            jax.ShapeDtypeStruct((TAIL, state_size), F32),
            jax.ShapeDtypeStruct((state_size, block), BF16),
            jax.ShapeDtypeStruct((HALO, channels + 2 * state_size), BF16),
        ],
        in_specs=[vmem] * 12,
        out_specs=[vmem] * 8,
        compiler_params=PARAMS,
        name="states",
    )(x, own, other_bc, own_taps, other_taps, own_bias, other_bias, lags, gated, aux_early, passing, offset)
    r1, r2, r3 = exchange(s1, 1), exchange(s2, 2), exchange(s3, 3)
    halo = shifted(ends, 1)
    s0, x_late, aux_late = pl.pallas_call(
        rest_kernel,
        out_shape=[
            slice_shape,
            jax.ShapeDtypeStruct((block, width), BF16),
            jax.ShapeDtypeStruct((24, width), F32),
        ],
        in_specs=[vmem] * 10,
        out_specs=[vmem] * 3,
        scratch_shapes=[pltpu.VMEM((block, width), BF16)],
        compiler_params=PARAMS,
        cost_estimate=pl.CostEstimate(flops=400_000_000, bytes_accessed=2_000_000, transcendentals=200_000),
        name="rest",
    )(x, x_taps, x_bias, lags, late_parts, early_parts, passing, offset, turn, b_tail)
    received = [s0, r1, r2, r3]

    direct = groups == GROUP
    if direct:
        earlier = jnp.zeros((TAIL, width), BF16)
    else:
        last = received[0]
        for k in (1, 2, 3):
            last = jnp.where((here % GROUP) ^ k == GROUP - 1, received[k], last)
        earlier = shifted(last[state_size:], GROUP)
    total = pl.pallas_call(
        lambda *refs: group_kernel(*refs, complete=not direct),
        out_shape=slice_shape,
        in_specs=[vmem] * (GROUP + 4),
        out_specs=vmem,
        compiler_params=PARAMS,
        name="group",
    )(r3, r1, r2, s0, earlier, x_taps, x_bias, b_aux)
    total, halo = lax.optimization_barrier((total, halo))
    if direct:
        far = exchange(total, 2 * GROUP)
        pairs = [(GROUP + k, 2 * GROUP + k) for k in range(GROUP)]
        near_even = lax.ppermute(total, "seq", pairs + [(high, low) for low, high in pairs])
        near_odd = exchange(total, GROUP)
    else:
        near_odd, near_even, far = scan_groups(total, groups)

    entering = pl.pallas_call(
        entering_kernel,
        out_shape=[jax.ShapeDtypeStruct((state_size, width), BF16)] * GROUP,
        in_specs=[vmem] * (GROUP + 6),
        out_specs=[vmem] * GROUP,
        compiler_params=PARAMS,
        name="entering",
    )(r3, r1, r2, s0, near_even, far, near_odd, x_taps, x_bias, b_aux)
    mine = [entering[0]] + [exchange(entering[k], k) for k in (1, 2, 3)]

    intra, c_conv, carry = pl.pallas_call(
        intra_kernel,
        out_shape=[
            jax.ShapeDtypeStruct((block, channels), F32),
            jax.ShapeDtypeStruct((block, state_size), BF16),
            jax.ShapeDtypeStruct((block, channels), F32),
        ],
        in_specs=[vmem] * 18,
        out_specs=[vmem] * 3,
        scratch_shapes=[
            pltpu.VMEM((block, block), F32),
            pltpu.VMEM((block, block), F32),
            pltpu.VMEM((block, heads), F32),
            pltpu.VMEM((block, channels), BF16),
            pltpu.VMEM((block, state_size), BF16),
            pltpu.VMEM((16, channels), F32),
        ],
        compiler_params=PARAMS,
        cost_estimate=pl.CostEstimate(flops=600_000_000, bytes_accessed=4_000_000, transcendentals=1_000_000),
        name="intra",
    )(
        x_early, x_late, aux_early, aux_late, halo, own, other_bc, own_taps, other_taps, own_bias, other_bias,
        b_main, b_aux, x_taps, time_step, rate_sum, offset, lags,
    )
    out_shape = jax.ShapeDtypeStruct((block, channels), BF16)
    return pl.pallas_call(
        back_kernel,
        out_shape=out_shape,
        in_specs=[vmem] * (GROUP + 3),
        out_specs=hbm,
        scratch_shapes=[pltpu.VMEM((GROUP, block, width), BF16), pltpu.SemaphoreType.DMA((GROUP,))],
        compiler_params=PARAMS,
        name="back",
    )(c_conv, mine[3], mine[1], mine[2], mine[0], intra, carry)


def solution(mesh):
    return jax.shard_map(
        on_device,
        mesh=mesh,
        in_specs=(
            P("seq", "head"),
            P("seq", "head"),
            P(None, "head"),
            P("head"),
            P(None, "head"),
            P("head"),
            P("head", "seq"),
            P("head"),
            P("head"),
            P("head"),
            P("seq"),
        ),
        out_specs=P("seq", "head"),
        check_vma=False,
    )
```

```python
import jax
import jax.numpy as jnp
from jax import lax
from jax.experimental import pallas as pl
from jax.experimental.pallas import tpu as pltpu
from jax.sharding import PartitionSpec as P

HEADDIM = 64
GROUP = 4
TAIL = 16
GATE_AT, X_LAST_AT, X_FIRST_AT, B_LAST_AT, B_FIRST_AT = 1, 4, 7, 10, 13
HALO = 16
LANES = 128
NEG = -1e30
F32 = jnp.float32
BF16 = jnp.bfloat16
PARAMS = pltpu.CompilerParams(vmem_limit_bytes=24 * 1024 * 1024)


def dot(a, b, dims=((1,), (0,))):
    return lax.dot_general(a, b, (dims, ((), ())), preferred_element_type=F32)


def two_parts(value):
    high = value.astype(BF16).astype(F32)
    return high, value - high


def silu(v):
    return 0.5 * v * (1.0 + jnp.tanh(0.5 * v))


def iota(shape, dim):
    return lax.broadcasted_iota(jnp.int32, shape, dim)


def member_here():
    return lax.axis_index("seq") % GROUP


def group_here():
    return lax.axis_index("seq") // GROUP


def holds_b():
    return lax.axis_index("head") % 2 == 0


def column(row):
    shape = (row.shape[1], row.shape[1])
    wide = jnp.broadcast_to(row, shape)
    return jnp.sum(jnp.where(iota(shape, 0) == iota(shape, 1), wide, 0.0), axis=1, keepdims=True)


def spread(parts, first_channel, width):
    heads = parts.shape[1] // 2
    shape = (2 * heads, width)
    head = iota(shape, 0) & (heads - 1)
    channel = iota(shape, 1) + first_channel
    return dot(parts, (channel // HEADDIM == head).astype(F32).astype(BF16))


def turned(per_head):
    high, low = two_parts(per_head)
    return jnp.concatenate([high, low], axis=0).T.astype(BF16)


def rates(step, step_bias, decay_log):
    heads, block = step.shape
    time_step = jax.nn.softplus(step + step_bias)
    log_decay = -jnp.exp(decay_log) * time_step
    shape = (block, block)
    upto = (iota(shape, 0) <= iota(shape, 1)).astype(F32).astype(BF16)
    first, rest = two_parts(log_decay)
    second, third = two_parts(rest)
    sums = dot(jnp.concatenate([first, second, third], axis=0).astype(BF16), upto)
    return time_step, sums[0:heads] + (sums[heads : 2 * heads] + sums[2 * heads :])


def offset_columns(offset_row):
    wide = jnp.broadcast_to(offset_row.astype(F32), (LANES, offset_row.shape[1]))
    return wide.T


def lag_matrices(offset_col, count):
    block = offset_col.shape[0]
    gap = iota((block, block), 0) - iota((block, block), 1)
    offset_wide = jnp.concatenate([offset_col] * (block // LANES), axis=1)
    return [
        jnp.where(jnp.logical_and(gap == lag, offset_wide >= lag), 1.0, 0.0).astype(BF16)
        for lag in range(1, count)
    ]


def convolve(source, taps, bias, lags):
    count = len(lags) + 1
    total = taps[count - 1 : count] * source.astype(F32) + bias
    for lag, matrix in enumerate(lags, 1):
        total = total + taps[count - 1 - lag : count - lag] * dot(matrix, source)
    return total


def quarter(k, width):
    return pl.ds(pl.multiple_of((member_here() ^ k) * width, width), width)


def channel_slice(k, slot, x, taps, bias, lags, late_parts, early_parts, x_out, gated, aux):
    block = x.shape[0]
    width = x.shape[1] // GROUP
    cols, to = quarter(k, width), slice(slot * width, (slot + 1) * width)
    source = x[:, cols]
    before = convolve(source, taps[:, cols], bias[:, cols], [lags[lag] for lag in range(lags.shape[0])])
    value = silu(before).astype(BF16)
    x_out[:, to] = value
    first_channel = (member_here() ^ k) * width
    gated[:, to] = (value.astype(F32) * spread(late_parts[...], first_channel, width)).astype(BF16)
    aux[0:8, to] = before[0:8]
    early = spread(early_parts[...], first_channel, width)
    first = source[0:TAIL].astype(F32)
    last_rows = source[block - TAIL : block].astype(F32)
    aux[8:24, to] = jnp.concatenate(
        [early[3:4], early[0:3], last_rows[TAIL - 3 :], first[0:3], jnp.zeros((TAIL - 10, width), F32)], axis=0
    )


def channels_kernel(
    x_hbm, taps_hbm, bias_hbm, own_hbm, own_taps_hbm, own_bias_hbm, step_hbm, offset_hbm,
    step_bias_hbm, decay_hbm, skip_hbm,
    x_out, gated, aux, passing_out, step_out, sums_out, x, taps, bias, own, own_taps, own_bias, offset,
    lags, late_parts, early_parts, step, step_bias, decay_log, skip, sems,
):
    block = x.shape[0]
    count = taps.shape[0]
    pairs = [
        (x_hbm, x), (offset_hbm, offset), (step_hbm, step), (step_bias_hbm, step_bias), (decay_hbm, decay_log),
        (skip_hbm, skip), (taps_hbm, taps), (bias_hbm, bias), (own_taps_hbm, own_taps), (own_bias_hbm, own_bias),
        (own_hbm, own),
    ]
    copies = [pltpu.make_async_copy(*pair, sems.at[k]) for k, pair in enumerate(pairs)]
    for copy in copies:
        copy.start()
    for copy in copies[1:8]:
        copy.wait()
    for lag, matrix in enumerate(lag_matrices(offset_columns(offset[...]), count)):
        lags[lag] = matrix
    time_step, rate_sum = rates(step[...], column(step_bias[...]), column(decay_log[...]))
    step_out[...] = time_step
    sums_out[...] = rate_sum
    last_offset = offset[0, block - 1]
    place = iota(rate_sum.shape, 1)
    last = rate_sum[:, block - 1 : block]
    gate = jnp.exp(jnp.where(last_offset >= block - 1 - place, last - rate_sum, NEG)) * time_step
    passing = jnp.exp(last) * (last_offset >= block).astype(F32)
    passing_out[...] = jnp.broadcast_to(passing, passing_out.shape)
    early_parts[...] = turned(jnp.where(place == count - 1, column(skip[...]), gate))[0:TAIL]
    late_parts[...] = turned(jnp.where(place >= count - 1, gate, 0.0))
    copies[0].wait()
    for slot, k in enumerate((1, 2, 3)):
        channel_slice(k, slot, x, taps, bias, lags, late_parts, early_parts, x_out, gated, aux)
    for copy in copies[8:]:
        copy.wait()


def message(out, k, state, passing, offset, count, gates_and_x, b_tail):
    rows, width = state.shape
    heads = passing.shape[0]
    slice_heads = heads // GROUP
    out[0:rows, :] = state.astype(BF16)
    lane = iota((heads, width), 1)
    head = iota((heads, width), 0)
    high, low = two_parts(passing[:, 0:1])
    offsets = pltpu.roll(jnp.minimum(offset[...], count - 1).astype(F32), 2 * slice_heads, 1)
    offsets = jnp.where(
        jnp.logical_and(lane[0:1] >= 2 * slice_heads, lane[0:1] < 2 * slice_heads + count - 1), offsets, 0.0
    )
    at = lane + (member_here() ^ k) * slice_heads
    packed = jnp.where(lane < slice_heads, jnp.where(at == head, high, 0.0), 0.0)
    packed = jnp.where(jnp.logical_and(lane >= slice_heads, at == head + slice_heads), low, packed)
    packed = jnp.where(lane < 2 * slice_heads, packed, 0.0)
    misc = jnp.sum(packed, axis=0, keepdims=True) + offsets
    row = iota((TAIL, width), 0)
    tail = jnp.where(row == 0, misc, jnp.where(row < B_LAST_AT, gates_and_x, b_tail))
    out[rows:, :] = tail.astype(BF16)


def states_kernel(
    x, own, other, own_taps, other_taps, own_bias, other_bias, lags, gated, aux, passing, offset,
    s1, s2, s3, b_out, b_taps, b_tail, turn, ends,
):
    first = holds_b()
    block, state_size = own.shape
    count = own_taps.shape[0]
    channels = x.shape[1]
    ends[:, 0:channels] = x[block - HALO : block, :]
    ends[:, channels : channels + state_size] = own[block - HALO : block, :]
    ends[:, channels + state_size :] = other[block - HALO : block, :]
    taps = jnp.where(first, own_taps[...], other_taps[...])
    bias = jnp.where(first, own_bias[...], other_bias[...])
    source = jnp.where(first, own[...].astype(F32), other[...].astype(F32))
    before = convolve(source.astype(BF16), taps, bias, [lags[lag] for lag in range(count - 1)])
    value = silu(before)
    b_out[...] = value.astype(BF16)
    turn[...] = value.T.astype(BF16)
    b_taps[...] = jnp.concatenate([taps, bias, jnp.zeros((8 - count - 1, state_size), F32), before[0:8]], axis=0)
    b_tail[...] = jnp.concatenate(
        [jnp.zeros((B_LAST_AT, state_size), F32), source[block - 3 :], source[0:3]], axis=0
    )
    width = gated.shape[1] // (GROUP - 1)
    for slot, (k, out) in enumerate(((1, s1), (2, s2), (3, s3))):
        cols = slice(slot * width, (slot + 1) * width)
        message(out, k, dot(turn[...], gated[:, cols]), passing, offset, count, aux[8:24, cols], b_tail[...])


def rest_kernel(
    x, taps, bias, lags, late_parts, early_parts, passing, offset, turn, b_tail, s0, x_out, aux, gated,
):
    channel_slice(0, 0, x, taps, bias, lags, late_parts, early_parts, x_out, gated, aux)
    state = dot(turn[...], gated[...])
    message(s0, 0, state, passing, offset, taps.shape[0], aux[8:24, :], b_tail[...])


def tail_of(state):
    rows = state.shape[0]
    return state[rows - TAIL : rows, :].astype(F32)


def decay_of(tail):
    width = tail.shape[1]
    slice_heads = width // HEADDIM
    channel = iota((1, width), 1)
    value = jnp.zeros((1, width), F32)
    for head in range(slice_heads):
        both = tail[0:1, head : head + 1] + tail[0:1, slice_heads + head : slice_heads + head + 1]
        value = jnp.where(channel // HEADDIM == head, both, value)
    return value


def pack_decay(decay, tail):
    width = decay.shape[1]
    slice_heads = width // HEADDIM
    lane = iota((1, width), 1)
    high, low = two_parts(decay)
    row = jnp.where(lane >= 2 * slice_heads, tail[0:1], 0.0)
    for head in range(slice_heads):
        at = head * HEADDIM
        row = jnp.where(lane == head, high[:, at : at + 1], row)
        row = jnp.where(lane == slice_heads + head, low[:, at : at + 1], row)
    return row


def tail_taps(x_taps, x_bias, b_taps, count):
    width = x_taps.shape[1]
    upper = iota((TAIL, width), 0) < B_LAST_AT
    taps = [jnp.where(upper, x_taps[k : k + 1], b_taps[k : k + 1]) for k in range(count)]
    return taps, jnp.where(upper, x_bias, b_taps[count : count + 1])


def early_tokens(tail, earlier, taps, bias):
    width = tail.shape[1]
    slice_heads = width // HEADDIM
    count = len(taps)
    row = iota(tail.shape, 0)
    is_last = jnp.logical_or(
        jnp.logical_and(row >= X_LAST_AT, row < X_FIRST_AT),
        jnp.logical_and(row >= B_LAST_AT, row < B_FIRST_AT),
    )
    rows = jnp.where(is_last, earlier, tail)
    offset = jnp.full(tail.shape, -1.0, F32)
    for token in range(count - 1):
        lane = 2 * slice_heads + token
        here = jnp.logical_or(row == X_FIRST_AT + token, row == B_FIRST_AT + token)
        offset = jnp.where(here, tail[0:1, lane : lane + 1], offset)
    total = taps[count - 1] * rows + bias
    for lag in range(1, count):
        total = total + taps[count - 1 - lag] * jnp.where(offset >= lag, pltpu.roll(rows, lag, 0), 0.0)
    value = silu(total).astype(BF16).astype(F32)
    gate = pltpu.roll(tail, B_FIRST_AT - GATE_AT, 0)
    wanted = row >= B_FIRST_AT
    b = jnp.where(wanted, value, 0.0)
    x = jnp.where(wanted, pltpu.roll(value, B_FIRST_AT - X_FIRST_AT, 0) * gate, 0.0)
    return b, x


def group_kernel(r3, r1, r2, r0, earlier, x_taps, x_bias, b_taps, total, *, complete):
    rows = r0.shape[0] - TAIL
    width = r0.shape[1]
    count = x_taps.shape[0]
    held = (r0, r1, r2, r3)

    def run(member):
        cols = slice(member * width, (member + 1) * width)
        taps, bias = tail_taps(x_taps[:, cols], x_bias[:, cols], b_taps[...], count)
        states = [held[member ^ k] for k in range(GROUP)]
        tails = [tail_of(state) for state in states]
        decays = [decay_of(tail) for tail in tails]
        factors = [None] * GROUP
        factor = jnp.ones((1, width), F32)
        for k in reversed(range(GROUP)):
            factors[k] = factor
            factor = factor * decays[k]
        early_b, early_x = [], []
        for k in range(0 if complete else 1, GROUP):
            before = tails[k - 1] if k else tail_of(earlier)
            b, x = early_tokens(tails[k], before, taps, bias)
            early_b.append(b)
            early_x.append(x * factors[k])
        b_turned = jnp.concatenate(early_b, axis=0).T.astype(BF16)
        added = dot(b_turned, jnp.concatenate(early_x, axis=0).astype(BF16))
        step = 64
        for top in range(0, rows, step):
            part = slice(top, top + step)
            value = added[part]
            for k in range(GROUP):
                value = value + factors[k] * states[k][part, :].astype(F32)
            total[part, :] = value.astype(BF16)
        row = iota((TAIL, width), 0)
        is_last = jnp.logical_or(
            jnp.logical_and(row >= X_LAST_AT, row < X_FIRST_AT),
            jnp.logical_and(row >= B_LAST_AT, row < B_FIRST_AT),
        )
        gates = jnp.zeros((1, width), F32) if complete else factors[0]
        tail = jnp.where(is_last, tails[GROUP - 1], tails[0])
        tail = jnp.where(row < X_LAST_AT, tail * gates, tail)
        tail = jnp.where(row == 0, pack_decay(factor, tails[0]), tail)
        total[rows:, :] = tail.astype(BF16)

    for member in range(GROUP):
        pl.when(member_here() == member)(lambda member=member: run(member))


def entering_kernel(
    r3, r1, r2, r0, far, near, x_taps, x_bias, b_taps, e0, e1, e2, e3
):
    group = group_here()
    one = jnp.ones((1, r0.shape[1]), F32)
    from_near = jnp.where(group >= 1, one, 0.0)
    from_far = jnp.where(group >= 2, one, 0.0)
    rows = r0.shape[0] - TAIL
    width = r0.shape[1]
    count = x_taps.shape[0]
    held, outs = (r0, r1, r2, r3), (e0, e1, e2, e3)

    def run(member):
        cols = slice(member * width, (member + 1) * width)
        taps, bias = tail_taps(x_taps[:, cols], x_bias[:, cols], b_taps[...], count)
        states = [held[member ^ k] for k in range(GROUP)]
        targets = [outs[member ^ k] for k in range(GROUP)]
        tails = [tail_of(state) for state in states]
        near_tail = from_near * tail_of(near)
        far_tail = from_far * tail_of(far)
        decays = [decay_of(tail) for tail in tails]
        near_decay = decay_of(near_tail)
        far_factor = near_decay * from_far
        far_b, far_x = early_tokens(far_tail, jnp.zeros_like(far_tail), taps, bias)
        near_b, near_x = early_tokens(near_tail, far_tail, taps, bias)
        early_b, early_x = [far_b, near_b], [far_x * near_decay, near_x]
        for k in range(GROUP - 1):
            b, x = early_tokens(tails[k], tails[k - 1] if k else near_tail, taps, bias)
            early_b.append(b)
            early_x.append(x)
        b_turned = jnp.concatenate(early_b, axis=0).T.astype(BF16)
        x_rows = jnp.concatenate(early_x, axis=0).astype(BF16)
        added = [dot(b_turned[:, : 2 * TAIL], x_rows[: 2 * TAIL])]
        for k in range(GROUP - 1):
            part = slice((k + 2) * TAIL, (k + 3) * TAIL)
            added.append(dot(b_turned[:, part], x_rows[part]))
        step = 32
        for top in range(0, rows, step):
            part = slice(top, top + step)
            value = from_near * near[part, :].astype(F32) + far_factor * far[part, :].astype(F32) + added[0][part]
            targets[0][part, :] = value.astype(BF16)
            for k in range(GROUP - 1):
                value = decays[k] * value + states[k][part, :].astype(F32) + added[k + 1][part]
                targets[k + 1][part, :] = value.astype(BF16)

    for member in range(GROUP):
        pl.when(member_here() == member)(lambda member=member: run(member))


def patched(before, halo, taps, offset_col):
    width = before.shape[1]
    count = taps.shape[0]
    extended = jnp.concatenate([halo[HALO - 8 :].astype(F32), jnp.zeros((8, width), F32)], axis=0)
    total = before
    for lag in range(1, count):
        shifted_rows = extended[8 - lag : 16 - lag]
        total = total + taps[count - 1 - lag : count - lag] * jnp.where(
            offset_col[0:8, 0:1] >= lag, shifted_rows, 0.0
        )
    return silu(total)


def intra_kernel(
    x_early, x_late, aux_early, aux_late, halo, own, other, own_taps, other_taps, own_bias, other_bias, b, b_aux,
    x_taps, step, sums, offset, lags, y, c_out, carry, bias, scores, columns, x_full, b_full, aux,
):
    first = holds_b()
    block, channels = x_full.shape
    heads = step.shape[0]
    state_size = b.shape[1]
    width = channels // GROUP
    for k, (part, rows, slot) in enumerate(
        ((x_late, aux_late, 0), (x_early, aux_early, 0), (x_early, aux_early, 1), (x_early, aux_early, 2))
    ):
        source = slice(slot * width, (slot + 1) * width)
        x_full[:, quarter(k, width)] = part[:, source]
        aux[:, quarter(k, width)] = rows[0:16, source]
    count = x_taps.shape[0]
    half = block // 2
    time_step, rate_sum = step[...], sums[...]
    columns[...] = rate_sum.T
    offset_col = offset_columns(offset[...])

    early = patched(aux[0:8, :], halo[:, 0:channels], x_taps[...], offset_col)
    x_full[0:16, :] = jnp.concatenate([early, x_full[0:16, :].astype(F32)[8:16]], axis=0).astype(BF16)
    own_halo = halo[:, channels : channels + state_size].astype(F32)
    other_halo = halo[:, channels + state_size :].astype(F32)
    b_full[...] = b[...]
    early = patched(b_aux[8:16, :], jnp.where(first, own_halo, other_halo), b_aux[0:count, :], offset_col)
    b_full[0:16, :] = jnp.concatenate([early, b[0:16, :].astype(F32)[8:16]], axis=0).astype(BF16)
    c_taps = jnp.where(first, other_taps[...], own_taps[...])
    c_bias = jnp.where(first, other_bias[...], own_bias[...])
    c_source = jnp.where(first, other[...].astype(F32), own[...].astype(F32)).astype(BF16)
    before = convolve(c_source, c_taps, c_bias, [lags[lag] for lag in range(count - 1)])
    c_value = silu(before)
    early = patched(before[0:8], jnp.where(first, other_halo, own_halo), c_taps, offset_col)
    c_out[...] = c_value.astype(BF16)
    c_out[0:16, :] = jnp.concatenate([early, c_value[8:16]], axis=0).astype(BF16)

    row = iota((block, LANES), 0)
    for left in range(0, block, LANES):
        gap = row - (iota((block, LANES), 1) + left)
        linked = jnp.logical_and(gap >= 0, offset_col >= gap.astype(F32))
        bias[:, left : left + LANES] = jnp.where(linked, 0.0, NEG)
    scores[...] = dot(c_out[...], b_full[...], ((1,), (1,)))
    reach = rate_sum - jnp.log(time_step)
    starts = iota(rate_sum.shape, 1) + 1
    factor = turned(jnp.where(offset[...] >= starts, jnp.exp(rate_sum), 0.0))
    for k in range(GROUP):
        carry[:, k * width : (k + 1) * width] = spread(factor, k * width, width)
    lane = iota((1, LANES), 1)
    per_tile = LANES // HEADDIM
    for tile in range(heads // per_tile):
        cols = slice(tile * LANES, (tile + 1) * LANES)
        skip_row = aux[8:9, cols]
        for top in range(0, block, half):
            part = slice(top, top + half)
            seen = top + half
            value = skip_row * x_full[part, cols].astype(F32)
            for k in range(per_tile):
                h = tile * per_tile + k
                gap = columns[part, h : h + 1] - reach[h : h + 1, 0:seen] + bias[part, 0:seen]
                weights = (scores[part, 0:seen] * jnp.exp(gap)).astype(BF16)
                chosen = jnp.where(lane // HEADDIM == k, x_full[0:seen, cols], jnp.zeros((), BF16))
                value = value + dot(weights, chosen)
            y[part, cols] = value


def back_kernel(c, f3, f1, f2, f0, intra, carry, out, held, sems):
    member = member_here()
    width = out.shape[1] // GROUP
    copies = []
    for k, state in enumerate((f0, f1, f2, f3)):
        cols = pl.ds(pl.multiple_of((member ^ k) * width, width), width)
        value = intra[:, cols] + carry[:, cols] * dot(c[...], state[...])
        held[k] = value.astype(BF16)
        copies.append(pltpu.make_async_copy(held.at[k], out.at[:, cols], sems.at[k]))
        copies[-1].start()
    for copy in copies:
        copy.wait()


def exchange(array, mask):
    return lax.ppermute(array, "seq", [(i, i ^ mask) for i in range(lax.axis_size("seq"))])


def turned_on(array, distance):
    count = lax.axis_size("seq")
    return lax.ppermute(array, "seq", [(i, (i + distance) % count) for i in range(count)])


def shifted(array, distance):
    count = lax.axis_size("seq")
    return lax.ppermute(array, "seq", [(i, i + distance) for i in range(count - distance)])


def scan_groups(total, groups):
    rows = total.shape[0] - TAIL
    last = shifted(total[rows:], GROUP)
    held, decay = total[:rows].astype(F32), decay_of(total[rows:].astype(F32))
    held = shifted(held, GROUP)
    decay = shifted(decay, GROUP)
    distance = 1
    while distance < groups:
        held = held + decay * shifted(held, GROUP * distance)
        decay = decay * shifted(decay, GROUP * distance)
        distance *= 2
    near_tail = jnp.concatenate([jnp.zeros((X_LAST_AT, last.shape[1]), BF16), last[X_LAST_AT:]], axis=0)
    near = jnp.concatenate([held.astype(BF16), near_tail], axis=0)
    return near, jnp.zeros_like(near)


def on_device(
    ssm_input, bc_input, conv_taps, conv_bias, bc_taps, bc_bias,
    step_input, step_bias, decay_log, skip_gain, request_offset,
):
    block, channels = ssm_input.shape
    state_size = bc_input.shape[1]
    heads = step_input.shape[0]
    width = channels // GROUP
    groups = lax.axis_size("seq") // GROUP
    here = lax.axis_index("seq")
    hbm = pl.BlockSpec(memory_space=pltpu.HBM)
    vmem = pl.BlockSpec(memory_space=pltpu.VMEM)

    swap = [(i, i ^ 1) for i in range(lax.axis_size("head"))]
    other_bc, other_taps, other_bias = [lax.ppermute(part, "head", swap) for part in (bc_input, bc_taps, bc_bias)]
    other_bias = other_bias[None, :]

    others = jax.ShapeDtypeStruct((block, (GROUP - 1) * width), BF16)
    slice_shape = jax.ShapeDtypeStruct((state_size + TAIL, width), BF16)
    (
        x_early, gated, aux_early, passing, time_step, rate_sum, x, x_taps, x_bias, own, own_taps, own_bias, offset,
        lags, late_parts, early_parts,
    ) = pl.pallas_call(
        channels_kernel,
        out_shape=[
            others,
            others,
            jax.ShapeDtypeStruct((24, (GROUP - 1) * width), F32),
            jax.ShapeDtypeStruct((heads, LANES), F32),
            jax.ShapeDtypeStruct((heads, block), F32),
            jax.ShapeDtypeStruct((heads, block), F32),
            jax.ShapeDtypeStruct((block, channels), BF16),
            jax.ShapeDtypeStruct(conv_taps.shape, F32),
            jax.ShapeDtypeStruct((1, channels), F32),
            jax.ShapeDtypeStruct(bc_input.shape, BF16),
            jax.ShapeDtypeStruct(bc_taps.shape, F32),
            jax.ShapeDtypeStruct((1, state_size), F32),
            jax.ShapeDtypeStruct((1, block), jnp.int32),
            jax.ShapeDtypeStruct((conv_taps.shape[0] - 1, block, block), BF16),
            jax.ShapeDtypeStruct((block, 2 * heads), BF16),
            jax.ShapeDtypeStruct((TAIL, 2 * heads), BF16),
        ],
        in_specs=[hbm] * 11,
        out_specs=[vmem] * 16,
        scratch_shapes=[
            pltpu.VMEM((heads, block), F32),
            pltpu.VMEM((1, heads), F32),
            pltpu.VMEM((1, heads), F32),
            pltpu.VMEM((1, heads), F32),
            pltpu.SemaphoreType.DMA((11,)),
        ],
        compiler_params=PARAMS,
        name="channels",
    )(
        *[
            pltpu.with_memory_space_constraint(array, pltpu.HBM)
            for array in (
                ssm_input, conv_taps, conv_bias[None, :], bc_input, bc_taps, bc_bias[None, :], step_input,
                request_offset[None, :], step_bias[None, :], decay_log[None, :], skip_gain[None, :],
            )
        ]
    )
    s1, s2, s3, b_main, b_aux, b_tail, turn, ends = pl.pallas_call(
        states_kernel,
        out_shape=[
            slice_shape,
            slice_shape,
            slice_shape,
            jax.ShapeDtypeStruct((block, state_size), BF16),
            jax.ShapeDtypeStruct((16, state_size), F32),
            jax.ShapeDtypeStruct((TAIL, state_size), F32),
            jax.ShapeDtypeStruct((state_size, block), BF16),
            jax.ShapeDtypeStruct((HALO, channels + 2 * state_size), BF16),
        ],
        in_specs=[vmem] * 12,
        out_specs=[vmem] * 8,
        compiler_params=PARAMS,
        name="states",
    )(x, own, other_bc, own_taps, other_taps, own_bias, other_bias, lags, gated, aux_early, passing, offset)
    r1, r2, r3 = exchange(s1, 1), exchange(s2, 2), exchange(s3, 3)
    halo = shifted(ends, 1)
    s0, x_late, aux_late = pl.pallas_call(
        rest_kernel,
        out_shape=[
            slice_shape,
            jax.ShapeDtypeStruct((block, width), BF16),
            jax.ShapeDtypeStruct((24, width), F32),
        ],
        in_specs=[vmem] * 10,
        out_specs=[vmem] * 3,
        scratch_shapes=[pltpu.VMEM((block, width), BF16)],
        compiler_params=PARAMS,
        cost_estimate=pl.CostEstimate(flops=400_000_000, bytes_accessed=2_000_000, transcendentals=200_000),
        name="rest",
    )(x, x_taps, x_bias, lags, late_parts, early_parts, passing, offset, turn, b_tail)
    received = [s0, r1, r2, r3]

    direct = groups == GROUP
    if direct:
        earlier = jnp.zeros((TAIL, width), BF16)
    else:
        last = received[0]
        for k in (1, 2, 3):
            last = jnp.where((here % GROUP) ^ k == GROUP - 1, received[k], last)
        earlier = shifted(last[state_size:], GROUP)
    total = pl.pallas_call(
        lambda *refs: group_kernel(*refs, complete=not direct),
        out_shape=slice_shape,
        in_specs=[vmem] * (GROUP + 4),
        out_specs=vmem,
        compiler_params=PARAMS,
        name="group",
    )(r3, r1, r2, s0, earlier, x_taps, x_bias, b_aux)
    total, halo = lax.optimization_barrier((total, halo))
    if direct:
        far = shifted(total, 2 * GROUP)
        near = turned_on(total, GROUP)
    else:
        near, far = scan_groups(total, groups)

    entering = pl.pallas_call(
        entering_kernel,
        out_shape=[jax.ShapeDtypeStruct((state_size, width), BF16)] * GROUP,
        in_specs=[vmem] * (GROUP + 5),
        out_specs=[vmem] * GROUP,
        compiler_params=PARAMS,
        name="entering",
    )(r3, r1, r2, s0, far, near, x_taps, x_bias, b_aux)
    mine = [entering[0]] + [exchange(entering[k], k) for k in (1, 2, 3)]

    intra, c_conv, carry = pl.pallas_call(
        intra_kernel,
        out_shape=[
            jax.ShapeDtypeStruct((block, channels), F32),
            jax.ShapeDtypeStruct((block, state_size), BF16),
            jax.ShapeDtypeStruct((block, channels), F32),
        ],
        in_specs=[vmem] * 18,
        out_specs=[vmem] * 3,
        scratch_shapes=[
            pltpu.VMEM((block, block), F32),
            pltpu.VMEM((block, block), F32),
            pltpu.VMEM((block, heads), F32),
            pltpu.VMEM((block, channels), BF16),
            pltpu.VMEM((block, state_size), BF16),
            pltpu.VMEM((16, channels), F32),
        ],
        compiler_params=PARAMS,
        cost_estimate=pl.CostEstimate(flops=600_000_000, bytes_accessed=4_000_000, transcendentals=1_000_000),
        name="intra",
    )(
        x_early, x_late, aux_early, aux_late, halo, own, other_bc, own_taps, other_taps, own_bias, other_bias,
        b_main, b_aux, x_taps, time_step, rate_sum, offset, lags,
    )
    out_shape = jax.ShapeDtypeStruct((block, channels), BF16)
    return pl.pallas_call(
        back_kernel,
        out_shape=out_shape,
        in_specs=[vmem] * (GROUP + 3),
        out_specs=hbm,
        scratch_shapes=[pltpu.VMEM((GROUP, block, width), BF16), pltpu.SemaphoreType.DMA((GROUP,))],
        compiler_params=PARAMS,
        name="back",
    )(c_conv, mine[3], mine[1], mine[2], mine[0], intra, carry)


def solution(mesh):
    return jax.shard_map(
        on_device,
        mesh=mesh,
        in_specs=(
            P("seq", "head"),
            P("seq", "head"),
            P(None, "head"),
            P("head"),
            P(None, "head"),
            P("head"),
            P("head", "seq"),
            P("head"),
            P("head"),
            P("head"),
            P("seq"),
        ),
        out_specs=P("seq", "head"),
        check_vma=False,
    )
```

```python
import jax
import jax.numpy as jnp
from jax import lax
from jax.experimental import pallas as pl
from jax.experimental.pallas import tpu as pltpu
from jax.sharding import PartitionSpec as P

HEADDIM = 64
GROUP = 4
TAIL = 16
GATE_AT, X_LAST_AT, X_FIRST_AT, B_LAST_AT, B_FIRST_AT = 1, 4, 7, 10, 13
HALO = 16
LANES = 128
NEG = -1e30
F32 = jnp.float32
BF16 = jnp.bfloat16
PARAMS = pltpu.CompilerParams(vmem_limit_bytes=24 * 1024 * 1024)


def dot(a, b, dims=((1,), (0,))):
    return lax.dot_general(a, b, (dims, ((), ())), preferred_element_type=F32)


def two_parts(value):
    high = value.astype(BF16).astype(F32)
    return high, value - high


def silu(half):
    return half + half * jnp.tanh(half)


def iota(shape, dim):
    return lax.broadcasted_iota(jnp.int32, shape, dim)


def member_here():
    return lax.axis_index("seq") % GROUP


def group_here():
    return lax.axis_index("seq") // GROUP


def holds_b():
    return lax.axis_index("head") % 2 == 0


def column(row):
    shape = (row.shape[1], row.shape[1])
    wide = jnp.broadcast_to(row, shape)
    return jnp.sum(jnp.where(iota(shape, 0) == iota(shape, 1), wide, 0.0), axis=1, keepdims=True)


def spread(parts, first_channel, width):
    heads = parts.shape[1] // 2
    shape = (2 * heads, width)
    head = iota(shape, 0) & (heads - 1)
    channel = iota(shape, 1) + first_channel
    return dot(parts, (channel // HEADDIM == head).astype(F32).astype(BF16))


def turned(per_head):
    high, low = two_parts(per_head)
    return jnp.concatenate([high, low], axis=0).T.astype(BF16)


def rates(step, step_bias, decay_log):
    heads, block = step.shape
    time_step = jax.nn.softplus(step + step_bias)
    log_decay = -jnp.exp(decay_log) * time_step
    shape = (block, block)
    upto = (iota(shape, 0) <= iota(shape, 1)).astype(F32).astype(BF16)
    first, rest = two_parts(log_decay)
    second, third = two_parts(rest)
    sums = dot(jnp.concatenate([first, second, third], axis=0).astype(BF16), upto)
    return time_step, sums[0:heads] + (sums[heads : 2 * heads] + sums[2 * heads :])


def offset_columns(offset_row):
    wide = jnp.broadcast_to(offset_row.astype(F32), (LANES, offset_row.shape[1]))
    return wide.T


def lag_matrices(offset_col, count):
    block = offset_col.shape[0]
    gap = iota((block, block), 0) - iota((block, block), 1)
    offset_wide = jnp.concatenate([offset_col] * (block // LANES), axis=1)
    return [
        jnp.where(jnp.logical_and(gap == lag, offset_wide >= lag), 1.0, 0.0).astype(BF16)
        for lag in range(1, count)
    ]


def convolve(source, taps, bias, lags):
    count = len(lags) + 1
    total = taps[count - 1 : count] * source.astype(F32) + bias
    for lag, matrix in enumerate(lags, 1):
        total = total + taps[count - 1 - lag : count - lag] * dot(matrix, source)
    return total


def quarter(k, width):
    return pl.ds(pl.multiple_of((member_here() ^ k) * width, width), width)


def channel_slice(k, slot, x, taps, bias, lags, late_parts, early_parts, x_out, gated, aux):
    block = x.shape[0]
    width = x.shape[1] // GROUP
    cols, to = quarter(k, width), slice(slot * width, (slot + 1) * width)
    source = x[:, cols]
    before = convolve(source, taps[:, cols], bias[:, cols], [lags[lag] for lag in range(lags.shape[0])])
    value = silu(before).astype(BF16)
    x_out[:, to] = value
    first_channel = (member_here() ^ k) * width
    gated[:, to] = (value.astype(F32) * spread(late_parts[...], first_channel, width)).astype(BF16)
    aux[0:8, to] = before[0:8]
    early = spread(early_parts[...], first_channel, width)
    first = source[0:TAIL].astype(F32)
    last_rows = source[block - TAIL : block].astype(F32)
    aux[8:24, to] = jnp.concatenate(
        [early[3:4], early[0:3], last_rows[TAIL - 3 :], first[0:3], jnp.zeros((TAIL - 10, width), F32)], axis=0
    )


def channels_kernel(
    x_hbm, taps_hbm, bias_hbm, own_hbm, own_taps_hbm, own_bias_hbm, step_hbm, offset_hbm,
    step_bias_hbm, decay_hbm, skip_hbm,
    x_out, gated, aux, passing_out, step_out, sums_out, x, taps, bias, own, own_taps, own_bias, offset,
    lags, late_parts, early_parts, step, step_bias, decay_log, skip, sems,
):
    block = x.shape[0]
    count = taps.shape[0]
    pairs = [
        (offset_hbm, offset), (step_hbm, step), (step_bias_hbm, step_bias), (decay_hbm, decay_log),
        (x_hbm, x), (taps_hbm, taps), (bias_hbm, bias), (skip_hbm, skip), (own_taps_hbm, own_taps),
        (own_bias_hbm, own_bias), (own_hbm, own),
    ]
    copies = [pltpu.make_async_copy(*pair, sems.at[k]) for k, pair in enumerate(pairs)]
    for copy in copies:
        copy.start()
    copies[0].wait()
    for lag, matrix in enumerate(lag_matrices(offset_columns(offset[...]), count)):
        lags[lag] = matrix
    for copy in copies[1:4]:
        copy.wait()
    time_step, rate_sum = rates(step[...], column(step_bias[...]), column(decay_log[...]))
    step_out[...] = time_step
    sums_out[...] = rate_sum
    last_offset = offset[0, block - 1]
    place = iota(rate_sum.shape, 1)
    last = rate_sum[:, block - 1 : block]
    gate = jnp.exp(jnp.where(last_offset >= block - 1 - place, last - rate_sum, NEG)) * time_step
    passing = jnp.exp(last) * (last_offset >= block).astype(F32)
    passing_out[...] = jnp.broadcast_to(passing, passing_out.shape)
    for copy in copies[4:8]:
        copy.wait()
    taps[...] = 0.5 * taps[...]
    bias[...] = 0.5 * bias[...]
    early_parts[...] = turned(jnp.where(place == count - 1, column(skip[...]), gate))[0:TAIL]
    late_parts[...] = turned(jnp.where(place >= count - 1, gate, 0.0))
    for slot, k in enumerate((1, 2, 3)):
        channel_slice(k, slot, x, taps, bias, lags, late_parts, early_parts, x_out, gated, aux)
    for copy in copies[8:]:
        copy.wait()
    own_taps[...] = 0.5 * own_taps[...]
    own_bias[...] = 0.5 * own_bias[...]


def message(out, k, state, passing, offset, count, gates_and_x, b_tail):
    rows, width = state.shape
    heads = passing.shape[0]
    slice_heads = heads // GROUP
    out[0:rows, :] = state.astype(BF16)
    lane = iota((heads, width), 1)
    head = iota((heads, width), 0)
    high, low = two_parts(passing[:, 0:1])
    offsets = pltpu.roll(jnp.minimum(offset[...], count - 1).astype(F32), 2 * slice_heads, 1)
    offsets = jnp.where(
        jnp.logical_and(lane[0:1] >= 2 * slice_heads, lane[0:1] < 2 * slice_heads + count - 1), offsets, 0.0
    )
    at = lane + (member_here() ^ k) * slice_heads
    packed = jnp.where(lane < slice_heads, jnp.where(at == head, high, 0.0), 0.0)
    packed = jnp.where(jnp.logical_and(lane >= slice_heads, at == head + slice_heads), low, packed)
    packed = jnp.where(lane < 2 * slice_heads, packed, 0.0)
    misc = jnp.sum(packed, axis=0, keepdims=True) + offsets
    row = iota((TAIL, width), 0)
    tail = jnp.where(row == 0, misc, jnp.where(row < B_LAST_AT, gates_and_x, b_tail))
    out[rows:, :] = tail.astype(BF16)


def states_kernel(
    x, own, other, own_taps, other_taps, own_bias, other_bias, lags, gated, aux, passing, offset,
    s1, s2, s3, b_out, b_taps, b_tail, turn, ends,
):
    first = holds_b()
    block, state_size = own.shape
    count = own_taps.shape[0]
    channels = x.shape[1]
    ends[:, 0:channels] = x[block - HALO : block, :]
    ends[:, channels : channels + state_size] = own[block - HALO : block, :]
    ends[:, channels + state_size :] = other[block - HALO : block, :]
    taps = jnp.where(first, own_taps[...], 0.5 * other_taps[...])
    bias = jnp.where(first, own_bias[...], 0.5 * other_bias[...])
    source = jnp.where(first, own[...].astype(F32), other[...].astype(F32))
    before = convolve(source.astype(BF16), taps, bias, [lags[lag] for lag in range(count - 1)])
    value = silu(before)
    b_out[...] = value.astype(BF16)
    turn[...] = value.T.astype(BF16)
    b_taps[...] = jnp.concatenate([taps, bias, jnp.zeros((8 - count - 1, state_size), F32), before[0:8]], axis=0)
    b_tail[...] = jnp.concatenate(
        [jnp.zeros((B_LAST_AT, state_size), F32), source[block - 3 :], source[0:3]], axis=0
    )
    width = gated.shape[1] // (GROUP - 1)
    for slot, (k, out) in enumerate(((1, s1), (2, s2), (3, s3))):
        cols = slice(slot * width, (slot + 1) * width)
        message(out, k, dot(turn[...], gated[:, cols]), passing, offset, count, aux[8:24, cols], b_tail[...])


def rest_kernel(
    x, taps, bias, lags, late_parts, early_parts, passing, offset, turn, b_tail, s0, x_out, aux, gated,
):
    channel_slice(0, 0, x, taps, bias, lags, late_parts, early_parts, x_out, gated, aux)
    state = dot(turn[...], gated[...])
    message(s0, 0, state, passing, offset, taps.shape[0], aux[8:24, :], b_tail[...])


def tail_of(state):
    rows = state.shape[0]
    return state[rows - TAIL : rows, :].astype(F32)


def decay_of(tail):
    width = tail.shape[1]
    slice_heads = width // HEADDIM
    channel = iota((1, width), 1)
    value = jnp.zeros((1, width), F32)
    for head in range(slice_heads):
        both = tail[0:1, head : head + 1] + tail[0:1, slice_heads + head : slice_heads + head + 1]
        value = jnp.where(channel // HEADDIM == head, both, value)
    return value


def pack_decay(decay, tail):
    width = decay.shape[1]
    slice_heads = width // HEADDIM
    lane = iota((1, width), 1)
    high, low = two_parts(decay)
    row = jnp.where(lane >= 2 * slice_heads, tail[0:1], 0.0)
    for head in range(slice_heads):
        at = head * HEADDIM
        row = jnp.where(lane == head, high[:, at : at + 1], row)
        row = jnp.where(lane == slice_heads + head, low[:, at : at + 1], row)
    return row


def tail_taps(x_taps, x_bias, b_taps, count):
    width = x_taps.shape[1]
    upper = iota((TAIL, width), 0) < B_LAST_AT
    taps = [jnp.where(upper, x_taps[k : k + 1], b_taps[k : k + 1]) for k in range(count)]
    return taps, jnp.where(upper, x_bias, b_taps[count : count + 1])


def early_tokens(tail, earlier, taps, bias):
    width = tail.shape[1]
    slice_heads = width // HEADDIM
    count = len(taps)
    row = iota(tail.shape, 0)
    is_last = jnp.logical_or(
        jnp.logical_and(row >= X_LAST_AT, row < X_FIRST_AT),
        jnp.logical_and(row >= B_LAST_AT, row < B_FIRST_AT),
    )
    rows = jnp.where(is_last, earlier, tail)
    offset = jnp.full(tail.shape, -1.0, F32)
    for token in range(count - 1):
        lane = 2 * slice_heads + token
        here = jnp.logical_or(row == X_FIRST_AT + token, row == B_FIRST_AT + token)
        offset = jnp.where(here, tail[0:1, lane : lane + 1], offset)
    total = taps[count - 1] * rows + bias
    for lag in range(1, count):
        total = total + taps[count - 1 - lag] * jnp.where(offset >= lag, pltpu.roll(rows, lag, 0), 0.0)
    value = silu(total).astype(BF16).astype(F32)
    gate = pltpu.roll(tail, B_FIRST_AT - GATE_AT, 0)
    wanted = row >= B_FIRST_AT
    b = jnp.where(wanted, value, 0.0)
    x = jnp.where(wanted, pltpu.roll(value, B_FIRST_AT - X_FIRST_AT, 0) * gate, 0.0)
    return b, x


def group_kernel(r3, r1, r2, r0, earlier, x_taps, x_bias, b_taps, total, *, complete):
    rows = r0.shape[0] - TAIL
    width = r0.shape[1]
    count = x_taps.shape[0]
    held = (r0, r1, r2, r3)

    def run(member):
        cols = slice(member * width, (member + 1) * width)
        taps, bias = tail_taps(x_taps[:, cols], x_bias[:, cols], b_taps[...], count)
        states = [held[member ^ k] for k in range(GROUP)]
        tails = [tail_of(state) for state in states]
        decays = [decay_of(tail) for tail in tails]
        factors = [None] * GROUP
        factor = jnp.ones((1, width), F32)
        for k in reversed(range(GROUP)):
            factors[k] = factor
            factor = factor * decays[k]
        early_b, early_x = [], []
        for k in range(0 if complete else 1, GROUP):
            before = tails[k - 1] if k else tail_of(earlier)
            b, x = early_tokens(tails[k], before, taps, bias)
            early_b.append(b)
            early_x.append(x * factors[k])
        b_rows = jnp.concatenate(early_b, axis=0).astype(BF16)
        added = dot(b_rows, jnp.concatenate(early_x, axis=0).astype(BF16), ((0,), (0,)))
        step = 64
        for top in range(0, rows, step):
            part = slice(top, top + step)
            value = added[part]
            for k in range(GROUP):
                value = value + factors[k] * states[k][part, :].astype(F32)
            total[part, :] = value.astype(BF16)
        row = iota((TAIL, width), 0)
        is_last = jnp.logical_or(
            jnp.logical_and(row >= X_LAST_AT, row < X_FIRST_AT),
            jnp.logical_and(row >= B_LAST_AT, row < B_FIRST_AT),
        )
        gates = jnp.zeros((1, width), F32) if complete else factors[0]
        tail = jnp.where(is_last, tails[GROUP - 1], tails[0])
        tail = jnp.where(row < X_LAST_AT, tail * gates, tail)
        tail = jnp.where(row == 0, pack_decay(factor, tails[0]), tail)
        total[rows:, :] = tail.astype(BF16)

    for member in range(GROUP):
        pl.when(member_here() == member)(lambda member=member: run(member))


def entering_kernel(
    r3, r1, r2, r0, far, near, x_taps, x_bias, b_taps, e0, e1, e2, e3
):
    group = group_here()
    one = jnp.ones((1, r0.shape[1]), F32)
    from_near = jnp.where(group >= 1, one, 0.0)
    from_far = jnp.where(group >= 2, one, 0.0)
    rows = r0.shape[0] - TAIL
    width = r0.shape[1]
    count = x_taps.shape[0]
    held, outs = (r0, r1, r2, r3), (e0, e1, e2, e3)

    def run(member):
        cols = slice(member * width, (member + 1) * width)
        taps, bias = tail_taps(x_taps[:, cols], x_bias[:, cols], b_taps[...], count)
        states = [held[member ^ k] for k in range(GROUP)]
        targets = [outs[member ^ k] for k in range(GROUP)]
        tails = [tail_of(state) for state in states]
        near_tail = from_near * tail_of(near)
        far_tail = from_far * tail_of(far)
        decays = [decay_of(tail) for tail in tails]
        near_decay = decay_of(near_tail)
        far_factor = near_decay * from_far
        far_b, far_x = early_tokens(far_tail, jnp.zeros_like(far_tail), taps, bias)
        near_b, near_x = early_tokens(near_tail, far_tail, taps, bias)
        early_b, early_x = [far_b, near_b], [far_x * near_decay, near_x]
        for k in range(GROUP - 1):
            b, x = early_tokens(tails[k], tails[k - 1] if k else near_tail, taps, bias)
            early_b.append(b)
            early_x.append(x)
        b_rows = jnp.concatenate(early_b, axis=0).astype(BF16)
        x_rows = jnp.concatenate(early_x, axis=0).astype(BF16)
        added = [dot(b_rows[: 2 * TAIL], x_rows[: 2 * TAIL], ((0,), (0,)))]
        for k in range(GROUP - 1):
            part = slice((k + 2) * TAIL, (k + 3) * TAIL)
            added.append(dot(b_rows[part], x_rows[part], ((0,), (0,))))
        step = 32
        for top in range(0, rows, step):
            part = slice(top, top + step)
            value = from_near * near[part, :].astype(F32) + far_factor * far[part, :].astype(F32) + added[0][part]
            targets[0][part, :] = value.astype(BF16)
            for k in range(GROUP - 1):
                value = decays[k] * value + states[k][part, :].astype(F32) + added[k + 1][part]
                targets[k + 1][part, :] = value.astype(BF16)

    for member in range(GROUP):
        pl.when(member_here() == member)(lambda member=member: run(member))


def patched(before, halo, taps, offset_col):
    width = before.shape[1]
    count = taps.shape[0]
    extended = jnp.concatenate([halo[HALO - 8 :].astype(F32), jnp.zeros((8, width), F32)], axis=0)
    total = before
    for lag in range(1, count):
        shifted_rows = extended[8 - lag : 16 - lag]
        total = total + taps[count - 1 - lag : count - lag] * jnp.where(
            offset_col[0:8, 0:1] >= lag, shifted_rows, 0.0
        )
    return silu(total)


def intra_kernel(
    x_early, x_late, aux_early, aux_late, halo, own, other, own_taps, other_taps, own_bias, other_bias, b, b_aux,
    x_taps, step, sums, offset, lags, y, c_out, carry, bias, scores, columns, x_full, b_full, aux,
):
    first = holds_b()
    block, channels = x_full.shape
    heads = step.shape[0]
    state_size = b.shape[1]
    width = channels // GROUP
    for k, (part, rows, slot) in enumerate(
        ((x_late, aux_late, 0), (x_early, aux_early, 0), (x_early, aux_early, 1), (x_early, aux_early, 2))
    ):
        source = slice(slot * width, (slot + 1) * width)
        x_full[:, quarter(k, width)] = part[:, source]
        aux[:, quarter(k, width)] = rows[0:16, source]
    count = x_taps.shape[0]
    half = block // 2
    time_step, rate_sum = step[...], sums[...]
    columns[...] = rate_sum.T
    offset_col = offset_columns(offset[...])

    early = patched(aux[0:8, :], halo[:, 0:channels], x_taps[...], offset_col)
    x_full[0:16, :] = jnp.concatenate([early, x_full[0:16, :].astype(F32)[8:16]], axis=0).astype(BF16)
    own_halo = halo[:, channels : channels + state_size].astype(F32)
    other_halo = halo[:, channels + state_size :].astype(F32)
    b_full[...] = b[...]
    early = patched(b_aux[8:16, :], jnp.where(first, own_halo, other_halo), b_aux[0:count, :], offset_col)
    b_full[0:16, :] = jnp.concatenate([early, b[0:16, :].astype(F32)[8:16]], axis=0).astype(BF16)
    c_taps = jnp.where(first, 0.5 * other_taps[...], own_taps[...])
    c_bias = jnp.where(first, 0.5 * other_bias[...], own_bias[...])
    c_source = jnp.where(first, other[...].astype(F32), own[...].astype(F32)).astype(BF16)
    before = convolve(c_source, c_taps, c_bias, [lags[lag] for lag in range(count - 1)])
    c_value = silu(before)
    early = patched(before[0:8], jnp.where(first, other_halo, own_halo), c_taps, offset_col)
    c_out[...] = c_value.astype(BF16)
    c_out[0:16, :] = jnp.concatenate([early, c_value[8:16]], axis=0).astype(BF16)

    row = iota((block, LANES), 0)
    for left in range(0, block, LANES):
        gap = row - (iota((block, LANES), 1) + left)
        linked = jnp.logical_and(gap >= 0, offset_col >= gap.astype(F32))
        bias[:, left : left + LANES] = jnp.where(linked, 0.0, NEG)
    scores[...] = dot(c_out[...], b_full[...], ((1,), (1,)))
    reach = rate_sum - jnp.log(time_step)
    starts = iota(rate_sum.shape, 1) + 1
    factor = turned(jnp.where(offset[...] >= starts, jnp.exp(rate_sum), 0.0))
    for k in range(GROUP):
        carry[:, k * width : (k + 1) * width] = spread(factor, k * width, width)
    lane = iota((1, LANES), 1)
    per_tile = LANES // HEADDIM
    for tile in range(heads // per_tile):
        cols = slice(tile * LANES, (tile + 1) * LANES)
        skip_row = aux[8:9, cols]
        for top in range(0, block, half):
            part = slice(top, top + half)
            seen = top + half
            value = skip_row * x_full[part, cols].astype(F32)
            for k in range(per_tile):
                h = tile * per_tile + k
                gap = columns[part, h : h + 1] - reach[h : h + 1, 0:seen] + bias[part, 0:seen]
                weights = (scores[part, 0:seen] * jnp.exp(gap)).astype(BF16)
                chosen = jnp.where(lane // HEADDIM == k, x_full[0:seen, cols], jnp.zeros((), BF16))
                value = value + dot(weights, chosen)
            y[part, cols] = value


def back_kernel(c, f3, f1, f2, f0, intra, carry, out, held, sems):
    member = member_here()
    width = out.shape[1] // GROUP
    copies = []
    for k, state in enumerate((f0, f1, f2, f3)):
        cols = pl.ds(pl.multiple_of((member ^ k) * width, width), width)
        value = intra[:, cols] + carry[:, cols] * dot(c[...], state[...])
        held[k] = value.astype(BF16)
        copies.append(pltpu.make_async_copy(held.at[k], out.at[:, cols], sems.at[k]))
        copies[-1].start()
    for copy in copies:
        copy.wait()


def exchange(array, mask):
    return lax.ppermute(array, "seq", [(i, i ^ mask) for i in range(lax.axis_size("seq"))])


def turned_on(array, distance):
    count = lax.axis_size("seq")
    return lax.ppermute(array, "seq", [(i, (i + distance) % count) for i in range(count)])


def shifted(array, distance):
    count = lax.axis_size("seq")
    return lax.ppermute(array, "seq", [(i, i + distance) for i in range(count - distance)])


def scan_groups(total, groups):
    rows = total.shape[0] - TAIL
    last = shifted(total[rows:], GROUP)
    held, decay = total[:rows].astype(F32), decay_of(total[rows:].astype(F32))
    held = shifted(held, GROUP)
    decay = shifted(decay, GROUP)
    distance = 1
    while distance < groups:
        held = held + decay * shifted(held, GROUP * distance)
        decay = decay * shifted(decay, GROUP * distance)
        distance *= 2
    near_tail = jnp.concatenate([jnp.zeros((X_LAST_AT, last.shape[1]), BF16), last[X_LAST_AT:]], axis=0)
    near = jnp.concatenate([held.astype(BF16), near_tail], axis=0)
    return near, jnp.zeros_like(near)


def on_device(
    ssm_input, bc_input, conv_taps, conv_bias, bc_taps, bc_bias,
    step_input, step_bias, decay_log, skip_gain, request_offset,
):
    block, channels = ssm_input.shape
    state_size = bc_input.shape[1]
    heads = step_input.shape[0]
    width = channels // GROUP
    groups = lax.axis_size("seq") // GROUP
    here = lax.axis_index("seq")
    hbm = pl.BlockSpec(memory_space=pltpu.HBM)
    vmem = pl.BlockSpec(memory_space=pltpu.VMEM)

    swap = [(i, i ^ 1) for i in range(lax.axis_size("head"))]
    other_bc, other_taps, other_bias = [lax.ppermute(part, "head", swap) for part in (bc_input, bc_taps, bc_bias)]
    other_bias = other_bias[None, :]

    others = jax.ShapeDtypeStruct((block, (GROUP - 1) * width), BF16)
    slice_shape = jax.ShapeDtypeStruct((state_size + TAIL, width), BF16)
    (
        x_early, gated, aux_early, passing, time_step, rate_sum, x, x_taps, x_bias, own, own_taps, own_bias, offset,
        lags, late_parts, early_parts,
    ) = pl.pallas_call(
        channels_kernel,
        out_shape=[
            others,
            others,
            jax.ShapeDtypeStruct((24, (GROUP - 1) * width), F32),
            jax.ShapeDtypeStruct((heads, LANES), F32),
            jax.ShapeDtypeStruct((heads, block), F32),
            jax.ShapeDtypeStruct((heads, block), F32),
            jax.ShapeDtypeStruct((block, channels), BF16),
            jax.ShapeDtypeStruct(conv_taps.shape, F32),
            jax.ShapeDtypeStruct((1, channels), F32),
            jax.ShapeDtypeStruct(bc_input.shape, BF16),
            jax.ShapeDtypeStruct(bc_taps.shape, F32),
            jax.ShapeDtypeStruct((1, state_size), F32),
            jax.ShapeDtypeStruct((1, block), jnp.int32),
            jax.ShapeDtypeStruct((conv_taps.shape[0] - 1, block, block), BF16),
            jax.ShapeDtypeStruct((block, 2 * heads), BF16),
            jax.ShapeDtypeStruct((TAIL, 2 * heads), BF16),
        ],
        in_specs=[hbm] * 11,
        out_specs=[vmem] * 16,
        scratch_shapes=[
            pltpu.VMEM((heads, block), F32),
            pltpu.VMEM((1, heads), F32),
            pltpu.VMEM((1, heads), F32),
            pltpu.VMEM((1, heads), F32),
            pltpu.SemaphoreType.DMA((11,)),
        ],
        compiler_params=PARAMS,
        name="channels",
    )(
        *[
            pltpu.with_memory_space_constraint(array, pltpu.HBM)
            for array in (
                ssm_input, conv_taps, conv_bias[None, :], bc_input, bc_taps, bc_bias[None, :], step_input,
                request_offset[None, :], step_bias[None, :], decay_log[None, :], skip_gain[None, :],
            )
        ]
    )
    s1, s2, s3, b_main, b_aux, b_tail, turn, ends = pl.pallas_call(
        states_kernel,
        out_shape=[
            slice_shape,
            slice_shape,
            slice_shape,
            jax.ShapeDtypeStruct((block, state_size), BF16),
            jax.ShapeDtypeStruct((16, state_size), F32),
            jax.ShapeDtypeStruct((TAIL, state_size), F32),
            jax.ShapeDtypeStruct((state_size, block), BF16),
            jax.ShapeDtypeStruct((HALO, channels + 2 * state_size), BF16),
        ],
        in_specs=[vmem] * 12,
        out_specs=[vmem] * 8,
        compiler_params=PARAMS,
        name="states",
    )(x, own, other_bc, own_taps, other_taps, own_bias, other_bias, lags, gated, aux_early, passing, offset)
    r1, r2, r3 = exchange(s1, 1), exchange(s2, 2), exchange(s3, 3)
    halo = shifted(ends, 1)
    s0, x_late, aux_late = pl.pallas_call(
        rest_kernel,
        out_shape=[
            slice_shape,
            jax.ShapeDtypeStruct((block, width), BF16),
            jax.ShapeDtypeStruct((24, width), F32),
        ],
        in_specs=[vmem] * 10,
        out_specs=[vmem] * 3,
        scratch_shapes=[pltpu.VMEM((block, width), BF16)],
        compiler_params=PARAMS,
        cost_estimate=pl.CostEstimate(flops=400_000_000, bytes_accessed=2_000_000, transcendentals=200_000),
        name="rest",
    )(x, x_taps, x_bias, lags, late_parts, early_parts, passing, offset, turn, b_tail)
    received = [s0, r1, r2, r3]

    direct = groups == GROUP
    if direct:
        earlier = jnp.zeros((TAIL, width), BF16)
    else:
        last = received[0]
        for k in (1, 2, 3):
            last = jnp.where((here % GROUP) ^ k == GROUP - 1, received[k], last)
        earlier = shifted(last[state_size:], GROUP)
    total = pl.pallas_call(
        lambda *refs: group_kernel(*refs, complete=not direct),
        out_shape=slice_shape,
        in_specs=[vmem] * (GROUP + 4),
        out_specs=vmem,
        compiler_params=PARAMS,
        name="group",
    )(r3, r1, r2, s0, earlier, x_taps, x_bias, b_aux)
    total, halo = lax.optimization_barrier((total, halo))
    if direct:
        far = shifted(total, 2 * GROUP)
        near = turned_on(total, GROUP)
    else:
        near, far = scan_groups(total, groups)

    entering = pl.pallas_call(
        entering_kernel,
        out_shape=[jax.ShapeDtypeStruct((state_size, width), BF16)] * GROUP,
        in_specs=[vmem] * (GROUP + 5),
        out_specs=[vmem] * GROUP,
        compiler_params=PARAMS,
        name="entering",
    )(r3, r1, r2, s0, far, near, x_taps, x_bias, b_aux)
    mine = [entering[0]] + [exchange(entering[k], k) for k in (1, 2, 3)]

    intra, c_conv, carry = pl.pallas_call(
        intra_kernel,
        out_shape=[
            jax.ShapeDtypeStruct((block, channels), F32),
            jax.ShapeDtypeStruct((block, state_size), BF16),
            jax.ShapeDtypeStruct((block, channels), F32),
        ],
        in_specs=[vmem] * 18,
        out_specs=[vmem] * 3,
        scratch_shapes=[
            pltpu.VMEM((block, block), F32),
            pltpu.VMEM((block, block), F32),
            pltpu.VMEM((block, heads), F32),
            pltpu.VMEM((block, channels), BF16),
            pltpu.VMEM((block, state_size), BF16),
            pltpu.VMEM((16, channels), F32),
        ],
        compiler_params=PARAMS,
        cost_estimate=pl.CostEstimate(flops=600_000_000, bytes_accessed=4_000_000, transcendentals=1_000_000),
        name="intra",
    )(
        x_early, x_late, aux_early, aux_late, halo, own, other_bc, own_taps, other_taps, own_bias, other_bias,
        b_main, b_aux, x_taps, time_step, rate_sum, offset, lags,
    )
    out_shape = jax.ShapeDtypeStruct((block, channels), BF16)
    return pl.pallas_call(
        back_kernel,
        out_shape=out_shape,
        in_specs=[vmem] * (GROUP + 3),
        out_specs=hbm,
        scratch_shapes=[pltpu.VMEM((GROUP, block, width), BF16), pltpu.SemaphoreType.DMA((GROUP,))],
        compiler_params=PARAMS,
        name="back",
    )(c_conv, mine[3], mine[1], mine[2], mine[0], intra, carry)


def solution(mesh):
    return jax.shard_map(
        on_device,
        mesh=mesh,
        in_specs=(
            P("seq", "head"),
            P("seq", "head"),
            P(None, "head"),
            P("head"),
            P(None, "head"),
            P("head"),
            P("head", "seq"),
            P("head"),
            P("head"),
            P("head"),
            P("seq"),
        ),
        out_specs=P("seq", "head"),
        check_vma=False,
    )
```

```python
import jax
import jax.numpy as jnp
from jax import lax
from jax.experimental import pallas as pl
from jax.experimental.pallas import tpu as pltpu
from jax.sharding import PartitionSpec as P

HEADDIM = 64
GROUP = 4
TAIL = 16
GATE_AT, X_LAST_AT, X_FIRST_AT, B_LAST_AT, B_FIRST_AT = 1, 4, 7, 10, 13
ENDS = 512
LANES = 128
NEG = -1e30
F32 = jnp.float32
BF16 = jnp.bfloat16
PARAMS = pltpu.CompilerParams(vmem_limit_bytes=24 * 1024 * 1024)


def dot(a, b, dims=((1,), (0,))):
    return lax.dot_general(a, b, (dims, ((), ())), preferred_element_type=F32)


def two_parts(value):
    high = value.astype(BF16).astype(F32)
    return high, value - high


def silu(half):
    return half + half * jnp.tanh(half)


def iota(shape, dim):
    return lax.broadcasted_iota(jnp.int32, shape, dim)


def member_here():
    return lax.axis_index("seq") % GROUP


def group_here():
    return lax.axis_index("seq") // GROUP


def holds_b():
    return lax.axis_index("head") % 2 == 0


def column(row):
    shape = (row.shape[1], row.shape[1])
    wide = jnp.broadcast_to(row, shape)
    return jnp.sum(jnp.where(iota(shape, 0) == iota(shape, 1), wide, 0.0), axis=1, keepdims=True)


def spread(parts, first_channel, width):
    heads = parts.shape[1] // 2
    shape = (2 * heads, width)
    head = iota(shape, 0) & (heads - 1)
    channel = iota(shape, 1) + first_channel
    return dot(parts, (channel // HEADDIM == head).astype(F32).astype(BF16))


def turned(per_head):
    high, low = two_parts(per_head)
    return jnp.concatenate([high, low], axis=0).T.astype(BF16)


def rates(step, step_bias, decay_log):
    heads, block = step.shape
    time_step = jax.nn.softplus(step + step_bias)
    log_decay = -jnp.exp(decay_log) * time_step
    shape = (block, block)
    upto = (iota(shape, 0) <= iota(shape, 1)).astype(F32).astype(BF16)
    first, rest = two_parts(log_decay)
    second, third = two_parts(rest)
    sums = dot(jnp.concatenate([first, second, third], axis=0).astype(BF16), upto)
    return time_step, sums[0:heads] + (sums[heads : 2 * heads] + sums[2 * heads :])


def offset_columns(offset_row):
    wide = jnp.broadcast_to(offset_row.astype(F32), (LANES, offset_row.shape[1]))
    return wide.T


def lag_matrices(offset_col, count):
    block = offset_col.shape[0]
    gap = iota((block, block), 0) - iota((block, block), 1)
    offset_wide = jnp.concatenate([offset_col] * (block // LANES), axis=1)
    return [
        jnp.where(jnp.logical_and(gap == lag, offset_wide >= lag), 1.0, 0.0).astype(BF16)
        for lag in range(1, count)
    ]


def convolve(source, taps, bias, lags):
    count = len(lags) + 1
    total = taps[count - 1 : count] * source.astype(F32) + bias
    for lag, matrix in enumerate(lags, 1):
        total = total + taps[count - 1 - lag : count - lag] * dot(matrix, source)
    return total


def quarter(k, width):
    return pl.ds(pl.multiple_of((member_here() ^ k) * width, width), width)


def channel_slice(k, slot, x, taps, bias, lags, late_parts, early_parts, x_out, gated, aux):
    block = x.shape[0]
    width = x.shape[1] // GROUP
    cols, to = quarter(k, width), slice(slot * width, (slot + 1) * width)
    source = x[:, cols]
    before = convolve(source, taps[:, cols], bias[:, cols], [lags[lag] for lag in range(lags.shape[0])])
    value = silu(before).astype(BF16)
    x_out[:, to] = value
    first_channel = (member_here() ^ k) * width
    gated[:, to] = (value.astype(F32) * spread(late_parts[...], first_channel, width)).astype(BF16)
    aux[0:8, to] = before[0:8]
    early = spread(early_parts[...], first_channel, width)
    first = source[0:TAIL].astype(F32)
    last_rows = source[block - TAIL : block].astype(F32)
    aux[8:24, to] = jnp.concatenate(
        [early[3:4], early[0:3], last_rows[TAIL - 3 :], first[0:3], jnp.zeros((TAIL - 10, width), F32)], axis=0
    )


def channels_kernel(
    x_hbm, taps_hbm, bias_hbm, own_hbm, own_taps_hbm, own_bias_hbm, step_hbm, offset_hbm,
    step_bias_hbm, decay_hbm, skip_hbm,
    x_out, gated, aux, passing_out, step_out, sums_out, x, taps, bias, own, own_taps, own_bias, offset,
    lags, late_parts, early_parts, step, step_bias, decay_log, skip, sems,
):
    block = x.shape[0]
    count = taps.shape[0]
    pairs = [
        (offset_hbm, offset), (step_hbm, step), (step_bias_hbm, step_bias), (decay_hbm, decay_log),
        (x_hbm, x), (taps_hbm, taps), (bias_hbm, bias), (skip_hbm, skip), (own_taps_hbm, own_taps),
        (own_bias_hbm, own_bias), (own_hbm, own),
    ]
    copies = [pltpu.make_async_copy(*pair, sems.at[k]) for k, pair in enumerate(pairs)]
    for copy in copies:
        copy.start()
    copies[0].wait()
    for lag, matrix in enumerate(lag_matrices(offset_columns(offset[...]), count)):
        lags[lag] = matrix
    for copy in copies[1:4]:
        copy.wait()
    time_step, rate_sum = rates(step[...], column(step_bias[...]), column(decay_log[...]))
    step_out[...] = time_step
    sums_out[...] = rate_sum
    last_offset = offset[0, block - 1]
    place = iota(rate_sum.shape, 1)
    last = rate_sum[:, block - 1 : block]
    gate = jnp.exp(jnp.where(last_offset >= block - 1 - place, last - rate_sum, NEG)) * time_step
    passing = jnp.exp(last) * (last_offset >= block).astype(F32)
    passing_out[...] = jnp.broadcast_to(passing, passing_out.shape)
    for copy in copies[4:8]:
        copy.wait()
    taps[...] = 0.5 * taps[...]
    bias[...] = 0.5 * bias[...]
    early_parts[...] = turned(jnp.where(place == count - 1, column(skip[...]), gate))[0:TAIL]
    late_parts[...] = turned(jnp.where(place >= count - 1, gate, 0.0))
    for slot, k in enumerate((1, 2, 3)):
        channel_slice(k, slot, x, taps, bias, lags, late_parts, early_parts, x_out, gated, aux)
    for copy in copies[8:]:
        copy.wait()
    own_taps[...] = 0.5 * own_taps[...]
    own_bias[...] = 0.5 * own_bias[...]


def message(out, k, state, passing, offset, count, gates_and_x, b_tail):
    rows, width = state.shape
    heads = passing.shape[0]
    slice_heads = heads // GROUP
    out[0:rows, :] = state.astype(BF16)
    lane = iota((heads, width), 1)
    head = iota((heads, width), 0)
    high, low = two_parts(passing[:, 0:1])
    offsets = pltpu.roll(jnp.minimum(offset[...], count - 1).astype(F32), 2 * slice_heads, 1)
    offsets = jnp.where(
        jnp.logical_and(lane[0:1] >= 2 * slice_heads, lane[0:1] < 2 * slice_heads + count - 1), offsets, 0.0
    )
    at = lane + (member_here() ^ k) * slice_heads
    packed = jnp.where(lane < slice_heads, jnp.where(at == head, high, 0.0), 0.0)
    packed = jnp.where(jnp.logical_and(lane >= slice_heads, at == head + slice_heads), low, packed)
    packed = jnp.where(lane < 2 * slice_heads, packed, 0.0)
    misc = jnp.sum(packed, axis=0, keepdims=True) + offsets
    row = iota((TAIL, width), 0)
    tail = jnp.where(row == 0, misc, jnp.where(row < B_LAST_AT, gates_and_x, b_tail))
    out[rows:, :] = tail.astype(BF16)


def states_kernel(
    x, own, other, own_taps, other_taps, own_bias, other_bias, lags, gated, aux, passing, offset,
    s1, s2, s3, b_out, b_taps, b_tail, turn, ends,
):
    first = holds_b()
    block, state_size = own.shape
    count = own_taps.shape[0]
    channels = x.shape[1]
    last_rows = jnp.concatenate(
        [part[block - TAIL : block, :].astype(F32)[TAIL - 3 :] for part in (x, own, other)], axis=1
    )
    packed = [last_rows[:, at : at + ENDS] for at in range(0, channels + 2 * state_size, ENDS)]
    blank = jnp.zeros((TAIL - 3 * len(packed), ENDS), F32)
    ends[...] = jnp.concatenate(packed + [blank], axis=0).astype(BF16)
    taps = jnp.where(first, own_taps[...], 0.5 * other_taps[...])
    bias = jnp.where(first, own_bias[...], 0.5 * other_bias[...])
    source = jnp.where(first, own[...].astype(F32), other[...].astype(F32))
    before = convolve(source.astype(BF16), taps, bias, [lags[lag] for lag in range(count - 1)])
    value = silu(before)
    b_out[...] = value.astype(BF16)
    turn[...] = value.T.astype(BF16)
    b_taps[...] = jnp.concatenate([taps, bias, jnp.zeros((8 - count - 1, state_size), F32), before[0:8]], axis=0)
    b_tail[...] = jnp.concatenate(
        [jnp.zeros((B_LAST_AT, state_size), F32), source[block - 3 :], source[0:3]], axis=0
    )
    width = gated.shape[1] // (GROUP - 1)
    for slot, (k, out) in enumerate(((1, s1), (2, s2), (3, s3))):
        cols = slice(slot * width, (slot + 1) * width)
        message(out, k, dot(turn[...], gated[:, cols]), passing, offset, count, aux[8:24, cols], b_tail[...])


def rest_kernel(
    x, taps, bias, lags, late_parts, early_parts, passing, offset, turn, b_tail, s0, x_out, aux, gated,
):
    channel_slice(0, 0, x, taps, bias, lags, late_parts, early_parts, x_out, gated, aux)
    state = dot(turn[...], gated[...])
    message(s0, 0, state, passing, offset, taps.shape[0], aux[8:24, :], b_tail[...])


def tail_of(state):
    rows = state.shape[0]
    return state[rows - TAIL : rows, :].astype(F32)


def decay_of(tail):
    width = tail.shape[1]
    slice_heads = width // HEADDIM
    channel = iota((1, width), 1)
    value = jnp.zeros((1, width), F32)
    for head in range(slice_heads):
        both = tail[0:1, head : head + 1] + tail[0:1, slice_heads + head : slice_heads + head + 1]
        value = jnp.where(channel // HEADDIM == head, both, value)
    return value


def pack_decay(decay, tail):
    width = decay.shape[1]
    slice_heads = width // HEADDIM
    lane = iota((1, width), 1)
    high, low = two_parts(decay)
    row = jnp.where(lane >= 2 * slice_heads, tail[0:1], 0.0)
    for head in range(slice_heads):
        at = head * HEADDIM
        row = jnp.where(lane == head, high[:, at : at + 1], row)
        row = jnp.where(lane == slice_heads + head, low[:, at : at + 1], row)
    return row


def tail_taps(x_taps, x_bias, b_taps, count):
    width = x_taps.shape[1]
    upper = iota((TAIL, width), 0) < B_LAST_AT
    taps = [jnp.where(upper, x_taps[k : k + 1], b_taps[k : k + 1]) for k in range(count)]
    return taps, jnp.where(upper, x_bias, b_taps[count : count + 1])


def early_tokens(tail, earlier, taps, bias):
    width = tail.shape[1]
    slice_heads = width // HEADDIM
    count = len(taps)
    row = iota(tail.shape, 0)
    is_last = jnp.logical_or(
        jnp.logical_and(row >= X_LAST_AT, row < X_FIRST_AT),
        jnp.logical_and(row >= B_LAST_AT, row < B_FIRST_AT),
    )
    rows = jnp.where(is_last, earlier, tail)
    offset = jnp.full(tail.shape, -1.0, F32)
    for token in range(count - 1):
        lane = 2 * slice_heads + token
        here = jnp.logical_or(row == X_FIRST_AT + token, row == B_FIRST_AT + token)
        offset = jnp.where(here, tail[0:1, lane : lane + 1], offset)
    total = taps[count - 1] * rows + bias
    for lag in range(1, count):
        total = total + taps[count - 1 - lag] * jnp.where(offset >= lag, pltpu.roll(rows, lag, 0), 0.0)
    value = silu(total).astype(BF16).astype(F32)
    gate = pltpu.roll(tail, B_FIRST_AT - GATE_AT, 0)
    wanted = row >= B_FIRST_AT
    b = jnp.where(wanted, value, 0.0)
    x = jnp.where(wanted, pltpu.roll(value, B_FIRST_AT - X_FIRST_AT, 0) * gate, 0.0)
    return b, x


def group_kernel(r3, r1, r2, r0, earlier, x_taps, x_bias, b_taps, total, *, complete):
    rows = r0.shape[0] - TAIL
    width = r0.shape[1]
    count = x_taps.shape[0]
    held = (r0, r1, r2, r3)

    def run(member):
        cols = slice(member * width, (member + 1) * width)
        taps, bias = tail_taps(x_taps[:, cols], x_bias[:, cols], b_taps[...], count)
        states = [held[member ^ k] for k in range(GROUP)]
        tails = [tail_of(state) for state in states]
        decays = [decay_of(tail) for tail in tails]
        factors = [None] * GROUP
        factor = jnp.ones((1, width), F32)
        for k in reversed(range(GROUP)):
            factors[k] = factor
            factor = factor * decays[k]
        early_b, early_x = [], []
        for k in range(0 if complete else 1, GROUP):
            before = tails[k - 1] if k else tail_of(earlier)
            b, x = early_tokens(tails[k], before, taps, bias)
            early_b.append(b)
            early_x.append(x * factors[k])
        b_rows = jnp.concatenate(early_b, axis=0).astype(BF16)
        added = dot(b_rows, jnp.concatenate(early_x, axis=0).astype(BF16), ((0,), (0,)))
        step = 32
        for top in range(0, rows, step):
            part = slice(top, top + step)
            value = added[part]
            for k in range(GROUP):
                value = value + factors[k] * states[k][part, :].astype(F32)
            total[part, :] = value.astype(BF16)
        row = iota((TAIL, width), 0)
        is_last = jnp.logical_or(
            jnp.logical_and(row >= X_LAST_AT, row < X_FIRST_AT),
            jnp.logical_and(row >= B_LAST_AT, row < B_FIRST_AT),
        )
        gates = jnp.zeros((1, width), F32) if complete else factors[0]
        tail = jnp.where(is_last, tails[GROUP - 1], tails[0])
        tail = jnp.where(row < X_LAST_AT, tail * gates, tail)
        tail = jnp.where(row == 0, pack_decay(factor, tails[0]), tail)
        total[rows:, :] = tail.astype(BF16)

    for member in range(GROUP):
        pl.when(member_here() == member)(lambda member=member: run(member))


def entering_kernel(
    r3, r1, r2, r0, far, near, x_taps, x_bias, b_taps, e0, e1, e2, e3
):
    group = group_here()
    one = jnp.ones((1, r0.shape[1]), F32)
    from_near = jnp.where(group >= 1, one, 0.0)
    from_far = jnp.where(group >= 2, one, 0.0)
    rows = r0.shape[0] - TAIL
    width = r0.shape[1]
    count = x_taps.shape[0]
    held, outs = (r0, r1, r2, r3), (e0, e1, e2, e3)

    def run(member):
        cols = slice(member * width, (member + 1) * width)
        taps, bias = tail_taps(x_taps[:, cols], x_bias[:, cols], b_taps[...], count)
        states = [held[member ^ k] for k in range(GROUP)]
        targets = [outs[member ^ k] for k in range(GROUP)]
        tails = [tail_of(state) for state in states]
        near_tail = from_near * tail_of(near)
        far_tail = from_far * tail_of(far)
        decays = [decay_of(tail) for tail in tails]
        near_decay = decay_of(near_tail)
        far_factor = near_decay * from_far
        far_b, far_x = early_tokens(far_tail, jnp.zeros_like(far_tail), taps, bias)
        near_b, near_x = early_tokens(near_tail, far_tail, taps, bias)
        early_b, early_x = [far_b, near_b], [far_x * near_decay, near_x]
        for k in range(GROUP - 1):
            b, x = early_tokens(tails[k], tails[k - 1] if k else near_tail, taps, bias)
            early_b.append(b)
            early_x.append(x)
        b_rows = jnp.concatenate(early_b, axis=0).astype(BF16)
        x_rows = jnp.concatenate(early_x, axis=0).astype(BF16)
        added = [dot(b_rows[: 2 * TAIL], x_rows[: 2 * TAIL], ((0,), (0,)))]
        for k in range(GROUP - 1):
            part = slice((k + 2) * TAIL, (k + 3) * TAIL)
            added.append(dot(b_rows[part], x_rows[part], ((0,), (0,))))
        step = 16
        for top in range(0, rows, step):
            part = slice(top, top + step)
            value = from_near * near[part, :].astype(F32) + far_factor * far[part, :].astype(F32) + added[0][part]
            targets[0][part, :] = value.astype(BF16)
            for k in range(GROUP - 1):
                value = decays[k] * value + states[k][part, :].astype(F32) + added[k + 1][part]
                targets[k + 1][part, :] = value.astype(BF16)

    for member in range(GROUP):
        pl.when(member_here() == member)(lambda member=member: run(member))


def patched(before, halo, taps, offset_col):
    width = before.shape[1]
    count = taps.shape[0]
    extended = jnp.concatenate([jnp.zeros((5, width), F32), halo, jnp.zeros((8, width), F32)], axis=0)
    total = before
    for lag in range(1, count):
        shifted_rows = extended[8 - lag : 16 - lag]
        total = total + taps[count - 1 - lag : count - lag] * jnp.where(
            offset_col[0:8, 0:1] >= lag, shifted_rows, 0.0
        )
    return silu(total)


def intra_kernel(
    x_early, x_late, aux_early, aux_late, halo, own, other, own_taps, other_taps, own_bias, other_bias, b, b_aux,
    x_taps, step, sums, offset, lags, y, c_out, carry, bias, scores, columns, x_full, b_full, aux,
):
    first = holds_b()
    block, channels = x_full.shape
    heads = step.shape[0]
    state_size = b.shape[1]
    width = channels // GROUP
    for k, (part, rows, slot) in enumerate(
        ((x_late, aux_late, 0), (x_early, aux_early, 0), (x_early, aux_early, 1), (x_early, aux_early, 2))
    ):
        source = slice(slot * width, (slot + 1) * width)
        x_full[:, quarter(k, width)] = part[:, source]
        aux[:, quarter(k, width)] = rows[0:16, source]
    count = x_taps.shape[0]
    half = block // 2
    time_step, rate_sum = step[...], sums[...]
    columns[...] = rate_sum.T
    offset_col = offset_columns(offset[...])

    packed = halo[...].astype(F32)
    last_rows = jnp.concatenate(
        [packed[3 * k : 3 * k + 3] for k in range((channels + 2 * state_size) // ENDS)], axis=1
    )
    early = patched(aux[0:8, :], last_rows[:, 0:channels], x_taps[...], offset_col)
    x_full[0:16, :] = jnp.concatenate([early, x_full[0:16, :].astype(F32)[8:16]], axis=0).astype(BF16)
    own_halo = last_rows[:, channels : channels + state_size]
    other_halo = last_rows[:, channels + state_size :]
    b_full[...] = b[...]
    early = patched(b_aux[8:16, :], jnp.where(first, own_halo, other_halo), b_aux[0:count, :], offset_col)
    b_full[0:16, :] = jnp.concatenate([early, b[0:16, :].astype(F32)[8:16]], axis=0).astype(BF16)
    c_taps = jnp.where(first, 0.5 * other_taps[...], own_taps[...])
    c_bias = jnp.where(first, 0.5 * other_bias[...], own_bias[...])
    c_source = jnp.where(first, other[...].astype(F32), own[...].astype(F32)).astype(BF16)
    before = convolve(c_source, c_taps, c_bias, [lags[lag] for lag in range(count - 1)])
    c_value = silu(before)
    early = patched(before[0:8], jnp.where(first, other_halo, own_halo), c_taps, offset_col)
    c_out[...] = c_value.astype(BF16)
    c_out[0:16, :] = jnp.concatenate([early, c_value[8:16]], axis=0).astype(BF16)

    row = iota((block, LANES), 0)
    for left in range(0, block, LANES):
        gap = row - (iota((block, LANES), 1) + left)
        linked = jnp.logical_and(gap >= 0, offset_col >= gap.astype(F32))
        bias[:, left : left + LANES] = jnp.where(linked, 0.0, NEG)
    scores[...] = dot(c_out[...], b_full[...], ((1,), (1,)))
    reach = rate_sum - jnp.log(time_step)
    starts = iota(rate_sum.shape, 1) + 1
    factor = turned(jnp.where(offset[...] >= starts, jnp.exp(rate_sum), 0.0))
    for k in range(GROUP):
        carry[:, k * width : (k + 1) * width] = spread(factor, k * width, width)
    lane = iota((1, LANES), 1)
    per_tile = LANES // HEADDIM
    for tile in range(heads // per_tile):
        cols = slice(tile * LANES, (tile + 1) * LANES)
        skip_row = aux[8:9, cols]
        for top in range(0, block, half):
            part = slice(top, top + half)
            seen = top + half
            value = skip_row * x_full[part, cols].astype(F32)
            for k in range(per_tile):
                h = tile * per_tile + k
                gap = columns[part, h : h + 1] - reach[h : h + 1, 0:seen] + bias[part, 0:seen]
                weights = (scores[part, 0:seen] * jnp.exp(gap)).astype(BF16)
                chosen = jnp.where(lane // HEADDIM == k, x_full[0:seen, cols], jnp.zeros((), BF16))
                value = value + dot(weights, chosen)
            y[part, cols] = value


def back_kernel(c, f3, f1, f2, f0, intra, carry, out, held, sems):
    member = member_here()
    width = out.shape[1] // GROUP
    copies = []
    for k, state in enumerate((f0, f1, f2, f3)):
        cols = pl.ds(pl.multiple_of((member ^ k) * width, width), width)
        value = intra[:, cols] + carry[:, cols] * dot(c[...], state[...])
        held[k] = value.astype(BF16)
        copies.append(pltpu.make_async_copy(held.at[k], out.at[:, cols], sems.at[k]))
        copies[-1].start()
    for copy in copies:
        copy.wait()


def exchange(array, mask):
    return lax.ppermute(array, "seq", [(i, i ^ mask) for i in range(lax.axis_size("seq"))])


def turned_on(array, distance):
    count = lax.axis_size("seq")
    return lax.ppermute(array, "seq", [(i, (i + distance) % count) for i in range(count)])


def shifted(array, distance):
    count = lax.axis_size("seq")
    return lax.ppermute(array, "seq", [(i, i + distance) for i in range(count - distance)])


def scan_groups(total, groups):
    rows = total.shape[0] - TAIL
    last = shifted(total[rows:], GROUP)
    held, decay = total[:rows].astype(F32), decay_of(total[rows:].astype(F32))
    held = shifted(held, GROUP)
    decay = shifted(decay, GROUP)
    distance = 1
    while distance < groups:
        held = held + decay * shifted(held, GROUP * distance)
        decay = decay * shifted(decay, GROUP * distance)
        distance *= 2
    near_tail = jnp.concatenate([jnp.zeros((X_LAST_AT, last.shape[1]), BF16), last[X_LAST_AT:]], axis=0)
    near = jnp.concatenate([held.astype(BF16), near_tail], axis=0)
    return near, jnp.zeros_like(near)


def on_device(
    ssm_input, bc_input, conv_taps, conv_bias, bc_taps, bc_bias,
    step_input, step_bias, decay_log, skip_gain, request_offset,
):
    block, channels = ssm_input.shape
    state_size = bc_input.shape[1]
    heads = step_input.shape[0]
    width = channels // GROUP
    groups = lax.axis_size("seq") // GROUP
    here = lax.axis_index("seq")
    hbm = pl.BlockSpec(memory_space=pltpu.HBM)
    vmem = pl.BlockSpec(memory_space=pltpu.VMEM)

    swap = [(i, i ^ 1) for i in range(lax.axis_size("head"))]
    other_bc, other_taps, other_bias = [lax.ppermute(part, "head", swap) for part in (bc_input, bc_taps, bc_bias)]
    other_bias = other_bias[None, :]

    others = jax.ShapeDtypeStruct((block, (GROUP - 1) * width), BF16)
    slice_shape = jax.ShapeDtypeStruct((state_size + TAIL, width), BF16)
    (
        x_early, gated, aux_early, passing, time_step, rate_sum, x, x_taps, x_bias, own, own_taps, own_bias, offset,
        lags, late_parts, early_parts,
    ) = pl.pallas_call(
        channels_kernel,
        out_shape=[
            others,
            others,
            jax.ShapeDtypeStruct((24, (GROUP - 1) * width), F32),
            jax.ShapeDtypeStruct((heads, LANES), F32),
            jax.ShapeDtypeStruct((heads, block), F32),
            jax.ShapeDtypeStruct((heads, block), F32),
            jax.ShapeDtypeStruct((block, channels), BF16),
            jax.ShapeDtypeStruct(conv_taps.shape, F32),
            jax.ShapeDtypeStruct((1, channels), F32),
            jax.ShapeDtypeStruct(bc_input.shape, BF16),
            jax.ShapeDtypeStruct(bc_taps.shape, F32),
            jax.ShapeDtypeStruct((1, state_size), F32),
            jax.ShapeDtypeStruct((1, block), jnp.int32),
            jax.ShapeDtypeStruct((conv_taps.shape[0] - 1, block, block), BF16),
            jax.ShapeDtypeStruct((block, 2 * heads), BF16),
            jax.ShapeDtypeStruct((TAIL, 2 * heads), BF16),
        ],
        in_specs=[hbm] * 11,
        out_specs=[vmem] * 16,
        scratch_shapes=[
            pltpu.VMEM((heads, block), F32),
            pltpu.VMEM((1, heads), F32),
            pltpu.VMEM((1, heads), F32),
            pltpu.VMEM((1, heads), F32),
            pltpu.SemaphoreType.DMA((11,)),
        ],
        compiler_params=PARAMS,
        name="channels",
    )(
        *[
            pltpu.with_memory_space_constraint(array, pltpu.HBM)
            for array in (
                ssm_input, conv_taps, conv_bias[None, :], bc_input, bc_taps, bc_bias[None, :], step_input,
                request_offset[None, :], step_bias[None, :], decay_log[None, :], skip_gain[None, :],
            )
        ]
    )
    s1, s2, s3, b_main, b_aux, b_tail, turn, ends = pl.pallas_call(
        states_kernel,
        out_shape=[
            slice_shape,
            slice_shape,
            slice_shape,
            jax.ShapeDtypeStruct((block, state_size), BF16),
            jax.ShapeDtypeStruct((16, state_size), F32),
            jax.ShapeDtypeStruct((TAIL, state_size), F32),
            jax.ShapeDtypeStruct((state_size, block), BF16),
            jax.ShapeDtypeStruct((TAIL, ENDS), BF16),
        ],
        in_specs=[vmem] * 12,
        out_specs=[vmem] * 8,
        compiler_params=PARAMS,
        name="states",
    )(x, own, other_bc, own_taps, other_taps, own_bias, other_bias, lags, gated, aux_early, passing, offset)
    r1, r2, r3 = exchange(s1, 1), exchange(s2, 2), exchange(s3, 3)
    halo = shifted(ends, 1)
    s0, x_late, aux_late = pl.pallas_call(
        rest_kernel,
        out_shape=[
            slice_shape,
            jax.ShapeDtypeStruct((block, width), BF16),
            jax.ShapeDtypeStruct((24, width), F32),
        ],
        in_specs=[vmem] * 10,
        out_specs=[vmem] * 3,
        scratch_shapes=[pltpu.VMEM((block, width), BF16)],
        compiler_params=PARAMS,
        cost_estimate=pl.CostEstimate(flops=400_000_000, bytes_accessed=2_000_000, transcendentals=200_000),
        name="rest",
    )(x, x_taps, x_bias, lags, late_parts, early_parts, passing, offset, turn, b_tail)
    received = [s0, r1, r2, r3]

    direct = groups == GROUP
    if direct:
        earlier = jnp.zeros((TAIL, width), BF16)
    else:
        last = received[0]
        for k in (1, 2, 3):
            last = jnp.where((here % GROUP) ^ k == GROUP - 1, received[k], last)
        earlier = shifted(last[state_size:], GROUP)
    total = pl.pallas_call(
        lambda *refs: group_kernel(*refs, complete=not direct),
        out_shape=slice_shape,
        in_specs=[vmem] * (GROUP + 4),
        out_specs=vmem,
        compiler_params=PARAMS,
        name="group",
    )(r3, r1, r2, s0, earlier, x_taps, x_bias, b_aux)
    total, halo = lax.optimization_barrier((total, halo))
    if direct:
        far = shifted(total, 2 * GROUP)
        near = turned_on(total, GROUP)
    else:
        near, far = scan_groups(total, groups)

    entering = pl.pallas_call(
        entering_kernel,
        out_shape=[jax.ShapeDtypeStruct((state_size, width), BF16)] * GROUP,
        in_specs=[vmem] * (GROUP + 5),
        out_specs=[vmem] * GROUP,
        compiler_params=PARAMS,
        name="entering",
    )(r3, r1, r2, s0, far, near, x_taps, x_bias, b_aux)
    mine = [entering[0]] + [exchange(entering[k], k) for k in (1, 2, 3)]

    intra, c_conv, carry = pl.pallas_call(
        intra_kernel,
        out_shape=[
            jax.ShapeDtypeStruct((block, channels), F32),
            jax.ShapeDtypeStruct((block, state_size), BF16),
            jax.ShapeDtypeStruct((block, channels), F32),
        ],
        in_specs=[vmem] * 18,
        out_specs=[vmem] * 3,
        scratch_shapes=[
            pltpu.VMEM((block, block), F32),
            pltpu.VMEM((block, block), F32),
            pltpu.VMEM((block, heads), F32),
            pltpu.VMEM((block, channels), BF16),
            pltpu.VMEM((block, state_size), BF16),
            pltpu.VMEM((16, channels), F32),
        ],
        compiler_params=PARAMS,
        cost_estimate=pl.CostEstimate(flops=600_000_000, bytes_accessed=4_000_000, transcendentals=1_000_000),
        name="intra",
    )(
        x_early, x_late, aux_early, aux_late, halo, own, other_bc, own_taps, other_taps, own_bias, other_bias,
        b_main, b_aux, x_taps, time_step, rate_sum, offset, lags,
    )
    out_shape = jax.ShapeDtypeStruct((block, channels), BF16)
    return pl.pallas_call(
        back_kernel,
        out_shape=out_shape,
        in_specs=[vmem] * (GROUP + 3),
        out_specs=hbm,
        scratch_shapes=[pltpu.VMEM((GROUP, block, width), BF16), pltpu.SemaphoreType.DMA((GROUP,))],
        compiler_params=PARAMS,
        name="back",
    )(c_conv, mine[3], mine[1], mine[2], mine[0], intra, carry)


def solution(mesh):
    return jax.shard_map(
        on_device,
        mesh=mesh,
        in_specs=(
            P("seq", "head"),
            P("seq", "head"),
            P(None, "head"),
            P("head"),
            P(None, "head"),
            P("head"),
            P("head", "seq"),
            P("head"),
            P("head"),
            P("head"),
            P("seq"),
        ),
        out_specs=P("seq", "head"),
        check_vma=False,
    )
```

```python
import jax
import jax.numpy as jnp
from jax import lax
from jax.experimental import pallas as pl
from jax.experimental.pallas import tpu as pltpu
from jax.sharding import PartitionSpec as P

HEADDIM = 64
GROUP = 4
TAIL = 16
GATE_AT, X_LAST_AT, X_FIRST_AT, B_LAST_AT, B_FIRST_AT = 1, 4, 7, 10, 13
ENDS = 512
LANES = 128
NEG = -1e30
F32 = jnp.float32
BF16 = jnp.bfloat16
PARAMS = pltpu.CompilerParams(vmem_limit_bytes=24 * 1024 * 1024)


def dot(a, b, dims=((1,), (0,))):
    return lax.dot_general(a, b, (dims, ((), ())), preferred_element_type=F32)


def two_parts(value):
    high = value.astype(BF16).astype(F32)
    return high, value - high


def silu(half):
    return half + half * jnp.tanh(half)


def iota(shape, dim):
    return lax.broadcasted_iota(jnp.int32, shape, dim)


def member_here():
    return lax.axis_index("seq") % GROUP


def group_here():
    return lax.axis_index("seq") // GROUP


def holds_b():
    return lax.axis_index("head") % 2 == 0


def column(row):
    shape = (row.shape[1], row.shape[1])
    wide = jnp.broadcast_to(row, shape)
    return jnp.sum(jnp.where(iota(shape, 0) == iota(shape, 1), wide, 0.0), axis=1, keepdims=True)


def spread(parts, first_channel, width):
    heads = parts.shape[1] // 2
    shape = (2 * heads, width)
    head = iota(shape, 0) & (heads - 1)
    channel = iota(shape, 1) + first_channel
    return dot(parts, (channel // HEADDIM == head).astype(F32).astype(BF16))


def turned(per_head):
    high, low = two_parts(per_head)
    return jnp.concatenate([high, low], axis=0).T.astype(BF16)


def rates(step, step_bias, decay_log):
    heads, block = step.shape
    time_step = jax.nn.softplus(step + step_bias)
    log_decay = -jnp.exp(decay_log) * time_step
    shape = (block, block)
    upto = (iota(shape, 0) <= iota(shape, 1)).astype(F32).astype(BF16)
    first, rest = two_parts(log_decay)
    second, third = two_parts(rest)
    sums = dot(jnp.concatenate([first, second, third], axis=0).astype(BF16), upto)
    return time_step, sums[0:heads] + (sums[heads : 2 * heads] + sums[2 * heads :])


def offset_columns(offset_row):
    wide = jnp.broadcast_to(offset_row.astype(F32), (LANES, offset_row.shape[1]))
    return wide.T


def lag_matrices(offset_col, count):
    block = offset_col.shape[0]
    gap = iota((block, block), 0) - iota((block, block), 1)
    offset_wide = jnp.concatenate([offset_col] * (block // LANES), axis=1)
    return [
        jnp.where(jnp.logical_and(gap == lag, offset_wide >= lag), 1.0, 0.0).astype(BF16)
        for lag in range(1, count)
    ]


def convolve(source, taps, bias, lags):
    count = len(lags) + 1
    total = taps[count - 1 : count] * source.astype(F32) + bias
    for lag, matrix in enumerate(lags, 1):
        total = total + taps[count - 1 - lag : count - lag] * dot(matrix, source)
    return total


def quarter(k, width):
    return pl.ds(pl.multiple_of((member_here() ^ k) * width, width), width)


def channel_slice(k, slot, x, taps, bias, lags, late_parts, early_parts, x_out, gated, aux):
    block = x.shape[0]
    width = x.shape[1] // GROUP
    cols, to = quarter(k, width), slice(slot * width, (slot + 1) * width)
    source = x[:, cols]
    before = convolve(source, taps[:, cols], bias[:, cols], [lags[lag] for lag in range(lags.shape[0])])
    value = silu(before).astype(BF16)
    x_out[:, to] = value
    first_channel = (member_here() ^ k) * width
    gated[:, to] = (value.astype(F32) * spread(late_parts[...], first_channel, width)).astype(BF16)
    aux[0:8, to] = before[0:8]
    early = spread(early_parts[...], first_channel, width)
    first = source[0:TAIL].astype(F32)
    last_rows = source[block - TAIL : block].astype(F32)
    aux[8:24, to] = jnp.concatenate(
        [early[3:4], early[0:3], last_rows[TAIL - 3 :], first[0:3], jnp.zeros((TAIL - 10, width), F32)], axis=0
    )


def channels_kernel(
    x_hbm, taps_hbm, bias_hbm, own_hbm, own_taps_hbm, own_bias_hbm, step_hbm, offset_hbm,
    step_bias_hbm, decay_hbm, skip_hbm,
    x_out, gated, aux, passing_out, step_out, sums_out, x, taps, bias, own, own_taps, own_bias, offset,
    lags, late_parts, early_parts, step, step_bias, decay_log, skip, sems,
):
    block = x.shape[0]
    count = taps.shape[0]
    pairs = [
        (offset_hbm, offset), (step_hbm, step), (step_bias_hbm, step_bias), (decay_hbm, decay_log),
        (x_hbm, x), (taps_hbm, taps), (bias_hbm, bias), (skip_hbm, skip), (own_taps_hbm, own_taps),
        (own_bias_hbm, own_bias), (own_hbm, own),
    ]
    copies = [pltpu.make_async_copy(*pair, sems.at[k]) for k, pair in enumerate(pairs)]
    for copy in copies:
        copy.start()
    copies[0].wait()
    for lag, matrix in enumerate(lag_matrices(offset_columns(offset[...]), count)):
        lags[lag] = matrix
    for copy in copies[1:4]:
        copy.wait()
    time_step, rate_sum = rates(step[...], column(step_bias[...]), column(decay_log[...]))
    step_out[...] = time_step
    sums_out[...] = rate_sum
    last_offset = offset[0, block - 1]
    place = iota(rate_sum.shape, 1)
    last = rate_sum[:, block - 1 : block]
    gate = jnp.exp(jnp.where(last_offset >= block - 1 - place, last - rate_sum, NEG)) * time_step
    passing = jnp.exp(last) * (last_offset >= block).astype(F32)
    passing_out[...] = jnp.broadcast_to(passing, passing_out.shape)
    for copy in copies[4:8]:
        copy.wait()
    taps[...] = 0.5 * taps[...]
    bias[...] = 0.5 * bias[...]
    early_parts[...] = turned(jnp.where(place == count - 1, column(skip[...]), gate))[0:TAIL]
    late_parts[...] = turned(jnp.where(place >= count - 1, gate, 0.0))
    for slot, k in enumerate((1, 2, 3)):
        channel_slice(k, slot, x, taps, bias, lags, late_parts, early_parts, x_out, gated, aux)
    for copy in copies[8:]:
        copy.wait()
    own_taps[...] = 0.5 * own_taps[...]
    own_bias[...] = 0.5 * own_bias[...]


def message(out, k, state, passing, offset, count, gates_and_x, b_tail):
    rows, width = state.shape
    heads = passing.shape[0]
    slice_heads = heads // GROUP
    out[0:rows, :] = state.astype(BF16)
    lane = iota((heads, width), 1)
    head = iota((heads, width), 0)
    high, low = two_parts(passing[:, 0:1])
    offsets = pltpu.roll(jnp.minimum(offset[...], count - 1).astype(F32), 2 * slice_heads, 1)
    offsets = jnp.where(
        jnp.logical_and(lane[0:1] >= 2 * slice_heads, lane[0:1] < 2 * slice_heads + count - 1), offsets, 0.0
    )
    at = lane + (member_here() ^ k) * slice_heads
    packed = jnp.where(lane < slice_heads, jnp.where(at == head, high, 0.0), 0.0)
    packed = jnp.where(jnp.logical_and(lane >= slice_heads, at == head + slice_heads), low, packed)
    packed = jnp.where(lane < 2 * slice_heads, packed, 0.0)
    misc = jnp.sum(packed, axis=0, keepdims=True) + offsets
    row = iota((TAIL, width), 0)
    tail = jnp.where(row == 0, misc, jnp.where(row < B_LAST_AT, gates_and_x, b_tail))
    out[rows:, :] = tail.astype(BF16)


def states_kernel(
    x, own, other, own_taps, other_taps, own_bias, other_bias, lags, gated, aux, passing, offset,
    s1, s2, s3, b_out, b_taps, b_tail, turn, ends,
):
    first = holds_b()
    block, state_size = own.shape
    count = own_taps.shape[0]
    channels = x.shape[1]
    last_rows = jnp.concatenate(
        [part[block - TAIL : block, :].astype(F32)[TAIL - 3 :] for part in (x, own, other)], axis=1
    )
    packed = [last_rows[:, at : at + ENDS] for at in range(0, channels + 2 * state_size, ENDS)]
    blank = jnp.zeros((TAIL - 3 * len(packed), ENDS), F32)
    ends[...] = jnp.concatenate(packed + [blank], axis=0).astype(BF16)
    taps = jnp.where(first, own_taps[...], 0.5 * other_taps[...])
    bias = jnp.where(first, own_bias[...], 0.5 * other_bias[...])
    source = jnp.where(first, own[...].astype(F32), other[...].astype(F32))
    before = convolve(source.astype(BF16), taps, bias, [lags[lag] for lag in range(count - 1)])
    value = silu(before)
    b_out[...] = value.astype(BF16)
    turn[...] = value.T.astype(BF16)
    b_taps[...] = jnp.concatenate([taps, bias, jnp.zeros((8 - count - 1, state_size), F32), before[0:8]], axis=0)
    b_tail[...] = jnp.concatenate(
        [jnp.zeros((B_LAST_AT, state_size), F32), source[block - 3 :], source[0:3]], axis=0
    )
    width = gated.shape[1] // (GROUP - 1)
    for slot, (k, out) in enumerate(((1, s1), (2, s2), (3, s3))):
        cols = slice(slot * width, (slot + 1) * width)
        message(out, k, dot(turn[...], gated[:, cols]), passing, offset, count, aux[8:24, cols], b_tail[...])


def rest_kernel(
    x, taps, bias, lags, late_parts, early_parts, passing, offset, turn, b_tail, s0, x_out, aux, gated,
):
    channel_slice(0, 0, x, taps, bias, lags, late_parts, early_parts, x_out, gated, aux)
    state = dot(turn[...], gated[...])
    message(s0, 0, state, passing, offset, taps.shape[0], aux[8:24, :], b_tail[...])


def tail_of(state):
    rows = state.shape[0]
    return state[rows - TAIL : rows, :].astype(F32)


def decay_of(tail):
    width = tail.shape[1]
    slice_heads = width // HEADDIM
    channel = iota((1, width), 1)
    value = jnp.zeros((1, width), F32)
    for head in range(slice_heads):
        both = tail[0:1, head : head + 1] + tail[0:1, slice_heads + head : slice_heads + head + 1]
        value = jnp.where(channel // HEADDIM == head, both, value)
    return value


def pack_decay(decay, tail):
    width = decay.shape[1]
    slice_heads = width // HEADDIM
    lane = iota((1, width), 1)
    high, low = two_parts(decay)
    row = jnp.where(lane >= 2 * slice_heads, tail[0:1], 0.0)
    for head in range(slice_heads):
        at = head * HEADDIM
        row = jnp.where(lane == head, high[:, at : at + 1], row)
        row = jnp.where(lane == slice_heads + head, low[:, at : at + 1], row)
    return row


def tail_taps(x_taps, x_bias, b_taps, count):
    width = x_taps.shape[1]
    upper = iota((TAIL, width), 0) < B_LAST_AT
    taps = [jnp.where(upper, x_taps[k : k + 1], b_taps[k : k + 1]) for k in range(count)]
    return taps, jnp.where(upper, x_bias, b_taps[count : count + 1])


def early_tokens(tail, earlier, taps, bias):
    width = tail.shape[1]
    slice_heads = width // HEADDIM
    count = len(taps)
    row = iota(tail.shape, 0)
    is_last = jnp.logical_or(
        jnp.logical_and(row >= X_LAST_AT, row < X_FIRST_AT),
        jnp.logical_and(row >= B_LAST_AT, row < B_FIRST_AT),
    )
    rows = jnp.where(is_last, earlier, tail)
    offset = jnp.full(tail.shape, -1.0, F32)
    for token in range(count - 1):
        lane = 2 * slice_heads + token
        here = jnp.logical_or(row == X_FIRST_AT + token, row == B_FIRST_AT + token)
        offset = jnp.where(here, tail[0:1, lane : lane + 1], offset)
    total = taps[count - 1] * rows + bias
    for lag in range(1, count):
        total = total + taps[count - 1 - lag] * jnp.where(offset >= lag, pltpu.roll(rows, lag, 0), 0.0)
    value = silu(total).astype(BF16).astype(F32)
    gate = pltpu.roll(tail, B_FIRST_AT - GATE_AT, 0)
    wanted = row >= B_FIRST_AT
    b = jnp.where(wanted, value, 0.0)
    x = jnp.where(wanted, pltpu.roll(value, B_FIRST_AT - X_FIRST_AT, 0) * gate, 0.0)
    return b, x


def group_kernel(r3, r1, r2, r0, earlier, x_taps, x_bias, b_taps, total, *, complete):
    rows = r0.shape[0] - TAIL
    width = r0.shape[1]
    count = x_taps.shape[0]
    held = (r0, r1, r2, r3)

    def run(member):
        cols = slice(member * width, (member + 1) * width)
        taps, bias = tail_taps(x_taps[:, cols], x_bias[:, cols], b_taps[...], count)
        states = [held[member ^ k] for k in range(GROUP)]
        tails = [tail_of(state) for state in states]
        decays = [decay_of(tail) for tail in tails]
        factors = [None] * GROUP
        factor = jnp.ones((1, width), F32)
        for k in reversed(range(GROUP)):
            factors[k] = factor
            factor = factor * decays[k]
        early_b, early_x = [], []
        for k in range(0 if complete else 1, GROUP):
            before = tails[k - 1] if k else tail_of(earlier)
            b, x = early_tokens(tails[k], before, taps, bias)
            early_b.append(b)
            early_x.append(x * factors[k])
        b_rows = jnp.concatenate(early_b, axis=0).astype(BF16)
        added = dot(b_rows, jnp.concatenate(early_x, axis=0).astype(BF16), ((0,), (0,)))
        step = 32
        for top in range(0, rows, step):
            part = slice(top, top + step)
            value = added[part]
            for k in range(GROUP):
                value = value + factors[k] * states[k][part, :].astype(F32)
            total[part, :] = value.astype(BF16)
        row = iota((TAIL, width), 0)
        is_last = jnp.logical_or(
            jnp.logical_and(row >= X_LAST_AT, row < X_FIRST_AT),
            jnp.logical_and(row >= B_LAST_AT, row < B_FIRST_AT),
        )
        gates = jnp.zeros((1, width), F32) if complete else factors[0]
        tail = jnp.where(is_last, tails[GROUP - 1], tails[0])
        tail = jnp.where(row < X_LAST_AT, tail * gates, tail)
        tail = jnp.where(row == 0, pack_decay(factor, tails[0]), tail)
        total[rows:, :] = tail.astype(BF16)

    for member in range(GROUP):
        pl.when(member_here() == member)(lambda member=member: run(member))


def before_kernel(r3, r1, r2, r0, near, x_taps, x_bias, b_taps, partial, factors):
    rows = r0.shape[0] - TAIL
    width = r0.shape[1]
    count = x_taps.shape[0]
    held = (r0, r1, r2, r3)
    one = jnp.ones((1, width), F32)
    from_near = jnp.where(group_here() >= 1, one, 0.0)

    def run(member):
        cols = slice(member * width, (member + 1) * width)
        taps, bias = tail_taps(x_taps[:, cols], x_bias[:, cols], b_taps[...], count)
        states = [held[member ^ k] for k in range(GROUP)]
        tails = [tail_of(state) for state in states]
        near_tail = from_near * tail_of(near)
        decays = [decay_of(tail) for tail in tails]
        added = []
        factor = one
        for k in range(GROUP):
            factors[member ^ k : (member ^ k) + 1, :] = factor
            factor = factor * decays[k]
        factors[GROUP : GROUP + 1, :] = decay_of(near_tail)
        for k in range(GROUP - 1):
            b, x = early_tokens(tails[k], tails[k - 1] if k else near_tail, taps, bias)
            added.append(dot(b.astype(BF16), x.astype(BF16), ((0,), (0,))))
        step = 32
        for top in range(0, rows, step):
            part = slice(top, top + step)
            value = from_near * near[part, :].astype(F32)
            partial[member, part, :] = value
            for k in range(GROUP - 1):
                value = decays[k] * value + states[k][part, :].astype(F32) + added[k][part]
                partial[member ^ (k + 1), part, :] = value

    for member in range(GROUP):
        pl.when(member_here() == member)(lambda member=member: run(member))


def entering_kernel(far, near, partial, factors, x_taps, x_bias, b_taps, e0, e1, e2, e3):
    group = group_here()
    outs = (e0, e1, e2, e3)
    rows, width = e0.shape
    one = jnp.ones((1, width), F32)
    from_far = jnp.where(group >= 2, one, 0.0)
    near_tail = jnp.where(group >= 1, one, 0.0) * tail_of(near)
    far_tail = from_far * tail_of(far)
    cols = quarter(0, width)
    taps, bias = tail_taps(x_taps[:, cols], x_bias[:, cols], b_taps[...], x_taps.shape[0])
    near_decay = factors[GROUP : GROUP + 1, :]
    far_factor = near_decay * from_far
    far_b, far_x = early_tokens(far_tail, jnp.zeros_like(far_tail), taps, bias)
    near_b, near_x = early_tokens(near_tail, far_tail, taps, bias)
    b_rows = jnp.concatenate([far_b, near_b], axis=0).astype(BF16)
    x_rows = jnp.concatenate([far_x * near_decay, near_x], axis=0).astype(BF16)
    added = dot(b_rows, x_rows, ((0,), (0,)))
    step = 32
    for top in range(0, rows, step):
        part = slice(top, top + step)
        value = far_factor * far[part, :].astype(F32) + added[part]
        for k, out in enumerate(outs):
            out[part, :] = (partial[k, part, :] + factors[k : k + 1, :] * value).astype(BF16)


def patched(before, halo, taps, offset_col):
    width = before.shape[1]
    count = taps.shape[0]
    extended = jnp.concatenate([jnp.zeros((5, width), F32), halo, jnp.zeros((8, width), F32)], axis=0)
    total = before
    for lag in range(1, count):
        shifted_rows = extended[8 - lag : 16 - lag]
        total = total + taps[count - 1 - lag : count - lag] * jnp.where(
            offset_col[0:8, 0:1] >= lag, shifted_rows, 0.0
        )
    return silu(total)


def intra_kernel(
    x_early, x_late, aux_early, aux_late, halo, own, other, own_taps, other_taps, own_bias, other_bias, b, b_aux,
    x_taps, step, sums, offset, lags, y, c_out, carry, bias, scores, columns, x_full, b_full, aux,
):
    first = holds_b()
    block, channels = x_full.shape
    heads = step.shape[0]
    state_size = b.shape[1]
    width = channels // GROUP
    for k, (part, rows, slot) in enumerate(
        ((x_late, aux_late, 0), (x_early, aux_early, 0), (x_early, aux_early, 1), (x_early, aux_early, 2))
    ):
        source = slice(slot * width, (slot + 1) * width)
        x_full[:, quarter(k, width)] = part[:, source]
        aux[:, quarter(k, width)] = rows[0:16, source]
    count = x_taps.shape[0]
    half = block // 2
    time_step, rate_sum = step[...], sums[...]
    columns[...] = rate_sum.T
    offset_col = offset_columns(offset[...])

    packed = halo[...].astype(F32)
    last_rows = jnp.concatenate(
        [packed[3 * k : 3 * k + 3] for k in range((channels + 2 * state_size) // ENDS)], axis=1
    )
    early = patched(aux[0:8, :], last_rows[:, 0:channels], x_taps[...], offset_col)
    x_full[0:16, :] = jnp.concatenate([early, x_full[0:16, :].astype(F32)[8:16]], axis=0).astype(BF16)
    own_halo = last_rows[:, channels : channels + state_size]
    other_halo = last_rows[:, channels + state_size :]
    b_full[...] = b[...]
    early = patched(b_aux[8:16, :], jnp.where(first, own_halo, other_halo), b_aux[0:count, :], offset_col)
    b_full[0:16, :] = jnp.concatenate([early, b[0:16, :].astype(F32)[8:16]], axis=0).astype(BF16)
    c_taps = jnp.where(first, 0.5 * other_taps[...], own_taps[...])
    c_bias = jnp.where(first, 0.5 * other_bias[...], own_bias[...])
    c_source = jnp.where(first, other[...].astype(F32), own[...].astype(F32)).astype(BF16)
    before = convolve(c_source, c_taps, c_bias, [lags[lag] for lag in range(count - 1)])
    c_value = silu(before)
    early = patched(before[0:8], jnp.where(first, other_halo, own_halo), c_taps, offset_col)
    c_out[...] = c_value.astype(BF16)
    c_out[0:16, :] = jnp.concatenate([early, c_value[8:16]], axis=0).astype(BF16)

    row = iota((block, LANES), 0)
    for left in range(0, block, LANES):
        gap = row - (iota((block, LANES), 1) + left)
        linked = jnp.logical_and(gap >= 0, offset_col >= gap.astype(F32))
        bias[:, left : left + LANES] = jnp.where(linked, 0.0, NEG)
    scores[...] = dot(c_out[...], b_full[...], ((1,), (1,)))
    reach = rate_sum - jnp.log(time_step)
    starts = iota(rate_sum.shape, 1) + 1
    factor = turned(jnp.where(offset[...] >= starts, jnp.exp(rate_sum), 0.0))
    for k in range(GROUP):
        carry[:, k * width : (k + 1) * width] = spread(factor, k * width, width)
    lane = iota((1, LANES), 1)
    per_tile = LANES // HEADDIM
    for tile in range(heads // per_tile):
        cols = slice(tile * LANES, (tile + 1) * LANES)
        skip_row = aux[8:9, cols]
        for top in range(0, block, half):
            part = slice(top, top + half)
            seen = top + half
            value = skip_row * x_full[part, cols].astype(F32)
            for k in range(per_tile):
                h = tile * per_tile + k
                gap = columns[part, h : h + 1] - reach[h : h + 1, 0:seen] + bias[part, 0:seen]
                weights = (scores[part, 0:seen] * jnp.exp(gap)).astype(BF16)
                chosen = jnp.where(lane // HEADDIM == k, x_full[0:seen, cols], jnp.zeros((), BF16))
                value = value + dot(weights, chosen)
            y[part, cols] = value


def back_kernel(c, f3, f1, f2, f0, intra, carry, out, held, sems):
    member = member_here()
    width = out.shape[1] // GROUP
    copies = []
    for k, state in enumerate((f0, f1, f2, f3)):
        cols = pl.ds(pl.multiple_of((member ^ k) * width, width), width)
        value = intra[:, cols] + carry[:, cols] * dot(c[...], state[...])
        held[k] = value.astype(BF16)
        copies.append(pltpu.make_async_copy(held.at[k], out.at[:, cols], sems.at[k]))
        copies[-1].start()
    for copy in copies:
        copy.wait()


def exchange(array, mask):
    return lax.ppermute(array, "seq", [(i, i ^ mask) for i in range(lax.axis_size("seq"))])


def turned_on(array, distance):
    count = lax.axis_size("seq")
    return lax.ppermute(array, "seq", [(i, (i + distance) % count) for i in range(count)])


def shifted(array, distance):
    count = lax.axis_size("seq")
    return lax.ppermute(array, "seq", [(i, i + distance) for i in range(count - distance)])


def scan_groups(total, groups):
    rows = total.shape[0] - TAIL
    last = shifted(total[rows:], GROUP)
    held, decay = total[:rows].astype(F32), decay_of(total[rows:].astype(F32))
    held = shifted(held, GROUP)
    decay = shifted(decay, GROUP)
    distance = 1
    while distance < groups:
        held = held + decay * shifted(held, GROUP * distance)
        decay = decay * shifted(decay, GROUP * distance)
        distance *= 2
    near_tail = jnp.concatenate([jnp.zeros((X_LAST_AT, last.shape[1]), BF16), last[X_LAST_AT:]], axis=0)
    near = jnp.concatenate([held.astype(BF16), near_tail], axis=0)
    return near, jnp.zeros_like(near)


def on_device(
    ssm_input, bc_input, conv_taps, conv_bias, bc_taps, bc_bias,
    step_input, step_bias, decay_log, skip_gain, request_offset,
):
    block, channels = ssm_input.shape
    state_size = bc_input.shape[1]
    heads = step_input.shape[0]
    width = channels // GROUP
    groups = lax.axis_size("seq") // GROUP
    here = lax.axis_index("seq")
    hbm = pl.BlockSpec(memory_space=pltpu.HBM)
    vmem = pl.BlockSpec(memory_space=pltpu.VMEM)

    swap = [(i, i ^ 1) for i in range(lax.axis_size("head"))]
    other_bc, other_taps, other_bias = [lax.ppermute(part, "head", swap) for part in (bc_input, bc_taps, bc_bias)]
    other_bias = other_bias[None, :]

    others = jax.ShapeDtypeStruct((block, (GROUP - 1) * width), BF16)
    slice_shape = jax.ShapeDtypeStruct((state_size + TAIL, width), BF16)
    (
        x_early, gated, aux_early, passing, time_step, rate_sum, x, x_taps, x_bias, own, own_taps, own_bias, offset,
        lags, late_parts, early_parts,
    ) = pl.pallas_call(
        channels_kernel,
        out_shape=[
            others,
            others,
            jax.ShapeDtypeStruct((24, (GROUP - 1) * width), F32),
            jax.ShapeDtypeStruct((heads, LANES), F32),
            jax.ShapeDtypeStruct((heads, block), F32),
            jax.ShapeDtypeStruct((heads, block), F32),
            jax.ShapeDtypeStruct((block, channels), BF16),
            jax.ShapeDtypeStruct(conv_taps.shape, F32),
            jax.ShapeDtypeStruct((1, channels), F32),
            jax.ShapeDtypeStruct(bc_input.shape, BF16),
            jax.ShapeDtypeStruct(bc_taps.shape, F32),
            jax.ShapeDtypeStruct((1, state_size), F32),
            jax.ShapeDtypeStruct((1, block), jnp.int32),
            jax.ShapeDtypeStruct((conv_taps.shape[0] - 1, block, block), BF16),
            jax.ShapeDtypeStruct((block, 2 * heads), BF16),
            jax.ShapeDtypeStruct((TAIL, 2 * heads), BF16),
        ],
        in_specs=[hbm] * 11,
        out_specs=[vmem] * 16,
        scratch_shapes=[
            pltpu.VMEM((heads, block), F32),
            pltpu.VMEM((1, heads), F32),
            pltpu.VMEM((1, heads), F32),
            pltpu.VMEM((1, heads), F32),
            pltpu.SemaphoreType.DMA((11,)),
        ],
        compiler_params=PARAMS,
        name="channels",
    )(
        *[
            pltpu.with_memory_space_constraint(array, pltpu.HBM)
            for array in (
                ssm_input, conv_taps, conv_bias[None, :], bc_input, bc_taps, bc_bias[None, :], step_input,
                request_offset[None, :], step_bias[None, :], decay_log[None, :], skip_gain[None, :],
            )
        ]
    )
    s1, s2, s3, b_main, b_aux, b_tail, turn, ends = pl.pallas_call(
        states_kernel,
        out_shape=[
            slice_shape,
            slice_shape,
            slice_shape,
            jax.ShapeDtypeStruct((block, state_size), BF16),
            jax.ShapeDtypeStruct((16, state_size), F32),
            jax.ShapeDtypeStruct((TAIL, state_size), F32),
            jax.ShapeDtypeStruct((state_size, block), BF16),
            jax.ShapeDtypeStruct((TAIL, ENDS), BF16),
        ],
        in_specs=[vmem] * 12,
        out_specs=[vmem] * 8,
        compiler_params=PARAMS,
        name="states",
    )(x, own, other_bc, own_taps, other_taps, own_bias, other_bias, lags, gated, aux_early, passing, offset)
    r1, r2, r3 = exchange(s1, 1), exchange(s2, 2), exchange(s3, 3)
    halo = shifted(ends, 1)
    s0, x_late, aux_late = pl.pallas_call(
        rest_kernel,
        out_shape=[
            slice_shape,
            jax.ShapeDtypeStruct((block, width), BF16),
            jax.ShapeDtypeStruct((24, width), F32),
        ],
        in_specs=[vmem] * 10,
        out_specs=[vmem] * 3,
        scratch_shapes=[pltpu.VMEM((block, width), BF16)],
        compiler_params=PARAMS,
        cost_estimate=pl.CostEstimate(flops=400_000_000, bytes_accessed=2_000_000, transcendentals=200_000),
        name="rest",
    )(x, x_taps, x_bias, lags, late_parts, early_parts, passing, offset, turn, b_tail)
    received = [s0, r1, r2, r3]

    direct = groups == GROUP
    if direct:
        earlier = jnp.zeros((TAIL, width), BF16)
    else:
        last = received[0]
        for k in (1, 2, 3):
            last = jnp.where((here % GROUP) ^ k == GROUP - 1, received[k], last)
        earlier = shifted(last[state_size:], GROUP)
    total = pl.pallas_call(
        lambda *refs: group_kernel(*refs, complete=not direct),
        out_shape=slice_shape,
        in_specs=[vmem] * (GROUP + 4),
        out_specs=vmem,
        compiler_params=PARAMS,
        name="group",
    )(r3, r1, r2, s0, earlier, x_taps, x_bias, b_aux)
    total, halo = lax.optimization_barrier((total, halo))
    if direct:
        far = shifted(total, 2 * GROUP)
        near = turned_on(total, GROUP)
    else:
        near, far = scan_groups(total, groups)

    partial, factors = pl.pallas_call(
        before_kernel,
        out_shape=[
            jax.ShapeDtypeStruct((GROUP, state_size, width), F32),
            jax.ShapeDtypeStruct((8, width), F32),
        ],
        in_specs=[vmem] * (GROUP + 4),
        out_specs=[vmem] * 2,
        compiler_params=PARAMS,
        cost_estimate=pl.CostEstimate(flops=100_000_000, bytes_accessed=2_000_000, transcendentals=10_000),
        name="before",
    )(r3, r1, r2, s0, near, x_taps, x_bias, b_aux)
    entering = pl.pallas_call(
        entering_kernel,
        out_shape=[jax.ShapeDtypeStruct((state_size, width), BF16)] * GROUP,
        in_specs=[vmem] * 7,
        out_specs=[vmem] * GROUP,
        compiler_params=PARAMS,
        name="entering",
    )(far, near, partial, factors, x_taps, x_bias, b_aux)
    mine = [entering[0]] + [exchange(entering[k], k) for k in (1, 2, 3)]

    intra, c_conv, carry = pl.pallas_call(
        intra_kernel,
        out_shape=[
            jax.ShapeDtypeStruct((block, channels), F32),
            jax.ShapeDtypeStruct((block, state_size), BF16),
            jax.ShapeDtypeStruct((block, channels), F32),
        ],
        in_specs=[vmem] * 18,
        out_specs=[vmem] * 3,
        scratch_shapes=[
            pltpu.VMEM((block, block), F32),
            pltpu.VMEM((block, block), F32),
            pltpu.VMEM((block, heads), F32),
            pltpu.VMEM((block, channels), BF16),
            pltpu.VMEM((block, state_size), BF16),
            pltpu.VMEM((16, channels), F32),
        ],
        compiler_params=PARAMS,
        cost_estimate=pl.CostEstimate(flops=600_000_000, bytes_accessed=4_000_000, transcendentals=1_000_000),
        name="intra",
    )(
        x_early, x_late, aux_early, aux_late, halo, own, other_bc, own_taps, other_taps, own_bias, other_bias,
        b_main, b_aux, x_taps, time_step, rate_sum, offset, lags,
    )
    out_shape = jax.ShapeDtypeStruct((block, channels), BF16)
    return pl.pallas_call(
        back_kernel,
        out_shape=out_shape,
        in_specs=[vmem] * (GROUP + 3),
        out_specs=hbm,
        scratch_shapes=[pltpu.VMEM((GROUP, block, width), BF16), pltpu.SemaphoreType.DMA((GROUP,))],
        compiler_params=PARAMS,
        name="back",
    )(c_conv, mine[3], mine[1], mine[2], mine[0], intra, carry)


def solution(mesh):
    return jax.shard_map(
        on_device,
        mesh=mesh,
        in_specs=(
            P("seq", "head"),
            P("seq", "head"),
            P(None, "head"),
            P("head"),
            P(None, "head"),
            P("head"),
            P("head", "seq"),
            P("head"),
            P("head"),
            P("head"),
            P("seq"),
        ),
        out_specs=P("seq", "head"),
        check_vma=False,
    )
```

```python
import jax
import jax.numpy as jnp
from jax import lax
from jax.experimental import pallas as pl
from jax.experimental.pallas import tpu as pltpu
from jax.sharding import PartitionSpec as P

HEADDIM = 64
GROUP = 4
TAIL = 16
GATE_AT, X_LAST_AT, X_FIRST_AT, B_LAST_AT, B_FIRST_AT = 1, 4, 7, 10, 13
ENDS = 512
LANES = 128
NEG = -1e30
F32 = jnp.float32
BF16 = jnp.bfloat16
PARAMS = pltpu.CompilerParams(vmem_limit_bytes=24 * 1024 * 1024)


def dot(a, b, dims=((1,), (0,))):
    return lax.dot_general(a, b, (dims, ((), ())), preferred_element_type=F32)


def two_parts(value):
    high = value.astype(BF16).astype(F32)
    return high, value - high


def silu(half):
    return half + half * jnp.tanh(half)


def iota(shape, dim):
    return lax.broadcasted_iota(jnp.int32, shape, dim)


def member_here():
    return lax.axis_index("seq") % GROUP


def group_here():
    return lax.axis_index("seq") // GROUP


def holds_b():
    return lax.axis_index("head") % 2 == 0


def column(row):
    shape = (row.shape[1], row.shape[1])
    wide = jnp.broadcast_to(row, shape)
    return jnp.sum(jnp.where(iota(shape, 0) == iota(shape, 1), wide, 0.0), axis=1, keepdims=True)


def spread(parts, first_channel, width):
    heads = parts.shape[1] // 2
    shape = (2 * heads, width)
    head = iota(shape, 0) & (heads - 1)
    channel = iota(shape, 1) + first_channel
    return dot(parts, (channel // HEADDIM == head).astype(F32).astype(BF16))


def turned(per_head):
    high, low = two_parts(per_head)
    return jnp.concatenate([high, low], axis=0).T.astype(BF16)


def rates(step, step_bias, decay_log):
    heads, block = step.shape
    time_step = jax.nn.softplus(step + step_bias)
    log_decay = -jnp.exp(decay_log) * time_step
    shape = (block, block)
    upto = (iota(shape, 0) <= iota(shape, 1)).astype(F32).astype(BF16)
    first, rest = two_parts(log_decay)
    second, third = two_parts(rest)
    sums = dot(jnp.concatenate([first, second, third], axis=0).astype(BF16), upto)
    return time_step, sums[0:heads] + (sums[heads : 2 * heads] + sums[2 * heads :])


def offset_columns(offset_row):
    wide = jnp.broadcast_to(offset_row.astype(F32), (LANES, offset_row.shape[1]))
    return wide.T


def lag_matrices(offset_col, count):
    block = offset_col.shape[0]
    gap = iota((block, block), 0) - iota((block, block), 1)
    offset_wide = jnp.concatenate([offset_col] * (block // LANES), axis=1)
    return [
        jnp.where(jnp.logical_and(gap == lag, offset_wide >= lag), 1.0, 0.0).astype(BF16)
        for lag in range(1, count)
    ]


def convolve(source, taps, bias, lags):
    count = len(lags) + 1
    total = taps[count - 1 : count] * source.astype(F32) + bias
    for lag, matrix in enumerate(lags, 1):
        total = total + taps[count - 1 - lag : count - lag] * dot(matrix, source)
    return total


def quarter(k, width):
    return pl.ds(pl.multiple_of((member_here() ^ k) * width, width), width)


def channel_slice(k, slot, x, taps, bias, lags, late_parts, early_parts, x_out, gated, aux):
    block = x.shape[0]
    width = x.shape[1] // GROUP
    cols, to = quarter(k, width), slice(slot * width, (slot + 1) * width)
    source = x[:, cols]
    before = convolve(source, taps[:, cols], bias[:, cols], [lags[lag] for lag in range(lags.shape[0])])
    value = silu(before).astype(BF16)
    x_out[:, to] = value
    first_channel = (member_here() ^ k) * width
    gated[:, to] = (value.astype(F32) * spread(late_parts[...], first_channel, width)).astype(BF16)
    aux[0:8, to] = before[0:8]
    early = spread(early_parts[...], first_channel, width)
    first = source[0:TAIL].astype(F32)
    last_rows = source[block - TAIL : block].astype(F32)
    aux[8:24, to] = jnp.concatenate(
        [early[3:4], early[0:3], last_rows[TAIL - 3 :], first[0:3], jnp.zeros((TAIL - 10, width), F32)], axis=0
    )


def channels_kernel(
    x_hbm, taps_hbm, bias_hbm, own_hbm, own_taps_hbm, own_bias_hbm, step_hbm, offset_hbm,
    step_bias_hbm, decay_hbm, skip_hbm,
    x_out, gated, aux, passing_out, step_out, sums_out, x, taps, bias, own, own_taps, own_bias, offset,
    lags, late_parts, early_parts, step, step_bias, decay_log, skip, sems,
):
    block = x.shape[0]
    count = taps.shape[0]
    pairs = [
        (offset_hbm, offset), (step_hbm, step), (step_bias_hbm, step_bias), (decay_hbm, decay_log),
        (x_hbm, x), (taps_hbm, taps), (bias_hbm, bias), (skip_hbm, skip), (own_taps_hbm, own_taps),
        (own_bias_hbm, own_bias), (own_hbm, own),
    ]
    copies = [pltpu.make_async_copy(*pair, sems.at[k]) for k, pair in enumerate(pairs)]
    for copy in copies:
        copy.start()
    copies[0].wait()
    for lag, matrix in enumerate(lag_matrices(offset_columns(offset[...]), count)):
        lags[lag] = matrix
    for copy in copies[1:4]:
        copy.wait()
    time_step, rate_sum = rates(step[...], column(step_bias[...]), column(decay_log[...]))
    step_out[...] = time_step
    sums_out[...] = rate_sum
    last_offset = offset[0, block - 1]
    place = iota(rate_sum.shape, 1)
    last = rate_sum[:, block - 1 : block]
    gate = jnp.exp(jnp.where(last_offset >= block - 1 - place, last - rate_sum, NEG)) * time_step
    passing = jnp.exp(last) * (last_offset >= block).astype(F32)
    passing_out[...] = jnp.broadcast_to(passing, passing_out.shape)
    for copy in copies[4:8]:
        copy.wait()
    taps[...] = 0.5 * taps[...]
    bias[...] = 0.5 * bias[...]
    early_parts[...] = turned(jnp.where(place == count - 1, column(skip[...]), gate))[0:TAIL]
    late_parts[...] = turned(jnp.where(place >= count - 1, gate, 0.0))
    for slot, k in enumerate((1, 2, 3)):
        channel_slice(k, slot, x, taps, bias, lags, late_parts, early_parts, x_out, gated, aux)
    for copy in copies[8:]:
        copy.wait()
    own_taps[...] = 0.5 * own_taps[...]
    own_bias[...] = 0.5 * own_bias[...]


def message(out, k, state, passing, offset, count, gates_and_x, b_tail):
    rows, width = state.shape
    heads = passing.shape[0]
    slice_heads = heads // GROUP
    out[0:rows, :] = state.astype(BF16)
    lane = iota((heads, width), 1)
    head = iota((heads, width), 0)
    high, low = two_parts(passing[:, 0:1])
    offsets = pltpu.roll(jnp.minimum(offset[...], count - 1).astype(F32), 2 * slice_heads, 1)
    offsets = jnp.where(
        jnp.logical_and(lane[0:1] >= 2 * slice_heads, lane[0:1] < 2 * slice_heads + count - 1), offsets, 0.0
    )
    at = lane + (member_here() ^ k) * slice_heads
    packed = jnp.where(lane < slice_heads, jnp.where(at == head, high, 0.0), 0.0)
    packed = jnp.where(jnp.logical_and(lane >= slice_heads, at == head + slice_heads), low, packed)
    packed = jnp.where(lane < 2 * slice_heads, packed, 0.0)
    misc = jnp.sum(packed, axis=0, keepdims=True) + offsets
    row = iota((TAIL, width), 0)
    tail = jnp.where(row == 0, misc, jnp.where(row < B_LAST_AT, gates_and_x, b_tail))
    out[rows:, :] = tail.astype(BF16)


def states_kernel(
    x, own, other, own_taps, other_taps, own_bias, other_bias, lags, gated, aux, passing, offset,
    s1, s2, s3, b_out, b_taps, b_tail, turn, ends,
):
    first = holds_b()
    block, state_size = own.shape
    count = own_taps.shape[0]
    channels = x.shape[1]
    last_rows = jnp.concatenate(
        [part[block - TAIL : block, :].astype(F32)[TAIL - 3 :] for part in (x, own, other)], axis=1
    )
    packed = [last_rows[:, at : at + ENDS] for at in range(0, channels + 2 * state_size, ENDS)]
    blank = jnp.zeros((TAIL - 3 * len(packed), ENDS), F32)
    ends[...] = jnp.concatenate(packed + [blank], axis=0).astype(BF16)
    taps = jnp.where(first, own_taps[...], 0.5 * other_taps[...])
    bias = jnp.where(first, own_bias[...], 0.5 * other_bias[...])
    source = jnp.where(first, own[...].astype(F32), other[...].astype(F32))
    before = convolve(source.astype(BF16), taps, bias, [lags[lag] for lag in range(count - 1)])
    value = silu(before)
    b_out[...] = value.astype(BF16)
    turn[...] = value.T.astype(BF16)
    b_taps[...] = jnp.concatenate([taps, bias, jnp.zeros((8 - count - 1, state_size), F32), before[0:8]], axis=0)
    b_tail[...] = jnp.concatenate(
        [jnp.zeros((B_LAST_AT, state_size), F32), source[block - 3 :], source[0:3]], axis=0
    )
    width = gated.shape[1] // (GROUP - 1)
    for slot, (k, out) in enumerate(((1, s1), (2, s2), (3, s3))):
        cols = slice(slot * width, (slot + 1) * width)
        message(out, k, dot(turn[...], gated[:, cols]), passing, offset, count, aux[8:24, cols], b_tail[...])


def rest_kernel(
    x, taps, bias, lags, late_parts, early_parts, passing, offset, turn, b_tail, s0, x_out, aux, gated,
):
    channel_slice(0, 0, x, taps, bias, lags, late_parts, early_parts, x_out, gated, aux)
    state = dot(turn[...], gated[...])
    message(s0, 0, state, passing, offset, taps.shape[0], aux[8:24, :], b_tail[...])


def tail_of(state):
    rows = state.shape[0]
    return state[rows - TAIL : rows, :].astype(F32)


def decay_of(tail):
    width = tail.shape[1]
    slice_heads = width // HEADDIM
    channel = iota((1, width), 1)
    value = jnp.zeros((1, width), F32)
    for head in range(slice_heads):
        both = tail[0:1, head : head + 1] + tail[0:1, slice_heads + head : slice_heads + head + 1]
        value = jnp.where(channel // HEADDIM == head, both, value)
    return value


def pack_decay(decay, tail):
    width = decay.shape[1]
    slice_heads = width // HEADDIM
    lane = iota((1, width), 1)
    high, low = two_parts(decay)
    row = jnp.where(lane >= 2 * slice_heads, tail[0:1], 0.0)
    for head in range(slice_heads):
        at = head * HEADDIM
        row = jnp.where(lane == head, high[:, at : at + 1], row)
        row = jnp.where(lane == slice_heads + head, low[:, at : at + 1], row)
    return row


def tail_taps(x_taps, x_bias, b_taps, count):
    width = x_taps.shape[1]
    upper = iota((TAIL, width), 0) < B_LAST_AT
    taps = [jnp.where(upper, x_taps[k : k + 1], b_taps[k : k + 1]) for k in range(count)]
    return taps, jnp.where(upper, x_bias, b_taps[count : count + 1])


def early_tokens(tail, earlier, taps, bias):
    width = tail.shape[1]
    slice_heads = width // HEADDIM
    count = len(taps)
    row = iota(tail.shape, 0)
    is_last = jnp.logical_or(
        jnp.logical_and(row >= X_LAST_AT, row < X_FIRST_AT),
        jnp.logical_and(row >= B_LAST_AT, row < B_FIRST_AT),
    )
    rows = jnp.where(is_last, earlier, tail)
    offset = jnp.full(tail.shape, -1.0, F32)
    for token in range(count - 1):
        lane = 2 * slice_heads + token
        here = jnp.logical_or(row == X_FIRST_AT + token, row == B_FIRST_AT + token)
        offset = jnp.where(here, tail[0:1, lane : lane + 1], offset)
    total = taps[count - 1] * rows + bias
    for lag in range(1, count):
        total = total + taps[count - 1 - lag] * jnp.where(offset >= lag, pltpu.roll(rows, lag, 0), 0.0)
    value = silu(total).astype(BF16).astype(F32)
    gate = pltpu.roll(tail, B_FIRST_AT - GATE_AT, 0)
    wanted = row >= B_FIRST_AT
    b = jnp.where(wanted, value, 0.0)
    x = jnp.where(wanted, pltpu.roll(value, B_FIRST_AT - X_FIRST_AT, 0) * gate, 0.0)
    return b, x


def group_kernel(r3, r1, r2, r0, earlier, x_taps, x_bias, b_taps, total, *, complete):
    rows = r0.shape[0] - TAIL
    width = r0.shape[1]
    count = x_taps.shape[0]
    held = (r0, r1, r2, r3)

    def run(member):
        cols = slice(member * width, (member + 1) * width)
        taps, bias = tail_taps(x_taps[:, cols], x_bias[:, cols], b_taps[...], count)
        states = [held[member ^ k] for k in range(GROUP)]
        tails = [tail_of(state) for state in states]
        decays = [decay_of(tail) for tail in tails]
        factors = [None] * GROUP
        factor = jnp.ones((1, width), F32)
        for k in reversed(range(GROUP)):
            factors[k] = factor
            factor = factor * decays[k]
        early_b, early_x = [], []
        for k in range(0 if complete else 1, GROUP):
            before = tails[k - 1] if k else tail_of(earlier)
            b, x = early_tokens(tails[k], before, taps, bias)
            early_b.append(b)
            early_x.append(x * factors[k])
        b_rows = jnp.concatenate(early_b, axis=0).astype(BF16)
        added = dot(b_rows, jnp.concatenate(early_x, axis=0).astype(BF16), ((0,), (0,)))
        step = 32
        for top in range(0, rows, step):
            part = slice(top, top + step)
            value = added[part]
            for k in range(GROUP):
                value = value + factors[k] * states[k][part, :].astype(F32)
            total[part, :] = value.astype(BF16)
        row = iota((TAIL, width), 0)
        is_last = jnp.logical_or(
            jnp.logical_and(row >= X_LAST_AT, row < X_FIRST_AT),
            jnp.logical_and(row >= B_LAST_AT, row < B_FIRST_AT),
        )
        gates = jnp.zeros((1, width), F32) if complete else factors[0]
        tail = jnp.where(is_last, tails[GROUP - 1], tails[0])
        tail = jnp.where(row < X_LAST_AT, tail * gates, tail)
        tail = jnp.where(row == 0, pack_decay(factor, tails[0]), tail)
        total[rows:, :] = tail.astype(BF16)

    for member in range(GROUP):
        pl.when(member_here() == member)(lambda member=member: run(member))


def before_kernel(r3, r1, r2, r0, near, x_taps, x_bias, b_taps, partial, factors):
    rows = r0.shape[0] - TAIL
    width = r0.shape[1]
    count = x_taps.shape[0]
    held = (r0, r1, r2, r3)
    one = jnp.ones((1, width), F32)
    from_near = jnp.where(group_here() >= 1, one, 0.0)

    def run(member):
        cols = slice(member * width, (member + 1) * width)
        taps, bias = tail_taps(x_taps[:, cols], x_bias[:, cols], b_taps[...], count)
        states = [held[member ^ k] for k in range(GROUP)]
        tails = [tail_of(state) for state in states]
        near_tail = from_near * tail_of(near)
        decays = [decay_of(tail) for tail in tails]
        added = []
        factor = one
        for k in range(GROUP):
            factors[member ^ k : (member ^ k) + 1, :] = factor
            factor = factor * decays[k]
        factors[GROUP : GROUP + 1, :] = decay_of(near_tail)
        for k in range(GROUP - 1):
            b, x = early_tokens(tails[k], tails[k - 1] if k else near_tail, taps, bias)
            added.append(dot(b.astype(BF16), x.astype(BF16), ((0,), (0,))))
        step = 32
        for top in range(0, rows, step):
            part = slice(top, top + step)
            value = from_near * near[part, :].astype(F32)
            partial[member, part, :] = value
            for k in range(GROUP - 1):
                value = decays[k] * value + states[k][part, :].astype(F32) + added[k][part]
                partial[member ^ (k + 1), part, :] = value

    for member in range(GROUP):
        pl.when(member_here() == member)(lambda member=member: run(member))


def entering_kernel(far, near, partial, factors, x_taps, x_bias, b_taps, e0, e1, e2, e3):
    group = group_here()
    outs = (e0, e1, e2, e3)
    rows, width = e0.shape
    one = jnp.ones((1, width), F32)
    from_far = jnp.where(group >= 2, one, 0.0)
    near_tail = jnp.where(group >= 1, one, 0.0) * tail_of(near)
    far_tail = from_far * tail_of(far)
    cols = quarter(0, width)
    taps, bias = tail_taps(x_taps[:, cols], x_bias[:, cols], b_taps[...], x_taps.shape[0])
    near_decay = factors[GROUP : GROUP + 1, :]
    far_factor = near_decay * from_far
    far_b, far_x = early_tokens(far_tail, jnp.zeros_like(far_tail), taps, bias)
    near_b, near_x = early_tokens(near_tail, far_tail, taps, bias)
    b_rows = jnp.concatenate([far_b, near_b], axis=0).astype(BF16)
    x_rows = jnp.concatenate([far_x * near_decay, near_x], axis=0).astype(BF16)
    added = dot(b_rows, x_rows, ((0,), (0,)))
    step = 32
    for top in range(0, rows, step):
        part = slice(top, top + step)
        value = far_factor * far[part, :].astype(F32) + added[part]
        for k, out in enumerate(outs):
            out[part, :] = (partial[k, part, :] + factors[k : k + 1, :] * value).astype(BF16)


def patched(before, halo, taps, offset_col):
    width = before.shape[1]
    count = taps.shape[0]
    extended = jnp.concatenate([jnp.zeros((5, width), F32), halo, jnp.zeros((8, width), F32)], axis=0)
    total = before
    for lag in range(1, count):
        shifted_rows = extended[8 - lag : 16 - lag]
        total = total + taps[count - 1 - lag : count - lag] * jnp.where(
            offset_col[0:8, 0:1] >= lag, shifted_rows, 0.0
        )
    return silu(total)


def intra_kernel(
    x_early, x_late, aux_early, aux_late, halo, own, other, own_taps, other_taps, own_bias, other_bias, b, b_aux,
    x_taps, step, sums, offset, lags, y, c_out, carry, bias, scores, columns, x_full, b_full, aux,
):
    first = holds_b()
    block, channels = x_full.shape
    heads = step.shape[0]
    state_size = b.shape[1]
    width = channels // GROUP
    for k, (part, rows, slot) in enumerate(
        ((x_late, aux_late, 0), (x_early, aux_early, 0), (x_early, aux_early, 1), (x_early, aux_early, 2))
    ):
        source = slice(slot * width, (slot + 1) * width)
        x_full[:, quarter(k, width)] = part[:, source]
        aux[:, quarter(k, width)] = rows[0:16, source]
    count = x_taps.shape[0]
    half = block // 2
    time_step, rate_sum = step[...], sums[...]
    columns[...] = rate_sum.T
    offset_col = offset_columns(offset[...])

    packed = halo[...].astype(F32)
    last_rows = jnp.concatenate(
        [packed[3 * k : 3 * k + 3] for k in range((channels + 2 * state_size) // ENDS)], axis=1
    )
    early = patched(aux[0:8, :], last_rows[:, 0:channels], x_taps[...], offset_col)
    x_full[0:16, :] = jnp.concatenate([early, x_full[0:16, :].astype(F32)[8:16]], axis=0).astype(BF16)
    own_halo = last_rows[:, channels : channels + state_size]
    other_halo = last_rows[:, channels + state_size :]
    b_full[...] = b[...]
    early = patched(b_aux[8:16, :], jnp.where(first, own_halo, other_halo), b_aux[0:count, :], offset_col)
    b_full[0:16, :] = jnp.concatenate([early, b[0:16, :].astype(F32)[8:16]], axis=0).astype(BF16)
    c_taps = jnp.where(first, 0.5 * other_taps[...], own_taps[...])
    c_bias = jnp.where(first, 0.5 * other_bias[...], own_bias[...])
    c_source = jnp.where(first, other[...].astype(F32), own[...].astype(F32)).astype(BF16)
    before = convolve(c_source, c_taps, c_bias, [lags[lag] for lag in range(count - 1)])
    c_value = silu(before)
    early = patched(before[0:8], jnp.where(first, other_halo, own_halo), c_taps, offset_col)
    c_out[...] = c_value.astype(BF16)
    c_out[0:16, :] = jnp.concatenate([early, c_value[8:16]], axis=0).astype(BF16)

    row = iota((block, LANES), 0)
    for left in range(0, block, LANES):
        gap = row - (iota((block, LANES), 1) + left)
        linked = jnp.logical_and(gap >= 0, offset_col >= gap.astype(F32))
        bias[:, left : left + LANES] = jnp.where(linked, 0.0, NEG)
    scores[...] = dot(c_out[...], b_full[...], ((1,), (1,)))
    reach = rate_sum - jnp.log(time_step)
    starts = iota(rate_sum.shape, 1) + 1
    factor = turned(jnp.where(offset[...] >= starts, jnp.exp(rate_sum), 0.0))
    for k in range(GROUP):
        carry[:, k * width : (k + 1) * width] = spread(factor, k * width, width)
    lane = iota((1, LANES), 1)
    per_tile = LANES // HEADDIM
    for tile in range(heads // per_tile):
        cols = slice(tile * LANES, (tile + 1) * LANES)
        skip_row = aux[8:9, cols]
        for top in range(0, block, half):
            part = slice(top, top + half)
            seen = top + half
            value = skip_row * x_full[part, cols].astype(F32)
            for k in range(per_tile):
                h = tile * per_tile + k
                gap = columns[part, h : h + 1] - reach[h : h + 1, 0:seen] + bias[part, 0:seen]
                weights = (scores[part, 0:seen] * jnp.exp(gap)).astype(BF16)
                chosen = jnp.where(lane // HEADDIM == k, x_full[0:seen, cols], jnp.zeros((), BF16))
                value = value + dot(weights, chosen)
            y[part, cols] = value


def back_kernel(c, *refs, members):
    *parts, intra, carry, out, held, sems = refs
    width = out.shape[1] // GROUP
    copies = []
    for slot, (k, state) in enumerate(zip(members, parts)):
        cols = quarter(k, width)
        held[slot] = (intra[:, cols] + carry[:, cols] * dot(c[...], state[...])).astype(BF16)
        copies.append(pltpu.make_async_copy(held.at[slot], out.at[:, cols], sems.at[slot]))
        copies[-1].start()
    for copy in copies:
        copy.wait()


def exchange(array, mask):
    return lax.ppermute(array, "seq", [(i, i ^ mask) for i in range(lax.axis_size("seq"))])


def turned_on(array, distance):
    count = lax.axis_size("seq")
    return lax.ppermute(array, "seq", [(i, (i + distance) % count) for i in range(count)])


def shifted(array, distance):
    count = lax.axis_size("seq")
    return lax.ppermute(array, "seq", [(i, i + distance) for i in range(count - distance)])


def scan_groups(total, groups):
    rows = total.shape[0] - TAIL
    last = shifted(total[rows:], GROUP)
    held, decay = total[:rows].astype(F32), decay_of(total[rows:].astype(F32))
    held = shifted(held, GROUP)
    decay = shifted(decay, GROUP)
    distance = 1
    while distance < groups:
        held = held + decay * shifted(held, GROUP * distance)
        decay = decay * shifted(decay, GROUP * distance)
        distance *= 2
    near_tail = jnp.concatenate([jnp.zeros((X_LAST_AT, last.shape[1]), BF16), last[X_LAST_AT:]], axis=0)
    near = jnp.concatenate([held.astype(BF16), near_tail], axis=0)
    return near, jnp.zeros_like(near)


def on_device(
    ssm_input, bc_input, conv_taps, conv_bias, bc_taps, bc_bias,
    step_input, step_bias, decay_log, skip_gain, request_offset,
):
    block, channels = ssm_input.shape
    state_size = bc_input.shape[1]
    heads = step_input.shape[0]
    width = channels // GROUP
    groups = lax.axis_size("seq") // GROUP
    here = lax.axis_index("seq")
    hbm = pl.BlockSpec(memory_space=pltpu.HBM)
    vmem = pl.BlockSpec(memory_space=pltpu.VMEM)

    swap = [(i, i ^ 1) for i in range(lax.axis_size("head"))]
    other_bc, other_taps, other_bias = [lax.ppermute(part, "head", swap) for part in (bc_input, bc_taps, bc_bias)]
    other_bias = other_bias[None, :]

    others = jax.ShapeDtypeStruct((block, (GROUP - 1) * width), BF16)
    slice_shape = jax.ShapeDtypeStruct((state_size + TAIL, width), BF16)
    (
        x_early, gated, aux_early, passing, time_step, rate_sum, x, x_taps, x_bias, own, own_taps, own_bias, offset,
        lags, late_parts, early_parts,
    ) = pl.pallas_call(
        channels_kernel,
        out_shape=[
            others,
            others,
            jax.ShapeDtypeStruct((24, (GROUP - 1) * width), F32),
            jax.ShapeDtypeStruct((heads, LANES), F32),
            jax.ShapeDtypeStruct((heads, block), F32),
            jax.ShapeDtypeStruct((heads, block), F32),
            jax.ShapeDtypeStruct((block, channels), BF16),
            jax.ShapeDtypeStruct(conv_taps.shape, F32),
            jax.ShapeDtypeStruct((1, channels), F32),
            jax.ShapeDtypeStruct(bc_input.shape, BF16),
            jax.ShapeDtypeStruct(bc_taps.shape, F32),
            jax.ShapeDtypeStruct((1, state_size), F32),
            jax.ShapeDtypeStruct((1, block), jnp.int32),
            jax.ShapeDtypeStruct((conv_taps.shape[0] - 1, block, block), BF16),
            jax.ShapeDtypeStruct((block, 2 * heads), BF16),
            jax.ShapeDtypeStruct((TAIL, 2 * heads), BF16),
        ],
        in_specs=[hbm] * 11,
        out_specs=[vmem] * 16,
        scratch_shapes=[
            pltpu.VMEM((heads, block), F32),
            pltpu.VMEM((1, heads), F32),
            pltpu.VMEM((1, heads), F32),
            pltpu.VMEM((1, heads), F32),
            pltpu.SemaphoreType.DMA((11,)),
        ],
        compiler_params=PARAMS,
        name="channels",
    )(
        *[
            pltpu.with_memory_space_constraint(array, pltpu.HBM)
            for array in (
                ssm_input, conv_taps, conv_bias[None, :], bc_input, bc_taps, bc_bias[None, :], step_input,
                request_offset[None, :], step_bias[None, :], decay_log[None, :], skip_gain[None, :],
            )
        ]
    )
    s1, s2, s3, b_main, b_aux, b_tail, turn, ends = pl.pallas_call(
        states_kernel,
        out_shape=[
            slice_shape,
            slice_shape,
            slice_shape,
            jax.ShapeDtypeStruct((block, state_size), BF16),
            jax.ShapeDtypeStruct((16, state_size), F32),
            jax.ShapeDtypeStruct((TAIL, state_size), F32),
            jax.ShapeDtypeStruct((state_size, block), BF16),
            jax.ShapeDtypeStruct((TAIL, ENDS), BF16),
        ],
        in_specs=[vmem] * 12,
        out_specs=[vmem] * 8,
        compiler_params=PARAMS,
        name="states",
    )(x, own, other_bc, own_taps, other_taps, own_bias, other_bias, lags, gated, aux_early, passing, offset)
    r1, r2, r3 = exchange(s1, 1), exchange(s2, 2), exchange(s3, 3)
    halo = shifted(ends, 1)
    s0, x_late, aux_late = pl.pallas_call(
        rest_kernel,
        out_shape=[
            slice_shape,
            jax.ShapeDtypeStruct((block, width), BF16),
            jax.ShapeDtypeStruct((24, width), F32),
        ],
        in_specs=[vmem] * 10,
        out_specs=[vmem] * 3,
        scratch_shapes=[pltpu.VMEM((block, width), BF16)],
        compiler_params=PARAMS,
        cost_estimate=pl.CostEstimate(flops=400_000_000, bytes_accessed=2_000_000, transcendentals=200_000),
        name="rest",
    )(x, x_taps, x_bias, lags, late_parts, early_parts, passing, offset, turn, b_tail)
    received = [s0, r1, r2, r3]

    direct = groups == GROUP
    if direct:
        earlier = jnp.zeros((TAIL, width), BF16)
    else:
        last = received[0]
        for k in (1, 2, 3):
            last = jnp.where((here % GROUP) ^ k == GROUP - 1, received[k], last)
        earlier = shifted(last[state_size:], GROUP)
    total = pl.pallas_call(
        lambda *refs: group_kernel(*refs, complete=not direct),
        out_shape=slice_shape,
        in_specs=[vmem] * (GROUP + 4),
        out_specs=vmem,
        compiler_params=PARAMS,
        name="group",
    )(r3, r1, r2, s0, earlier, x_taps, x_bias, b_aux)
    total, halo = lax.optimization_barrier((total, halo))
    if direct:
        far = shifted(total, 2 * GROUP)
        near = turned_on(total, GROUP)
    else:
        near, far = scan_groups(total, groups)

    partial, factors = pl.pallas_call(
        before_kernel,
        out_shape=[
            jax.ShapeDtypeStruct((GROUP, state_size, width), F32),
            jax.ShapeDtypeStruct((8, width), F32),
        ],
        in_specs=[vmem] * (GROUP + 4),
        out_specs=[vmem] * 2,
        compiler_params=PARAMS,
        cost_estimate=pl.CostEstimate(flops=100_000_000, bytes_accessed=2_000_000, transcendentals=10_000),
        name="before",
    )(r3, r1, r2, s0, near, x_taps, x_bias, b_aux)
    entering = pl.pallas_call(
        entering_kernel,
        out_shape=[jax.ShapeDtypeStruct((state_size, width), BF16)] * GROUP,
        in_specs=[vmem] * 7,
        out_specs=[vmem] * GROUP,
        compiler_params=PARAMS,
        name="entering",
    )(far, near, partial, factors, x_taps, x_bias, b_aux)
    mine = [entering[0]] + [exchange(entering[k], k) for k in (1, 2, 3)]

    intra, c_conv, carry = pl.pallas_call(
        intra_kernel,
        out_shape=[
            jax.ShapeDtypeStruct((block, channels), F32),
            jax.ShapeDtypeStruct((block, state_size), BF16),
            jax.ShapeDtypeStruct((block, channels), F32),
        ],
        in_specs=[vmem] * 18,
        out_specs=[vmem] * 3,
        scratch_shapes=[
            pltpu.VMEM((block, block), F32),
            pltpu.VMEM((block, block), F32),
            pltpu.VMEM((block, heads), F32),
            pltpu.VMEM((block, channels), BF16),
            pltpu.VMEM((block, state_size), BF16),
            pltpu.VMEM((16, channels), F32),
        ],
        compiler_params=PARAMS,
        cost_estimate=pl.CostEstimate(flops=600_000_000, bytes_accessed=4_000_000, transcendentals=1_000_000),
        name="intra",
    )(
        x_early, x_late, aux_early, aux_late, halo, own, other_bc, own_taps, other_taps, own_bias, other_bias,
        b_main, b_aux, x_taps, time_step, rate_sum, offset, lags,
    )
    out_shape = jax.ShapeDtypeStruct((block, channels), BF16)
    early, late = (0, 3), (1, 2)
    begun = pl.pallas_call(
        lambda *refs: back_kernel(*refs, members=early),
        out_shape=out_shape,
        in_specs=[vmem] * (len(early) + 3),
        out_specs=hbm,
        scratch_shapes=[pltpu.VMEM((len(early), block, width), BF16), pltpu.SemaphoreType.DMA((len(early),))],
        compiler_params=PARAMS,
        name="begin",
    )(c_conv, *[mine[k] for k in early], intra, carry)

    def last_kernel(c, f1, f2, intra, carry, begun, out, held, sems):
        back_kernel(c, f1, f2, intra, carry, out, held, sems, members=late)

    return pl.pallas_call(
        last_kernel,
        out_shape=out_shape,
        in_specs=[vmem] * (len(late) + 3) + [hbm],
        out_specs=hbm,
        scratch_shapes=[pltpu.VMEM((len(late), block, width), BF16), pltpu.SemaphoreType.DMA((len(late),))],
        input_output_aliases={len(late) + 3: 0},
        compiler_params=PARAMS,
        name="back",
    )(c_conv, *[mine[k] for k in late], intra, carry, begun)


def solution(mesh):
    return jax.shard_map(
        on_device,
        mesh=mesh,
        in_specs=(
            P("seq", "head"),
            P("seq", "head"),
            P(None, "head"),
            P("head"),
            P(None, "head"),
            P("head"),
            P("head", "seq"),
            P("head"),
            P("head"),
            P("head"),
            P("seq"),
        ),
        out_specs=P("seq", "head"),
        check_vma=False,
    )
```

```python
import jax
import jax.numpy as jnp
from jax import lax
from jax.experimental import pallas as pl
from jax.experimental.pallas import tpu as pltpu
from jax.sharding import PartitionSpec as P

HEADDIM = 64
GROUP = 4
TAIL = 16
GATE_AT, X_LAST_AT, X_FIRST_AT, B_LAST_AT, B_FIRST_AT = 1, 4, 7, 10, 13
ENDS = 512
LANES = 128
NEG = -1e30
F32 = jnp.float32
BF16 = jnp.bfloat16
PARAMS = pltpu.CompilerParams(vmem_limit_bytes=24 * 1024 * 1024)


def dot(a, b, dims=((1,), (0,))):
    return lax.dot_general(a, b, (dims, ((), ())), preferred_element_type=F32)


def two_parts(value):
    high = value.astype(BF16).astype(F32)
    return high, value - high


def silu(half):
    return half + half * jnp.tanh(half)


def iota(shape, dim):
    return lax.broadcasted_iota(jnp.int32, shape, dim)


def member_here():
    return lax.axis_index("seq") % GROUP


def group_here():
    return lax.axis_index("seq") // GROUP


def holds_b():
    return lax.axis_index("head") % 2 == 0


def column(row):
    shape = (row.shape[1], row.shape[1])
    wide = jnp.broadcast_to(row, shape)
    return jnp.sum(jnp.where(iota(shape, 0) == iota(shape, 1), wide, 0.0), axis=1, keepdims=True)


def spread(parts, first_channel, width):
    heads = parts.shape[1] // 2
    shape = (2 * heads, width)
    head = iota(shape, 0) & (heads - 1)
    channel = iota(shape, 1) + first_channel
    return dot(parts, (channel // HEADDIM == head).astype(F32).astype(BF16))


def turned(per_head):
    high, low = two_parts(per_head)
    return jnp.concatenate([high, low], axis=0).T.astype(BF16)


def rates(step, step_bias, decay_log):
    heads, block = step.shape
    time_step = jax.nn.softplus(step + step_bias)
    log_decay = -jnp.exp(decay_log) * time_step
    shape = (block, block)
    upto = (iota(shape, 0) <= iota(shape, 1)).astype(F32).astype(BF16)
    first, rest = two_parts(log_decay)
    second, third = two_parts(rest)
    sums = dot(jnp.concatenate([first, second, third], axis=0).astype(BF16), upto)
    return time_step, sums[0:heads] + (sums[heads : 2 * heads] + sums[2 * heads :])


def offset_columns(offset_row):
    wide = jnp.broadcast_to(offset_row.astype(F32), (LANES, offset_row.shape[1]))
    return wide.T


def lag_matrices(offset_col, count):
    block = offset_col.shape[0]
    gap = iota((block, block), 0) - iota((block, block), 1)
    offset_wide = jnp.concatenate([offset_col] * (block // LANES), axis=1)
    return [
        jnp.where(jnp.logical_and(gap == lag, offset_wide >= lag), 1.0, 0.0).astype(BF16)
        for lag in range(1, count)
    ]


def convolve(source, taps, bias, lags):
    count = len(lags) + 1
    total = taps[count - 1 : count] * source.astype(F32) + bias
    for lag, matrix in enumerate(lags, 1):
        total = total + taps[count - 1 - lag : count - lag] * dot(matrix, source)
    return total


def quarter(k, width):
    return pl.ds(pl.multiple_of((member_here() ^ k) * width, width), width)


def channel_slice(k, slot, x, taps, bias, lags, late_parts, early_parts, x_out, gated, aux):
    block = x.shape[0]
    width = x.shape[1] // GROUP
    cols, to = quarter(k, width), slice(slot * width, (slot + 1) * width)
    source = x[:, cols]
    before = convolve(source, taps[:, cols], bias[:, cols], [lags[lag] for lag in range(lags.shape[0])])
    value = silu(before).astype(BF16)
    x_out[:, to] = value
    first_channel = (member_here() ^ k) * width
    gated[:, to] = (value.astype(F32) * spread(late_parts[...], first_channel, width)).astype(BF16)
    aux[0:8, to] = before[0:8]
    early = spread(early_parts[...], first_channel, width)
    first = source[0:TAIL].astype(F32)
    last_rows = source[block - TAIL : block].astype(F32)
    aux[8:24, to] = jnp.concatenate(
        [early[3:4], early[0:3], last_rows[TAIL - 3 :], first[0:3], jnp.zeros((TAIL - 10, width), F32)], axis=0
    )


def channels_kernel(
    x_hbm, taps_hbm, bias_hbm, own_hbm, own_taps_hbm, own_bias_hbm, step_hbm, offset_hbm,
    step_bias_hbm, decay_hbm, skip_hbm,
    x_out, gated, aux, passing_out, step_out, sums_out, x, taps, bias, own, own_taps, own_bias, offset,
    lags, late_parts, early_parts, step, step_bias, decay_log, skip, sems,
):
    block = x.shape[0]
    count = taps.shape[0]
    pairs = [
        (offset_hbm, offset), (step_hbm, step), (step_bias_hbm, step_bias), (decay_hbm, decay_log),
        (x_hbm, x), (taps_hbm, taps), (bias_hbm, bias), (skip_hbm, skip), (own_taps_hbm, own_taps),
        (own_bias_hbm, own_bias), (own_hbm, own),
    ]
    copies = [pltpu.make_async_copy(*pair, sems.at[k]) for k, pair in enumerate(pairs)]
    for copy in copies:
        copy.start()
    copies[0].wait()
    for lag, matrix in enumerate(lag_matrices(offset_columns(offset[...]), count)):
        lags[lag] = matrix
    for copy in copies[1:4]:
        copy.wait()
    time_step, rate_sum = rates(step[...], column(step_bias[...]), column(decay_log[...]))
    step_out[...] = time_step
    sums_out[...] = rate_sum
    last_offset = offset[0, block - 1]
    place = iota(rate_sum.shape, 1)
    last = rate_sum[:, block - 1 : block]
    gate = jnp.exp(jnp.where(last_offset >= block - 1 - place, last - rate_sum, NEG)) * time_step
    passing = jnp.exp(last) * (last_offset >= block).astype(F32)
    passing_out[...] = jnp.broadcast_to(passing, passing_out.shape)
    for copy in copies[4:8]:
        copy.wait()
    taps[...] = 0.5 * taps[...]
    bias[...] = 0.5 * bias[...]
    early_parts[...] = turned(jnp.where(place == count - 1, column(skip[...]), gate))[0:TAIL]
    late_parts[...] = turned(jnp.where(place >= count - 1, gate, 0.0))
    for slot, k in enumerate((1, 2, 3)):
        channel_slice(k, slot, x, taps, bias, lags, late_parts, early_parts, x_out, gated, aux)
    for copy in copies[8:]:
        copy.wait()
    own_taps[...] = 0.5 * own_taps[...]
    own_bias[...] = 0.5 * own_bias[...]


def message(out, k, state, passing, offset, count, gates_and_x, b_tail):
    rows, width = state.shape
    heads = passing.shape[0]
    slice_heads = heads // GROUP
    out[0:rows, :] = state.astype(BF16)
    lane = iota((heads, width), 1)
    head = iota((heads, width), 0)
    high, low = two_parts(passing[:, 0:1])
    offsets = pltpu.roll(jnp.minimum(offset[...], count - 1).astype(F32), 2 * slice_heads, 1)
    offsets = jnp.where(
        jnp.logical_and(lane[0:1] >= 2 * slice_heads, lane[0:1] < 2 * slice_heads + count - 1), offsets, 0.0
    )
    at = lane + (member_here() ^ k) * slice_heads
    packed = jnp.where(lane < slice_heads, jnp.where(at == head, high, 0.0), 0.0)
    packed = jnp.where(jnp.logical_and(lane >= slice_heads, at == head + slice_heads), low, packed)
    packed = jnp.where(lane < 2 * slice_heads, packed, 0.0)
    misc = jnp.sum(packed, axis=0, keepdims=True) + offsets
    row = iota((TAIL, width), 0)
    tail = jnp.where(row == 0, misc, jnp.where(row < B_LAST_AT, gates_and_x, b_tail))
    out[rows:, :] = tail.astype(BF16)


def states_kernel(
    x, own, other, own_taps, other_taps, own_bias, other_bias, lags, gated, aux, passing, offset,
    s1, s2, s3, b_out, b_taps, b_tail, turn, ends,
):
    first = holds_b()
    block, state_size = own.shape
    count = own_taps.shape[0]
    channels = x.shape[1]
    last_rows = jnp.concatenate(
        [part[block - TAIL : block, :].astype(F32)[TAIL - 3 :] for part in (x, own, other)], axis=1
    )
    packed = [last_rows[:, at : at + ENDS] for at in range(0, channels + 2 * state_size, ENDS)]
    blank = jnp.zeros((TAIL - 3 * len(packed), ENDS), F32)
    ends[...] = jnp.concatenate(packed + [blank], axis=0).astype(BF16)
    taps = jnp.where(first, own_taps[...], 0.5 * other_taps[...])
    bias = jnp.where(first, own_bias[...], 0.5 * other_bias[...])
    source = jnp.where(first, own[...].astype(F32), other[...].astype(F32))
    before = convolve(source.astype(BF16), taps, bias, [lags[lag] for lag in range(count - 1)])
    value = silu(before)
    b_out[...] = value.astype(BF16)
    turn[...] = value.T.astype(BF16)
    b_taps[...] = jnp.concatenate([taps, bias, jnp.zeros((8 - count - 1, state_size), F32), before[0:8]], axis=0)
    b_tail[...] = jnp.concatenate(
        [jnp.zeros((B_LAST_AT, state_size), F32), source[block - 3 :], source[0:3]], axis=0
    )
    width = gated.shape[1] // (GROUP - 1)
    for slot, (k, out) in enumerate(((1, s1), (2, s2), (3, s3))):
        cols = slice(slot * width, (slot + 1) * width)
        message(out, k, dot(turn[...], gated[:, cols]), passing, offset, count, aux[8:24, cols], b_tail[...])


def rest_kernel(
    x, taps, bias, lags, late_parts, early_parts, passing, offset, turn, b_tail, s0, x_out, aux, gated,
):
    channel_slice(0, 0, x, taps, bias, lags, late_parts, early_parts, x_out, gated, aux)
    state = dot(turn[...], gated[...])
    message(s0, 0, state, passing, offset, taps.shape[0], aux[8:24, :], b_tail[...])


def tail_of(state):
    rows = state.shape[0]
    return state[rows - TAIL : rows, :].astype(F32)


def decay_of(tail):
    width = tail.shape[1]
    slice_heads = width // HEADDIM
    channel = iota((1, width), 1)
    value = jnp.zeros((1, width), F32)
    for head in range(slice_heads):
        both = tail[0:1, head : head + 1] + tail[0:1, slice_heads + head : slice_heads + head + 1]
        value = jnp.where(channel // HEADDIM == head, both, value)
    return value


def pack_decay(decay, tail):
    width = decay.shape[1]
    slice_heads = width // HEADDIM
    lane = iota((1, width), 1)
    high, low = two_parts(decay)
    row = jnp.where(lane >= 2 * slice_heads, tail[0:1], 0.0)
    for head in range(slice_heads):
        at = head * HEADDIM
        row = jnp.where(lane == head, high[:, at : at + 1], row)
        row = jnp.where(lane == slice_heads + head, low[:, at : at + 1], row)
    return row


def tail_taps(x_taps, x_bias, b_taps, count):
    width = x_taps.shape[1]
    upper = iota((TAIL, width), 0) < B_LAST_AT
    taps = [jnp.where(upper, x_taps[k : k + 1], b_taps[k : k + 1]) for k in range(count)]
    return taps, jnp.where(upper, x_bias, b_taps[count : count + 1])


def early_tokens(tail, earlier, taps, bias):
    width = tail.shape[1]
    slice_heads = width // HEADDIM
    count = len(taps)
    row = iota(tail.shape, 0)
    is_last = jnp.logical_or(
        jnp.logical_and(row >= X_LAST_AT, row < X_FIRST_AT),
        jnp.logical_and(row >= B_LAST_AT, row < B_FIRST_AT),
    )
    rows = jnp.where(is_last, earlier, tail)
    offset = jnp.full(tail.shape, -1.0, F32)
    for token in range(count - 1):
        lane = 2 * slice_heads + token
        here = jnp.logical_or(row == X_FIRST_AT + token, row == B_FIRST_AT + token)
        offset = jnp.where(here, tail[0:1, lane : lane + 1], offset)
    total = taps[count - 1] * rows + bias
    for lag in range(1, count):
        total = total + taps[count - 1 - lag] * jnp.where(offset >= lag, pltpu.roll(rows, lag, 0), 0.0)
    value = silu(total).astype(BF16).astype(F32)
    gate = pltpu.roll(tail, B_FIRST_AT - GATE_AT, 0)
    wanted = row >= B_FIRST_AT
    b = jnp.where(wanted, value, 0.0)
    x = jnp.where(wanted, pltpu.roll(value, B_FIRST_AT - X_FIRST_AT, 0) * gate, 0.0)
    return b, x


def group_kernel(r3, r1, r2, r0, earlier, x_taps, x_bias, b_taps, total, *, complete):
    rows = r0.shape[0] - TAIL
    width = r0.shape[1]
    count = x_taps.shape[0]
    held = (r0, r1, r2, r3)

    def run(member):
        cols = slice(member * width, (member + 1) * width)
        taps, bias = tail_taps(x_taps[:, cols], x_bias[:, cols], b_taps[...], count)
        states = [held[member ^ k] for k in range(GROUP)]
        tails = [tail_of(state) for state in states]
        decays = [decay_of(tail) for tail in tails]
        factors = [None] * GROUP
        factor = jnp.ones((1, width), F32)
        for k in reversed(range(GROUP)):
            factors[k] = factor
            factor = factor * decays[k]
        early_b, early_x = [], []
        for k in range(0 if complete else 1, GROUP):
            before = tails[k - 1] if k else tail_of(earlier)
            b, x = early_tokens(tails[k], before, taps, bias)
            early_b.append(b)
            early_x.append(x * factors[k])
        b_rows = jnp.concatenate(early_b, axis=0).astype(BF16)
        added = dot(b_rows, jnp.concatenate(early_x, axis=0).astype(BF16), ((0,), (0,)))
        step = 32
        for top in range(0, rows, step):
            part = slice(top, top + step)
            value = added[part]
            for k in range(GROUP):
                value = value + factors[k] * states[k][part, :].astype(F32)
            total[part, :] = value.astype(BF16)
        row = iota((TAIL, width), 0)
        is_last = jnp.logical_or(
            jnp.logical_and(row >= X_LAST_AT, row < X_FIRST_AT),
            jnp.logical_and(row >= B_LAST_AT, row < B_FIRST_AT),
        )
        gates = jnp.zeros((1, width), F32) if complete else factors[0]
        tail = jnp.where(is_last, tails[GROUP - 1], tails[0])
        tail = jnp.where(row < X_LAST_AT, tail * gates, tail)
        tail = jnp.where(row == 0, pack_decay(factor, tails[0]), tail)
        total[rows:, :] = tail.astype(BF16)

    for member in range(GROUP):
        pl.when(member_here() == member)(lambda member=member: run(member))


def before_kernel(r3, r1, r2, r0, near, x_taps, x_bias, b_taps, partial, factors):
    rows = r0.shape[0] - TAIL
    width = r0.shape[1]
    count = x_taps.shape[0]
    held = (r0, r1, r2, r3)
    one = jnp.ones((1, width), F32)
    from_near = jnp.where(group_here() >= 1, one, 0.0)

    def run(member):
        cols = slice(member * width, (member + 1) * width)
        taps, bias = tail_taps(x_taps[:, cols], x_bias[:, cols], b_taps[...], count)
        states = [held[member ^ k] for k in range(GROUP)]
        tails = [tail_of(state) for state in states]
        near_tail = from_near * tail_of(near)
        decays = [decay_of(tail) for tail in tails]
        added = []
        factor = one
        for k in range(GROUP):
            factors[member ^ k : (member ^ k) + 1, :] = factor
            factor = factor * decays[k]
        factors[GROUP : GROUP + 1, :] = decay_of(near_tail)
        for k in range(GROUP - 1):
            b, x = early_tokens(tails[k], tails[k - 1] if k else near_tail, taps, bias)
            added.append(dot(b.astype(BF16), x.astype(BF16), ((0,), (0,))))
        step = 32
        for top in range(0, rows, step):
            part = slice(top, top + step)
            value = from_near * near[part, :].astype(F32)
            partial[member, part, :] = value
            for k in range(GROUP - 1):
                value = decays[k] * value + states[k][part, :].astype(F32) + added[k][part]
                partial[member ^ (k + 1), part, :] = value

    for member in range(GROUP):
        pl.when(member_here() == member)(lambda member=member: run(member))


def entering_kernel(far, near, partial, factors, x_taps, x_bias, b_taps, e0, e1, e2, e3):
    group = group_here()
    outs = (e0, e1, e2, e3)
    rows, width = e0.shape
    one = jnp.ones((1, width), F32)
    from_far = jnp.where(group >= 2, one, 0.0)
    near_tail = jnp.where(group >= 1, one, 0.0) * tail_of(near)
    far_tail = from_far * tail_of(far)
    cols = quarter(0, width)
    taps, bias = tail_taps(x_taps[:, cols], x_bias[:, cols], b_taps[...], x_taps.shape[0])
    near_decay = factors[GROUP : GROUP + 1, :]
    far_factor = near_decay * from_far
    far_b, far_x = early_tokens(far_tail, jnp.zeros_like(far_tail), taps, bias)
    near_b, near_x = early_tokens(near_tail, far_tail, taps, bias)
    b_rows = jnp.concatenate([far_b, near_b], axis=0).astype(BF16)
    x_rows = jnp.concatenate([far_x * near_decay, near_x], axis=0).astype(BF16)
    added = dot(b_rows, x_rows, ((0,), (0,)))
    step = 32
    for top in range(0, rows, step):
        part = slice(top, top + step)
        value = far_factor * far[part, :].astype(F32) + added[part]
        for k, out in enumerate(outs):
            out[part, :] = (partial[k, part, :] + factors[k : k + 1, :] * value).astype(BF16)


def patched(before, halo, taps, offset_col):
    width = before.shape[1]
    count = taps.shape[0]
    extended = jnp.concatenate([jnp.zeros((5, width), F32), halo, jnp.zeros((8, width), F32)], axis=0)
    total = before
    for lag in range(1, count):
        shifted_rows = extended[8 - lag : 16 - lag]
        total = total + taps[count - 1 - lag : count - lag] * jnp.where(
            offset_col[0:8, 0:1] >= lag, shifted_rows, 0.0
        )
    return silu(total)


def intra_kernel(
    x_early, x_late, aux_early, aux_late, halo, own, other, own_taps, other_taps, own_bias, other_bias, b, b_aux,
    x_taps, step, sums, offset, lags, y, c_out, carry, bias, scores, columns, x_full, b_full, aux,
):
    first = holds_b()
    block, channels = x_full.shape
    heads = step.shape[0]
    state_size = b.shape[1]
    width = channels // GROUP
    for k, (part, rows, slot) in enumerate(
        ((x_late, aux_late, 0), (x_early, aux_early, 0), (x_early, aux_early, 1), (x_early, aux_early, 2))
    ):
        source = slice(slot * width, (slot + 1) * width)
        x_full[:, quarter(k, width)] = part[:, source]
        aux[:, quarter(k, width)] = rows[0:16, source]
    count = x_taps.shape[0]
    half = block // 2
    time_step, rate_sum = step[...], sums[...]
    columns[...] = rate_sum.T
    offset_col = offset_columns(offset[...])

    packed = halo[...].astype(F32)
    last_rows = jnp.concatenate(
        [packed[3 * k : 3 * k + 3] for k in range((channels + 2 * state_size) // ENDS)], axis=1
    )
    early = patched(aux[0:8, :], last_rows[:, 0:channels], x_taps[...], offset_col)
    x_full[0:16, :] = jnp.concatenate([early, x_full[0:16, :].astype(F32)[8:16]], axis=0).astype(BF16)
    own_halo = last_rows[:, channels : channels + state_size]
    other_halo = last_rows[:, channels + state_size :]
    b_full[...] = b[...]
    early = patched(b_aux[8:16, :], jnp.where(first, own_halo, other_halo), b_aux[0:count, :], offset_col)
    b_full[0:16, :] = jnp.concatenate([early, b[0:16, :].astype(F32)[8:16]], axis=0).astype(BF16)
    c_taps = jnp.where(first, 0.5 * other_taps[...], own_taps[...])
    c_bias = jnp.where(first, 0.5 * other_bias[...], own_bias[...])
    c_source = jnp.where(first, other[...].astype(F32), own[...].astype(F32)).astype(BF16)
    before = convolve(c_source, c_taps, c_bias, [lags[lag] for lag in range(count - 1)])
    c_value = silu(before)
    early = patched(before[0:8], jnp.where(first, other_halo, own_halo), c_taps, offset_col)
    c_out[...] = c_value.astype(BF16)
    c_out[0:16, :] = jnp.concatenate([early, c_value[8:16]], axis=0).astype(BF16)

    row = iota((block, LANES), 0)
    for left in range(0, block, LANES):
        gap = row - (iota((block, LANES), 1) + left)
        linked = jnp.logical_and(gap >= 0, offset_col >= gap.astype(F32))
        bias[:, left : left + LANES] = jnp.where(linked, 0.0, NEG)
    scores[...] = dot(c_out[...], b_full[...], ((1,), (1,)))
    reach = rate_sum - jnp.log(time_step)
    starts = iota(rate_sum.shape, 1) + 1
    factor = turned(jnp.where(offset[...] >= starts, jnp.exp(rate_sum), 0.0))
    for k in range(GROUP):
        carry[:, k * width : (k + 1) * width] = spread(factor, k * width, width)
    lane = iota((1, LANES), 1)
    per_tile = LANES // HEADDIM
    for tile in range(heads // per_tile):
        cols = slice(tile * LANES, (tile + 1) * LANES)
        skip_row = aux[8:9, cols]
        for top in range(0, block, half):
            part = slice(top, top + half)
            seen = top + half
            value = skip_row * x_full[part, cols].astype(F32)
            for k in range(per_tile):
                h = tile * per_tile + k
                gap = columns[part, h : h + 1] - reach[h : h + 1, 0:seen] + bias[part, 0:seen]
                weights = (scores[part, 0:seen] * jnp.exp(gap)).astype(BF16)
                chosen = jnp.where(lane // HEADDIM == k, x_full[0:seen, cols], jnp.zeros((), BF16))
                value = value + dot(weights, chosen)
            y[part, cols] = value


def back_kernel(c, *refs, members):
    *parts, intra, carry, out, held, sems = refs
    width = out.shape[1] // GROUP
    copies = []
    for slot, (k, state) in enumerate(zip(members, parts)):
        cols = quarter(k, width)
        held[slot] = (intra[:, cols] + carry[:, cols] * dot(c[...], state[...])).astype(BF16)
        copies.append(pltpu.make_async_copy(held.at[slot], out.at[:, cols], sems.at[slot]))
        copies[-1].start()
    for copy in copies:
        copy.wait()


def exchange(array, mask):
    return lax.ppermute(array, "seq", [(i, i ^ mask) for i in range(lax.axis_size("seq"))])


def turned_on(array, distance):
    count = lax.axis_size("seq")
    return lax.ppermute(array, "seq", [(i, (i + distance) % count) for i in range(count)])


def shifted(array, distance):
    count = lax.axis_size("seq")
    return lax.ppermute(array, "seq", [(i, i + distance) for i in range(count - distance)])


def scan_groups(total, groups):
    rows = total.shape[0] - TAIL
    last = shifted(total[rows:], GROUP)
    held, decay = total[:rows].astype(F32), decay_of(total[rows:].astype(F32))
    held = shifted(held, GROUP)
    decay = shifted(decay, GROUP)
    distance = 1
    while distance < groups:
        held = held + decay * shifted(held, GROUP * distance)
        decay = decay * shifted(decay, GROUP * distance)
        distance *= 2
    near_tail = jnp.concatenate([jnp.zeros((X_LAST_AT, last.shape[1]), BF16), last[X_LAST_AT:]], axis=0)
    near = jnp.concatenate([held.astype(BF16), near_tail], axis=0)
    return near, jnp.zeros_like(near)


def on_device(
    ssm_input, bc_input, conv_taps, conv_bias, bc_taps, bc_bias,
    step_input, step_bias, decay_log, skip_gain, request_offset,
):
    block, channels = ssm_input.shape
    state_size = bc_input.shape[1]
    heads = step_input.shape[0]
    width = channels // GROUP
    groups = lax.axis_size("seq") // GROUP
    here = lax.axis_index("seq")
    hbm = pl.BlockSpec(memory_space=pltpu.HBM)
    vmem = pl.BlockSpec(memory_space=pltpu.VMEM)

    swap = [(i, i ^ 1) for i in range(lax.axis_size("head"))]
    other_bc, other_taps, other_bias = [lax.ppermute(part, "head", swap) for part in (bc_input, bc_taps, bc_bias)]
    other_bias = other_bias[None, :]

    others = jax.ShapeDtypeStruct((block, (GROUP - 1) * width), BF16)
    slice_shape = jax.ShapeDtypeStruct((state_size + TAIL, width), BF16)
    (
        x_early, gated, aux_early, passing, time_step, rate_sum, x, x_taps, x_bias, own, own_taps, own_bias, offset,
        lags, late_parts, early_parts,
    ) = pl.pallas_call(
        channels_kernel,
        out_shape=[
            others,
            others,
            jax.ShapeDtypeStruct((24, (GROUP - 1) * width), F32),
            jax.ShapeDtypeStruct((heads, LANES), F32),
            jax.ShapeDtypeStruct((heads, block), F32),
            jax.ShapeDtypeStruct((heads, block), F32),
            jax.ShapeDtypeStruct((block, channels), BF16),
            jax.ShapeDtypeStruct(conv_taps.shape, F32),
            jax.ShapeDtypeStruct((1, channels), F32),
            jax.ShapeDtypeStruct(bc_input.shape, BF16),
            jax.ShapeDtypeStruct(bc_taps.shape, F32),
            jax.ShapeDtypeStruct((1, state_size), F32),
            jax.ShapeDtypeStruct((1, block), jnp.int32),
            jax.ShapeDtypeStruct((conv_taps.shape[0] - 1, block, block), BF16),
            jax.ShapeDtypeStruct((block, 2 * heads), BF16),
            jax.ShapeDtypeStruct((TAIL, 2 * heads), BF16),
        ],
        in_specs=[hbm] * 11,
        out_specs=[vmem] * 16,
        scratch_shapes=[
            pltpu.VMEM((heads, block), F32),
            pltpu.VMEM((1, heads), F32),
            pltpu.VMEM((1, heads), F32),
            pltpu.VMEM((1, heads), F32),
            pltpu.SemaphoreType.DMA((11,)),
        ],
        compiler_params=PARAMS,
        name="channels",
    )(
        *[
            pltpu.with_memory_space_constraint(array, pltpu.HBM)
            for array in (
                ssm_input, conv_taps, conv_bias[None, :], bc_input, bc_taps, bc_bias[None, :], step_input,
                request_offset[None, :], step_bias[None, :], decay_log[None, :], skip_gain[None, :],
            )
        ]
    )
    s1, s2, s3, b_main, b_aux, b_tail, turn, ends = pl.pallas_call(
        states_kernel,
        out_shape=[
            slice_shape,
            slice_shape,
            slice_shape,
            jax.ShapeDtypeStruct((block, state_size), BF16),
            jax.ShapeDtypeStruct((16, state_size), F32),
            jax.ShapeDtypeStruct((TAIL, state_size), F32),
            jax.ShapeDtypeStruct((state_size, block), BF16),
            jax.ShapeDtypeStruct((TAIL, ENDS), BF16),
        ],
        in_specs=[vmem] * 12,
        out_specs=[vmem] * 8,
        compiler_params=PARAMS,
        name="states",
    )(x, own, other_bc, own_taps, other_taps, own_bias, other_bias, lags, gated, aux_early, passing, offset)
    r1, r2, r3 = exchange(s1, 1), exchange(s2, 2), exchange(s3, 3)
    halo = shifted(ends, 1)
    s0, x_late, aux_late = pl.pallas_call(
        rest_kernel,
        out_shape=[
            slice_shape,
            jax.ShapeDtypeStruct((block, width), BF16),
            jax.ShapeDtypeStruct((24, width), F32),
        ],
        in_specs=[vmem] * 10,
        out_specs=[vmem] * 3,
        scratch_shapes=[pltpu.VMEM((block, width), BF16)],
        compiler_params=PARAMS,
        cost_estimate=pl.CostEstimate(flops=400_000_000, bytes_accessed=2_000_000, transcendentals=200_000),
        name="rest",
    )(x, x_taps, x_bias, lags, late_parts, early_parts, passing, offset, turn, b_tail)
    received = [s0, r1, r2, r3]

    direct = groups == GROUP
    if direct:
        earlier = jnp.zeros((TAIL, width), BF16)
    else:
        last = received[0]
        for k in (1, 2, 3):
            last = jnp.where((here % GROUP) ^ k == GROUP - 1, received[k], last)
        earlier = shifted(last[state_size:], GROUP)
    total = pl.pallas_call(
        lambda *refs: group_kernel(*refs, complete=not direct),
        out_shape=slice_shape,
        in_specs=[vmem] * (GROUP + 4),
        out_specs=vmem,
        compiler_params=PARAMS,
        name="group",
    )(r3, r1, r2, s0, earlier, x_taps, x_bias, b_aux)
    total, halo = lax.optimization_barrier((total, halo))
    if direct:
        far = shifted(total, 2 * GROUP)
        near = turned_on(total, GROUP)
    else:
        near, far = scan_groups(total, groups)

    partial, factors = pl.pallas_call(
        before_kernel,
        out_shape=[
            jax.ShapeDtypeStruct((GROUP, state_size, width), F32),
            jax.ShapeDtypeStruct((8, width), F32),
        ],
        in_specs=[vmem] * (GROUP + 4),
        out_specs=[vmem] * 2,
        compiler_params=PARAMS,
        cost_estimate=pl.CostEstimate(flops=100_000_000, bytes_accessed=2_000_000, transcendentals=10_000),
        name="before",
    )(r3, r1, r2, s0, near, x_taps, x_bias, b_aux)
    entering = pl.pallas_call(
        entering_kernel,
        out_shape=[jax.ShapeDtypeStruct((state_size, width), BF16)] * GROUP,
        in_specs=[vmem] * 7,
        out_specs=[vmem] * GROUP,
        compiler_params=PARAMS,
        name="entering",
    )(far, near, partial, factors, x_taps, x_bias, b_aux)
    mine = [entering[0]] + [exchange(entering[k], k) for k in (1, 2, 3)]

    intra, c_conv, carry = pl.pallas_call(
        intra_kernel,
        out_shape=[
            jax.ShapeDtypeStruct((block, channels), F32),
            jax.ShapeDtypeStruct((block, state_size), BF16),
            jax.ShapeDtypeStruct((block, channels), F32),
        ],
        in_specs=[vmem] * 18,
        out_specs=[vmem] * 3,
        scratch_shapes=[
            pltpu.VMEM((block, block), F32),
            pltpu.VMEM((block, block), F32),
            pltpu.VMEM((block, heads), F32),
            pltpu.VMEM((block, channels), BF16),
            pltpu.VMEM((block, state_size), BF16),
            pltpu.VMEM((16, channels), F32),
        ],
        compiler_params=PARAMS,
        cost_estimate=pl.CostEstimate(flops=600_000_000, bytes_accessed=4_000_000, transcendentals=1_000_000),
        name="intra",
    )(
        x_early, x_late, aux_early, aux_late, halo, own, other_bc, own_taps, other_taps, own_bias, other_bias,
        b_main, b_aux, x_taps, time_step, rate_sum, offset, lags,
    )
    out_shape = jax.ShapeDtypeStruct((block, channels), BF16)
    early, late = (0, 3), (2, 1)
    begun = pl.pallas_call(
        lambda *refs: back_kernel(*refs, members=early),
        out_shape=out_shape,
        in_specs=[vmem] * (len(early) + 3),
        out_specs=hbm,
        scratch_shapes=[pltpu.VMEM((len(early), block, width), BF16), pltpu.SemaphoreType.DMA((len(early),))],
        compiler_params=PARAMS,
        name="begin",
    )(c_conv, *[mine[k] for k in early], intra, carry)

    def last_kernel(c, f1, f2, intra, carry, begun, out, held, sems):
        back_kernel(c, f1, f2, intra, carry, out, held, sems, members=late)

    return pl.pallas_call(
        last_kernel,
        out_shape=out_shape,
        in_specs=[vmem] * (len(late) + 3) + [hbm],
        out_specs=hbm,
        scratch_shapes=[pltpu.VMEM((len(late), block, width), BF16), pltpu.SemaphoreType.DMA((len(late),))],
        input_output_aliases={len(late) + 3: 0},
        compiler_params=PARAMS,
        name="back",
    )(c_conv, *[mine[k] for k in late], intra, carry, begun)


def solution(mesh):
    return jax.shard_map(
        on_device,
        mesh=mesh,
        in_specs=(
            P("seq", "head"),
            P("seq", "head"),
            P(None, "head"),
            P("head"),
            P(None, "head"),
            P("head"),
            P("head", "seq"),
            P("head"),
            P("head"),
            P("head"),
            P("seq"),
        ),
        out_specs=P("seq", "head"),
        check_vma=False,
    )
```
